32 devices in a mesh: section: 2 (over core), node: 4 (over y, x), dev: 4 (over z).
Axes of the slice: x: 2, y: 2, z: 4, core: 2. Of those that a mesh axis runs over, the one named last changes fastest.
Arguments:
- inputs_forward: bfloat16 [2, 512, 3584], P('section', 'dev', 'node'), may hold values from -6 to 6
- routes_forward: int32 [2, 512, 2], P('section', 'dev'), may hold values from 0 to 3, all different within a row; in each aligned block of 128 rows (0 to 127, 128 to 255, ..., all dimensions but the last counted through in order) at most 128 rows name the same one
- gates_forward: float32 [2, 512, 2], P('section', 'dev'), may hold values from 0.2 to 1.2
- grads_backward: bfloat16 [2, 512, 3584], P('section', 'dev', 'node'), may hold values from -6 to 6
- routes_backward: int32 [2, 512, 2], P('section', 'dev'), may hold values from 0 to 3, all different within a row; in each aligned block of 128 rows (0 to 127, 128 to 255, ..., all dimensions but the last counted through in order) at most 128 rows name the same one
- gates_backward: float32 [2, 512, 2], P('section', 'dev'), may hold values from 0.2 to 1.2
- w_gate: bfloat16 [2, 4, 3584, 1024], P('section', 'dev', 'node'), may hold values from -0.09375 to 0.09375
- w_up: bfloat16 [2, 4, 3584, 1024], P('section', 'dev', 'node'), may hold values from -0.09375 to 0.09375
- w_down: bfloat16 [2, 4, 1024, 3584], P('section', 'dev', None, 'node'), may hold values from -0.1875 to 0.1875
- saved_gate: bfloat16 [2, 4, 512, 1024], P('section', 'dev'), may hold values from -5 to 5
- saved_up: bfloat16 [2, 4, 512, 1024], P('section', 'dev'), may hold values from -5 to 5
Outputs:
- forward_next: bfloat16 [2, 512, 3584], P('section', 'dev', 'node')
- backward_next: bfloat16 [2, 512, 3584], P('section', 'dev', 'node')
The draws below stay inside these ranges and needn't reach their ends.
Inputs may be any that keep to these rules, and one draw needn't show every extreme that they name: `routes_forward`: each row names 2 different experts. Among the rows of one device no expert is named more than 128 times, a bound that some block reaches. `routes_backward`: each row names 2 different experts. Among the rows of one device no expert is named more than 128 times, a bound that some block reaches.
All inputs are finite; a program needn't handle non-finite values.
Results may differ from the reference program's by a relative error of at most 0.014.
Values may be sent and summed in bfloat16 or wider, within the bound.
No kernel may reach another device: no remote copies, remote signals or barrier semaphores. Data moves between devices by JAX's collectives and lax.ppermute only.
A program may use at most 64 MiB of HBM per device.

```python
import math
import jax
import jax.numpy as jnp
import numpy as np
from jax import lax

D = 3584
FF = 1024
TOPK = 2
TOK_DEV = 128
EXPERTS = 4
CAP = 128
SLOTS = 512
TOKENS = 512
N_SECTION = 2
N_NODE = 4
N_DEV = 4


def levels(rng, dims, pieces, low, largest):
    def one(dim, blocks):
        steps = jax.random.uniform(jax.random.fold_in(jax.random.fold_in(rng, 6), dim), (blocks,), jnp.float32, low / len(pieces), largest / len(pieces))
        return jnp.repeat(jnp.exp(steps), dims[dim] // blocks).reshape((-1,) + (1,) * (len(dims) - dim - 1))

    level = one(*pieces[0])
    for cut in pieces[1:]:
        level = level * one(*cut)
    return level


def shared_out(key, own, number, rows, count, top, bound, lean):
    sequence = jax.random.permutation(key, count)
    crowded, common = load_shares(count, rows * top, bound, lean, True), load_shares(count, rows * top, bound, lean, False)
    places = jnp.arange(count)

    def named(sizes, turn):
        used = int((sizes > 0).sum())
        fixed = max(1, used // 4)
        shifted = fixed + (places - fixed + turn * (used - fixed)) % max(1, count - fixed)
        return jnp.zeros((count,), jnp.int32).at[sequence[jnp.where(places < fixed, places, shifted)]].set(jnp.asarray(sizes, jnp.int32))

    sizes = jnp.where(number % 4 == 0, named(crowded, number // 4), named(common, number - number // 4 - 1))
    mixed = jax.random.permutation(jax.random.fold_in(own, 3), count)
    source_of, receiver = mixed[0:count // 2 * 2:2], mixed[1:count // 2 * 2:2]
    room = jnp.minimum(sizes[source_of] - 1, bound - sizes[receiver]) // 2
    room = jnp.where((source_of == sequence[0]) | (receiver == sequence[0]) | (sizes[receiver] == 0), 0, jnp.maximum(room, 0))
    shifted = jax.random.randint(jax.random.fold_in(own, 4), (count // 2,), 0, 1 << 20) % (room + 1)
    sizes = sizes.at[source_of].add(-shifted).at[receiver].add(shifted)
    members = jnp.searchsorted(jnp.cumsum(sizes), jnp.arange(rows * top), side="right").astype(jnp.int32)
    grid = members.reshape(top, rows).T
    grid = grid[jax.random.permutation(jax.random.fold_in(own, 1), rows)]
    turn = jax.random.randint(jax.random.fold_in(own, 2), (rows, 1), 0, top)
    return jnp.take_along_axis(grid, (jnp.arange(top)[None, :] + turn) % top, axis=1)


def load_shares(count, total, bound, slope, full):
    loads = [(1 << 20) // math.isqrt(standing ** slope) + 1 for standing in range(1, count + 1)]
    largest = bound if full else min(bound, max(-(-total // count), total * loads[0] // sum(loads)))
    least = 1 if total - largest >= count - 1 else 0
    holding, surplus = [largest] + [least] * (count - 1), total - largest - least * (count - 1)
    while surplus > 0:
        candidates = [i for i in range(1, count) if holding[i] < largest] or [i for i in range(1, count) if holding[i] < bound]
        mass, budget = sum([loads[i] for i in candidates]), surplus
        for i in candidates:
            more = min(bound - holding[i], max(1, budget * loads[i] // mass), surplus)
            holding[i] = holding[i] + more
            surplus = surplus - more
    return np.array(holding)


def centred(own_key, extent, deviation, limit, pieces=(), kind=jnp.bfloat16):
    values = deviation * jax.random.normal(own_key, extent, jnp.float32)
    if pieces:
        values = values * levels(own_key, extent, pieces, -0.22, 0.18)
    return jnp.clip(values, -limit, limit).astype(kind)


def setup_inputs(seed: int = 0) -> dict:
    streams_of = jax.random.split(jax.random.key(seed), 12)
    inputs_forward = centred(streams_of[0], (N_SECTION, TOKENS, D), 1.0, 6.0, ((0, 2), (1, 4), (2, 4)))
    routes_forward_keys = jax.random.split(jax.random.fold_in(streams_of[1], 1), N_SECTION * TOKENS // TOK_DEV)
    routes_forward_turns = jax.random.permutation(jax.random.fold_in(streams_of[1], 3), N_SECTION * TOKENS // TOK_DEV)
    routes_forward = jax.vmap(lambda own, number: shared_out(jax.random.fold_in(streams_of[1], 2), own, number, TOK_DEV, EXPERTS, TOPK, CAP, 2))(routes_forward_keys, routes_forward_turns).reshape((N_SECTION, TOKENS, TOPK))
    gates_forward = jnp.clip(jnp.exp(math.log(1.2) - 1.7917595 * jax.random.uniform(streams_of[2], (N_SECTION, TOKENS, TOPK), jnp.float32) ** levels(streams_of[2], (N_SECTION, TOKENS, TOPK), ((0, 2), (1, 4)), -0.2, 0.2)), 0.2, 1.2)
    grads_backward = centred(streams_of[3], (N_SECTION, TOKENS, D), 1.0, 6.0, ((0, 2), (1, 4), (2, 4)))
    routes_backward_keys = jax.random.split(jax.random.fold_in(streams_of[4], 1), N_SECTION * TOKENS // TOK_DEV)
    routes_backward_turns = jax.random.permutation(jax.random.fold_in(streams_of[4], 3), N_SECTION * TOKENS // TOK_DEV)
    routes_backward = jax.vmap(lambda own, number: shared_out(jax.random.fold_in(streams_of[4], 2), own, number, TOK_DEV, EXPERTS, TOPK, CAP, 2))(routes_backward_keys, routes_backward_turns).reshape((N_SECTION, TOKENS, TOPK))
    gates_backward = jnp.clip(jnp.exp(math.log(1.2) - 1.7917595 * jax.random.uniform(streams_of[5], (N_SECTION, TOKENS, TOPK), jnp.float32) ** levels(streams_of[5], (N_SECTION, TOKENS, TOPK), ((0, 2), (1, 4)), -0.2, 0.2)), 0.2, 1.2)
    w_gate = centred(streams_of[6], (N_SECTION, EXPERTS, D, FF), D ** -0.5, 0.09375, ((0, 2), (1, 4), (2, 4)))
    w_up = centred(streams_of[7], (N_SECTION, EXPERTS, D, FF), D ** -0.5, 0.09375, ((0, 2), (1, 4), (2, 4)))
    w_down = centred(streams_of[8], (N_SECTION, EXPERTS, FF, D), FF ** -0.5, 0.1875, ((0, 2), (1, 4), (3, 4)))
    saved_gate = centred(streams_of[9], (N_SECTION, EXPERTS, SLOTS, FF), 1.0, 5.0, ((0, 2), (1, 4)))
    saved_up = centred(streams_of[10], (N_SECTION, EXPERTS, SLOTS, FF), 1.0, 5.0, ((0, 2), (1, 4)))
    return {"inputs_forward": inputs_forward, "routes_forward": routes_forward, "gates_forward": gates_forward, "grads_backward": grads_backward, "routes_backward": routes_backward, "gates_backward": gates_backward, "w_gate": w_gate, "w_up": w_up, "w_down": w_down, "saved_gate": saved_gate, "saved_up": saved_up}


def slot_of(routing):
    blocks = routing.reshape(N_DEV, TOK_DEV * TOPK)
    onehot = (blocks[:, :, None] == jnp.arange(EXPERTS, dtype=jnp.int32)[None, None, :]).astype(jnp.int32)
    earlier = jnp.cumsum(onehot, axis=1) - onehot
    position = jnp.sum(earlier * onehot, axis=2)
    slots = jnp.arange(N_DEV, dtype=jnp.int32)[:, None] * CAP + position
    return blocks.reshape(-1).astype(jnp.int32), slots.reshape(-1).astype(jnp.int32)


def dispatch_rows(token_rows, experts_of, slots):
    owners = (jnp.arange(TOKENS * TOPK, dtype=jnp.int32) // TOPK).astype(jnp.int32)
    filled = jnp.zeros((EXPERTS, SLOTS, D), token_rows.dtype)
    return filled.at[experts_of, slots].set(token_rows[owners])


def block_sum(partial_value):
    rounded = lax.optimization_barrier(partial_value.astype(jnp.bfloat16))
    return jnp.sum(rounded.astype(jnp.float32), axis=0)


def expert_forward(packed):
    slot_rows, gate_matrix, up_matrix, down_matrix = packed
    blocked = slot_rows.reshape(SLOTS, N_NODE, D // N_NODE).astype(jnp.float32)
    gate_blocks = gate_matrix.reshape(N_NODE, D // N_NODE, FF).astype(jnp.float32)
    up_blocks = up_matrix.reshape(N_NODE, D // N_NODE, FF).astype(jnp.float32)
    pre_gate = block_sum(jnp.einsum("snd,ndf->nsf", blocked, gate_blocks))
    pre_up = block_sum(jnp.einsum("snd,ndf->nsf", blocked, up_blocks))
    hidden = (jax.nn.silu(pre_gate) * pre_up).astype(jnp.bfloat16)
    return jnp.dot(hidden, down_matrix, preferred_element_type=jnp.float32).astype(jnp.bfloat16)


def expert_backward(packed):
    slot_rows, gate_matrix, up_matrix, down_matrix, stored_gate, stored_up = packed
    blocked = slot_rows.reshape(SLOTS, N_NODE, D // N_NODE).astype(jnp.float32)
    down_blocks = down_matrix.reshape(FF, N_NODE, D // N_NODE).astype(jnp.float32)
    grad_hidden = block_sum(jnp.einsum("snd,fnd->nsf", blocked, down_blocks))
    act_gate = stored_gate.astype(jnp.float32)
    act_up = stored_up.astype(jnp.float32)
    squash = jax.nn.sigmoid(act_gate)
    grad_gate = (grad_hidden * act_up * squash * (1.0 + act_gate * (1.0 - squash))).astype(jnp.bfloat16)
    grad_up = (grad_hidden * act_gate * squash).astype(jnp.bfloat16)
    total = jnp.dot(grad_gate, gate_matrix.T, preferred_element_type=jnp.float32)
    total = total + jnp.dot(grad_up, up_matrix.T, preferred_element_type=jnp.float32)
    return total.astype(jnp.bfloat16)


def combine(token_rows, weights_of, slot_out, experts_of, slots):
    picked = slot_out[experts_of, slots].reshape(TOKENS, TOPK, D).astype(jnp.float32)
    mixed = token_rows.astype(jnp.float32) + jnp.sum(weights_of[:, :, None] * picked, axis=1)
    return mixed.astype(jnp.bfloat16)


def segment_work(packed):
    (token_rows, routing_forward, weights_forward, grad_rows, routing_backward, weights_backward,
     gate_matrix, up_matrix, down_matrix, stored_gate, stored_up) = packed
    experts_forward, slots_forward = slot_of(routing_forward)
    sent_forward = dispatch_rows(token_rows, experts_forward, slots_forward)
    result_forward = lax.map(expert_forward, (sent_forward, gate_matrix, up_matrix, down_matrix))
    experts_backward, slots_backward = slot_of(routing_backward)
    sent_backward = dispatch_rows(grad_rows, experts_backward, slots_backward)
    result_backward = lax.map(expert_backward, (sent_backward, gate_matrix, up_matrix, down_matrix, stored_gate, stored_up))
    forward_out = combine(token_rows, weights_forward, result_forward, experts_forward, slots_forward)
    backward_out = combine(grad_rows, weights_backward, result_backward, experts_backward, slots_backward)
    return forward_out, backward_out


def next_section(values):
    return jnp.concatenate([values[-1:], values[:-1]], axis=0)


def previous_section(values):
    return jnp.concatenate([values[1:], values[:1]], axis=0)


def reference(inputs_forward, routes_forward, gates_forward, grads_backward, routes_backward, gates_backward, w_gate, w_up, w_down, saved_gate, saved_up):
    forward_out, backward_out = lax.map(segment_work, (inputs_forward, routes_forward, gates_forward, grads_backward, routes_backward, gates_backward, w_gate, w_up, w_down, saved_gate, saved_up))
    return next_section(forward_out), previous_section(backward_out)
```

```python
import functools

import jax
import jax.numpy as jnp
from jax import lax
from jax.experimental import pallas as pl
from jax.experimental.pallas import tpu as pltpu
from jax.sharding import PartitionSpec as P


def from_behind(value, axis, steps):
    count = lax.axis_size(axis)
    pairs = [(source, (source + steps) % count) for source in range(count)]
    return lax.ppermute(value, axis, pairs)


def slot_targets(routing, experts, capacity):
    flat = routing.reshape(-1)
    onehot = (flat[:, None] == jnp.arange(experts, dtype=jnp.int32)[None, :]).astype(jnp.int32)
    earlier = jnp.cumsum(onehot, axis=0) - onehot
    return flat * capacity + jnp.sum(earlier * onehot, axis=1)


def pack_rows(token_rows, targets, slot_count, chosen):
    match = (jnp.arange(slot_count, dtype=jnp.int32)[:, None] == targets[None, :]).astype(
        jnp.bfloat16
    )
    select = jnp.sum(match.reshape(slot_count, token_rows.shape[0], chosen), axis=2)
    return jnp.dot(select, token_rows, preferred_element_type=jnp.float32).astype(jnp.bfloat16)


def combine_rows(token_rows, weights_of, returned_rows, targets):
    width = token_rows.shape[1]
    picked = returned_rows.reshape(-1, width)[targets]
    picked = picked.reshape(token_rows.shape[0], weights_of.shape[1], width).astype(jnp.float32)
    mixed = token_rows.astype(jnp.float32) + jnp.sum(weights_of[:, :, None] * picked, axis=1)
    return mixed.astype(jnp.bfloat16)


def backward_act(grad_hidden, stored_gate, stored_up):
    act_gate = stored_gate.astype(jnp.float32)
    act_up = stored_up.astype(jnp.float32)
    squash = jax.nn.sigmoid(act_gate)
    grad_gate = (grad_hidden * act_up * squash * (1.0 + act_gate * (1.0 - squash))).astype(
        jnp.bfloat16
    )
    grad_up = (grad_hidden * act_gate * squash).astype(jnp.bfloat16)
    return (grad_gate, grad_up)


def shards_by_slots(
    inputs_forward,
    routes_forward,
    gates_forward,
    grads_backward,
    routes_backward,
    gates_backward,
    w_gate,
    w_up,
    w_down,
    saved_gate,
    saved_up,
):
    experts = lax.axis_size("dev")
    chosen = routes_forward.shape[2]
    token_rows = inputs_forward[0]
    grad_rows = grads_backward[0]
    slot_total = saved_gate.shape[2]
    capacity = slot_total // experts
    width = token_rows.shape[1]
    targets_forward = slot_targets(routes_forward[0], experts, capacity)
    targets_backward = slot_targets(routes_backward[0], experts, capacity)
    sent_forward = pack_rows(token_rows, targets_forward, slot_total, chosen).reshape(
        experts, capacity, width
    )
    sent_backward = pack_rows(grad_rows, targets_backward, slot_total, chosen).reshape(
        experts, capacity, width
    )
    arrived_forward, arrived_backward = (
        lax.all_to_all(sent_forward, "dev", split_axis=0, concat_axis=0, tiled=True),
        lax.all_to_all(sent_backward, "dev", split_axis=0, concat_axis=0, tiled=True),
    )
    arrived_forward = arrived_forward.reshape(slot_total, width)
    arrived_backward = arrived_backward.reshape(slot_total, width)
    gate_local = w_gate[0, 0]
    up_local = w_up[0, 0]
    down_local = w_down[0, 0]
    stored_gate = saved_gate[0, 0]
    stored_up = saved_up[0, 0]
    contract_last = (((1,), (1,)), ((), ()))
    part_gate = jnp.dot(arrived_forward, gate_local, preferred_element_type=jnp.float32)
    part_up = jnp.dot(arrived_forward, up_local, preferred_element_type=jnp.float32)
    part_grad = lax.dot_general(
        arrived_backward, down_local, contract_last, preferred_element_type=jnp.float32
    )
    gate_share, up_share = (
        lax.psum_scatter(
            part_gate.astype(jnp.bfloat16), "node", scatter_dimension=1, tiled=True
        ).astype(jnp.float32),
        lax.psum_scatter(
            part_up.astype(jnp.bfloat16), "node", scatter_dimension=1, tiled=True
        ).astype(jnp.float32),
    )
    hidden_share = (jax.nn.silu(gate_share) * up_share).astype(jnp.bfloat16)
    hidden = lax.all_gather(hidden_share, "node", axis=1, tiled=True)
    grad_hidden = lax.psum(part_grad.astype(jnp.bfloat16), "node").astype(jnp.float32)
    grad_gate, grad_up = backward_act(grad_hidden, stored_gate, stored_up)
    result_forward = jnp.dot(hidden, down_local, preferred_element_type=jnp.float32).astype(
        jnp.bfloat16
    )
    result_backward = lax.dot_general(
        grad_gate, gate_local, contract_last, preferred_element_type=jnp.float32
    )
    result_backward = result_backward + lax.dot_general(
        grad_up, up_local, contract_last, preferred_element_type=jnp.float32
    )
    result_backward = result_backward.astype(jnp.bfloat16)
    back_forward, back_backward = (
        lax.all_to_all(
            result_forward.reshape(experts, capacity, width),
            "dev",
            split_axis=0,
            concat_axis=0,
            tiled=True,
        ),
        lax.all_to_all(
            result_backward.reshape(experts, capacity, width),
            "dev",
            split_axis=0,
            concat_axis=0,
            tiled=True,
        ),
    )
    mixed_forward = combine_rows(token_rows, gates_forward[0], back_forward, targets_forward)
    mixed_backward = combine_rows(grad_rows, gates_backward[0], back_backward, targets_backward)
    next_forward = from_behind(mixed_forward[None], "section", 1)
    next_backward = from_behind(mixed_backward[None], "section", -1)
    return (next_forward, next_backward)


CONTRACT_LAST = (((1,), (1,)), ((), ()))
CONTRACT_FIRST = (((0,), (0,)), ((), ()))


def across(value, axis, mask):
    count = lax.axis_size(axis)
    return lax.ppermute(value, axis, [(source, source ^ mask) for source in range(count)])


def call(body, grid, in_specs, out_specs, out_shape, scratch, flops, touched, args):
    return pl.pallas_call(
        body,
        grid_spec=pltpu.PrefetchScalarGridSpec(
            num_scalar_prefetch=1,
            grid=(grid,),
            in_specs=in_specs,
            out_specs=out_specs,
            scratch_shapes=scratch,
        ),
        out_shape=out_shape,
        cost_estimate=pl.CostEstimate(flops=flops, bytes_accessed=touched, transcendentals=0),
        compiler_params=pltpu.CompilerParams(
            dimension_semantics=("arbitrary",), vmem_limit_bytes=32 << 20
        ),
    )(*args)


def whole(shape):
    return pl.BlockSpec(shape, lambda step, place: (0,) * len(shape))


def size_of(arrays):
    return sum(array.size * array.dtype.itemsize for array in arrays)


def by_owner(place, row_refs, sorted_rows, nodes):
    rows = row_refs[0].shape[0] // nodes
    group = len(row_refs)
    for mask in range(nodes):
        first = pl.multiple_of((place[0] ^ mask) * rows, rows)
        for index, ref in enumerate(row_refs):
            at = (mask * group + index) * rows
            sorted_rows[at : at + rows, :] = ref[pl.ds(first, rows), :]


def from_owners(place, piece_refs, joined):
    nodes, group = len(piece_refs), joined.shape[0]
    rows = joined.shape[1] // nodes
    for mask, ref in enumerate(piece_refs):
        first = pl.multiple_of((place[0] ^ mask) * rows, rows)
        for index in range(group):
            joined[index, pl.ds(first, rows), :] = ref[index * rows : (index + 1) * rows, :]


def gate_up_parts(place, rows, w_gate, w_up, nodes, tiles):
    group, (count, width), hidden = len(rows), rows[0].shape, w_gate.shape[1]
    tile, share = hidden // tiles, group * count // nodes

    def body(place_ref, *refs):
        row_refs, gate_ref, up_ref = refs[:group], refs[group], refs[group + 1]
        outs, sorted_rows = refs[group + 2 : -1], refs[-1]

        @pl.when(pl.program_id(0) == 0)
        def _():
            by_owner(place_ref, row_refs, sorted_rows, nodes)

        for half, weight_ref in enumerate((gate_ref, up_ref)):
            part = jnp.dot(sorted_rows[...], weight_ref[...], preferred_element_type=jnp.float32)
            part = part.astype(jnp.bfloat16)
            for mask in range(nodes):
                outs[mask][half] = part[mask * share : (mask + 1) * share]

    return call(
        body,
        tiles,
        [whole((count, width))] * group
        + [pl.BlockSpec((width, tile), lambda step, place: (0, step))] * 2,
        [pl.BlockSpec((2, share, tile), lambda step, place: (0, 0, step))] * nodes,
        [jax.ShapeDtypeStruct((2, share, hidden), jnp.bfloat16)] * nodes,
        [pltpu.VMEM((group * count, width), jnp.bfloat16)],
        4 * group * count * width * hidden,
        size_of(rows) + size_of((w_gate, w_up)) + 4 * group * count * hidden,
        (place, *rows, w_gate, w_up),
    )


def down_rows(place, pieces, w_down, group, tiles):
    nodes, (share, hidden), width = len(pieces), pieces[0].shape, w_down.shape[1]
    count, tile = share * nodes // group, hidden // tiles

    def body(place_ref, *refs):
        piece_refs, down_ref = refs[:nodes], refs[nodes]
        outs, (joined, total) = refs[nodes + 1 : -2], refs[-2:]
        step = pl.program_id(0)
        from_owners(place_ref, piece_refs, joined)
        part = jnp.dot(
            joined[...].reshape(group * count, tile),
            down_ref[...],
            preferred_element_type=jnp.float32,
        )

        @pl.when(step == 0)
        def _():
            total[...] = part

        @pl.when(step > 0)
        def _():
            total[...] += part

        @pl.when(step == tiles - 1)
        def _():
            for index, out in enumerate(outs):
                out[...] = total[index * count : (index + 1) * count].astype(jnp.bfloat16)

    return call(
        body,
        tiles,
        [pl.BlockSpec((share, tile), lambda step, place: (0, step))] * nodes
        + [pl.BlockSpec((tile, width), lambda step, place: (step, 0))],
        [whole((count, width))] * group,
        [jax.ShapeDtypeStruct((count, width), jnp.bfloat16)] * group,
        [
            pltpu.VMEM((group, count, tile), jnp.bfloat16),
            pltpu.VMEM((group * count, width), jnp.float32),
        ],
        2 * group * count * width * hidden,
        size_of(pieces) + size_of((w_down,)) + 2 * group * count * width,
        (place, *pieces, w_down),
    )


def grad_hidden_parts(place, rows, w_down, nodes, tiles):
    group, (count, width), hidden = len(rows), rows[0].shape, w_down.shape[0]
    tile, share = hidden // tiles, group * count // nodes

    def body(place_ref, *refs):
        row_refs, down_ref = refs[:group], refs[group]
        outs, sorted_rows = refs[group + 1 : -1], refs[-1]

        @pl.when(pl.program_id(0) == 0)
        def _():
            by_owner(place_ref, row_refs, sorted_rows, nodes)

        part = lax.dot_general(
            sorted_rows[...], down_ref[...], CONTRACT_LAST, preferred_element_type=jnp.float32
        ).astype(jnp.bfloat16)
        for mask in range(nodes):
            outs[mask][...] = part[mask * share : (mask + 1) * share]

    return call(
        body,
        tiles,
        [whole((count, width))] * group
        + [pl.BlockSpec((tile, width), lambda step, place: (step, 0))],
        [pl.BlockSpec((share, tile), lambda step, place: (0, step))] * nodes,
        [jax.ShapeDtypeStruct((share, hidden), jnp.bfloat16)] * nodes,
        [pltpu.VMEM((group * count, width), jnp.bfloat16)],
        2 * group * count * width * hidden,
        size_of(rows) + size_of((w_down,)) + 2 * group * count * hidden,
        (place, *rows, w_down),
    )


def input_grad_rows(place, pieces, w_gate, w_up, saved_gate, saved_up, masks, tiles):
    nodes, (share, hidden), width = len(pieces), pieces[0].shape, w_gate.shape[0]
    group = len(masks)
    count, tile = share * nodes // group, hidden // tiles

    def body(place_ref, *refs):
        piece_refs, (gate_ref, up_ref) = refs[:nodes], refs[nodes : nodes + 2]
        stored = refs[nodes + 2 : nodes + 2 + 2 * group]
        outs, (joined, total) = refs[nodes + 2 + 2 * group : -2], refs[-2:]
        step = pl.program_id(0)
        from_owners(place_ref, piece_refs, joined)
        grads_gate, grads_up = [], []
        for index in range(group):
            grad_gate, grad_up = backward_act(
                joined[index].astype(jnp.float32), stored[index][...], stored[group + index][...]
            )
            grads_gate.append(grad_gate)
            grads_up.append(grad_up)
        part = lax.dot_general(
            jnp.concatenate(grads_gate, axis=0),
            gate_ref[...],
            CONTRACT_LAST,
            preferred_element_type=jnp.float32,
        ) + lax.dot_general(
            jnp.concatenate(grads_up, axis=0),
            up_ref[...],
            CONTRACT_LAST,
            preferred_element_type=jnp.float32,
        )

        @pl.when(step == 0)
        def _():
            total[...] = part

        @pl.when(step > 0)
        def _():
            total[...] += part

        @pl.when(step == tiles - 1)
        def _():
            for index, out in enumerate(outs):
                out[...] = total[index * count : (index + 1) * count].astype(jnp.bfloat16)

    stored_specs = [
        pl.BlockSpec((count, tile), functools.partial(lambda mask, step, place: (place[1] ^ mask, step), mask))
        for mask in masks
    ]
    return call(
        body,
        tiles,
        [pl.BlockSpec((share, tile), lambda step, place: (0, step))] * nodes
        + [pl.BlockSpec((width, tile), lambda step, place: (0, step))] * 2
        + stored_specs * 2,
        [whole((count, width))] * group,
        [jax.ShapeDtypeStruct((count, width), jnp.bfloat16)] * group,
        [
            pltpu.VMEM((group, count, tile), jnp.bfloat16),
            pltpu.VMEM((group * count, width), jnp.float32),
        ],
        4 * group * count * width * hidden,
        size_of(pieces) + size_of((w_gate, w_up)) + 6 * group * count * hidden,
        (place, *pieces, w_gate, w_up) + (saved_gate,) * group + (saved_up,) * group,
    )


def selections(place_ref, routes_ref, experts, capacity):
    chosen, count = routes_ref.shape
    routes = routes_ref[...]
    line = lax.broadcasted_iota(jnp.int32, (experts, count), 0) ^ place_ref[1]
    named = jnp.zeros((experts, count), jnp.float32)
    for choice in range(chosen):
        named += (routes[choice : choice + 1] == line).astype(jnp.float32)
    earlier = lax.broadcasted_iota(jnp.int32, (count, count), 0) < lax.broadcasted_iota(
        jnp.int32, (count, count), 1
    )
    rank = jnp.dot(
        named.astype(jnp.bfloat16),
        earlier.astype(jnp.bfloat16),
        preferred_element_type=jnp.float32,
    )
    slot = jnp.where(named > 0, rank, -1.0)
    slots = lax.broadcasted_iota(jnp.int32, (capacity, count), 0).astype(jnp.float32)
    return [
        (slots == slot[mask : mask + 1]).astype(jnp.float32).astype(jnp.bfloat16)
        for mask in range(experts)
    ]


def slot_rows(place, routes, rows, experts, capacity):
    count, width = rows.shape

    def body(place_ref, routes_ref, rows_ref, *outs):
        for select, out in zip(selections(place_ref, routes_ref, experts, capacity), outs):
            out[...] = jnp.dot(
                select, rows_ref[...], preferred_element_type=jnp.float32
            ).astype(jnp.bfloat16)

    return call(
        body,
        1,
        [whole(routes.shape), whole(rows.shape)],
        [whole((capacity, width))] * experts,
        [jax.ShapeDtypeStruct((capacity, width), jnp.bfloat16)] * experts,
        [],
        2 * experts * capacity * count * width,
        (experts + 1) * size_of((rows,)),
        (place, routes, rows),
    )


def mix_slots(place, routes, routes_by_token, weights, rows, returned):
    experts, (capacity, width) = len(returned), returned[0].shape

    def body(place_ref, routes_ref, named_ref, weights_ref, rows_ref, *refs):
        returned_refs, out = refs[:-1], refs[-1]
        total = rows_ref[...].astype(jnp.float32)
        chosen = selections(place_ref, routes_ref, experts, capacity)
        for mask, (select, ref) in enumerate(zip(chosen, returned_refs)):
            weight = jnp.sum(
                jnp.where(named_ref[...] == (place_ref[1] ^ mask), weights_ref[...], 0.0),
                axis=1,
                keepdims=True,
            )
            total += weight * lax.dot_general(
                select, ref[...], CONTRACT_FIRST, preferred_element_type=jnp.float32
            )
        out[...] = total.astype(jnp.bfloat16)

    return call(
        body,
        1,
        [whole(routes.shape), whole(routes_by_token.shape), whole(weights.shape), whole(rows.shape)]
        + [whole((capacity, width))] * experts,
        whole(rows.shape),
        jax.ShapeDtypeStruct(rows.shape, jnp.bfloat16),
        [],
        2 * experts * capacity * rows.size,
        (experts + 2) * size_of((rows,)),
        (place, routes, routes_by_token, weights, rows, *returned),
    )


def mix_tokens(expert, routes, weights, rows, returned):
    total = rows.astype(jnp.float32)
    for mask, value in enumerate(returned):
        weight = jnp.sum(jnp.where(routes == (expert ^ mask), weights, 0.0), axis=1, keepdims=True)
        total = total + weight * value.astype(jnp.float32)
    return total.astype(jnp.bfloat16)


def sum_pieces(pieces):
    return sum(piece.astype(jnp.float32) for piece in pieces)


def sections_shards(
    inputs_forward,
    routes_forward,
    gates_forward,
    grads_backward,
    routes_backward,
    gates_backward,
    w_gate,
    w_up,
    w_down,
    saved_gate,
    saved_up,
):
    experts, nodes = lax.axis_size("dev"), lax.axis_size("node")
    expert = lax.axis_index("dev")
    place = jnp.stack([lax.axis_index("node"), expert]).astype(jnp.int32)
    capacity = saved_gate.shape[2] // experts
    token_rows, grad_rows = inputs_forward[0], grads_backward[0]
    gate_local, up_local, down_local = w_gate[0, 0], w_up[0, 0], w_down[0, 0]
    stored_gate, stored_up = saved_gate[0, 0], saved_up[0, 0]
    routes_lines = routes_backward[0].T

    arrived_forward = [token_rows] + [across(token_rows, "dev", m) for m in range(1, experts)]
    packed = slot_rows(place, routes_lines, grad_rows, experts, capacity)
    arrived_backward = [packed[0]] + [across(packed[m], "dev", m) for m in range(1, experts)]

    back_forward, back_backward = [None] * experts, [None] * experts
    for masks in GROUPS:
        parts = gate_up_parts(place, [arrived_forward[m] for m in masks], gate_local, up_local, nodes, 4)
        pieces = [parts[0]] + [across(parts[q], "node", q) for q in range(1, nodes)]
        gate_share, up_share = sum_pieces(pieces)
        hidden = (jax.nn.silu(gate_share) * up_share).astype(jnp.bfloat16)
        hidden_pieces = [hidden] + [across(hidden, "node", q) for q in range(1, nodes)]
        for m, value in zip(masks, down_rows(place, hidden_pieces, down_local, len(masks), 4)):
            back_forward[m] = across(value, "dev", m) if m else value

        parts = grad_hidden_parts(place, [arrived_backward[m] for m in masks], down_local, nodes, 4)
        pieces = [parts[0]] + [across(parts[q], "node", q) for q in range(1, nodes)]
        grad_hidden = sum_pieces(pieces).astype(jnp.bfloat16)
        grad_pieces = [grad_hidden] + [across(grad_hidden, "node", q) for q in range(1, nodes)]
        rows = input_grad_rows(
            place, grad_pieces, gate_local, up_local, stored_gate, stored_up, masks, 4
        )
        for m, value in zip(masks, rows):
            back_backward[m] = across(value, "dev", m) if m else value

    mixed_forward = mix_tokens(expert, routes_forward[0], gates_forward[0], token_rows, back_forward)
    next_forward = from_behind(mixed_forward[None], "section", 1)
    mixed_backward = mix_slots(
        place, routes_lines, routes_backward[0], gates_backward[0], grad_rows, back_backward
    )
    next_backward = from_behind(mixed_backward[None], "section", -1)
    return (next_forward, next_backward)


GROUPS = ((0, 1), (2, 3))


def power_of_two(number):
    return number & (number - 1) == 0


def shards(*args):
    experts, nodes = lax.axis_size("dev"), lax.axis_size("node")
    tokens, capacity = args[0].shape[1], args[9].shape[2] // experts
    if capacity == tokens and power_of_two(experts) and power_of_two(nodes) and tokens % (16 * nodes) == 0:
        return sections_shards(*args)
    return shards_by_slots(*args)


def solution(mesh):
    return jax.shard_map(
        shards,
        mesh=mesh,
        in_specs=(
            P("section", "dev", "node"),
            P("section", "dev", None),
            P("section", "dev", None),
            P("section", "dev", "node"),
            P("section", "dev", None),
            P("section", "dev", None),
            P("section", "dev", "node", None),
            P("section", "dev", "node", None),
            P("section", "dev", None, "node"),
            P("section", "dev", None, None),
            P("section", "dev", None, None),
        ),
        out_specs=(P("section", "dev", "node"), P("section", "dev", "node")),
        check_vma=False,
    )
```

```python
import functools

import jax
import jax.numpy as jnp
from jax import lax
from jax.experimental import pallas as pl
from jax.experimental.pallas import tpu as pltpu
from jax.sharding import PartitionSpec as P


def from_behind(value, axis, steps):
    count = lax.axis_size(axis)
    pairs = [(source, (source + steps) % count) for source in range(count)]
    return lax.ppermute(value, axis, pairs)


def slot_targets(routing, experts, capacity):
    flat = routing.reshape(-1)
    onehot = (flat[:, None] == jnp.arange(experts, dtype=jnp.int32)[None, :]).astype(jnp.int32)
    earlier = jnp.cumsum(onehot, axis=0) - onehot
    return flat * capacity + jnp.sum(earlier * onehot, axis=1)


def pack_rows(token_rows, targets, slot_count, chosen):
    match = (jnp.arange(slot_count, dtype=jnp.int32)[:, None] == targets[None, :]).astype(
        jnp.bfloat16
    )
    select = jnp.sum(match.reshape(slot_count, token_rows.shape[0], chosen), axis=2)
    return jnp.dot(select, token_rows, preferred_element_type=jnp.float32).astype(jnp.bfloat16)


def combine_rows(token_rows, weights_of, returned_rows, targets):
    width = token_rows.shape[1]
    picked = returned_rows.reshape(-1, width)[targets]
    picked = picked.reshape(token_rows.shape[0], weights_of.shape[1], width).astype(jnp.float32)
    mixed = token_rows.astype(jnp.float32) + jnp.sum(weights_of[:, :, None] * picked, axis=1)
    return mixed.astype(jnp.bfloat16)


def backward_act(grad_hidden, stored_gate, stored_up):
    act_gate = stored_gate.astype(jnp.float32)
    act_up = stored_up.astype(jnp.float32)
    squash = jax.nn.sigmoid(act_gate)
    grad_gate = (grad_hidden * act_up * squash * (1.0 + act_gate * (1.0 - squash))).astype(
        jnp.bfloat16
    )
    grad_up = (grad_hidden * act_gate * squash).astype(jnp.bfloat16)
    return (grad_gate, grad_up)


def shards_by_slots(
    inputs_forward,
    routes_forward,
    gates_forward,
    grads_backward,
    routes_backward,
    gates_backward,
    w_gate,
    w_up,
    w_down,
    saved_gate,
    saved_up,
):
    experts = lax.axis_size("dev")
    chosen = routes_forward.shape[2]
    token_rows = inputs_forward[0]
    grad_rows = grads_backward[0]
    slot_total = saved_gate.shape[2]
    capacity = slot_total // experts
    width = token_rows.shape[1]
    targets_forward = slot_targets(routes_forward[0], experts, capacity)
    targets_backward = slot_targets(routes_backward[0], experts, capacity)
    sent_forward = pack_rows(token_rows, targets_forward, slot_total, chosen).reshape(
        experts, capacity, width
    )
    sent_backward = pack_rows(grad_rows, targets_backward, slot_total, chosen).reshape(
        experts, capacity, width
    )
    arrived_forward, arrived_backward = (
        lax.all_to_all(sent_forward, "dev", split_axis=0, concat_axis=0, tiled=True),
        lax.all_to_all(sent_backward, "dev", split_axis=0, concat_axis=0, tiled=True),
    )
    arrived_forward = arrived_forward.reshape(slot_total, width)
    arrived_backward = arrived_backward.reshape(slot_total, width)
    gate_local = w_gate[0, 0]
    up_local = w_up[0, 0]
    down_local = w_down[0, 0]
    stored_gate = saved_gate[0, 0]
    stored_up = saved_up[0, 0]
    contract_last = (((1,), (1,)), ((), ()))
    part_gate = jnp.dot(arrived_forward, gate_local, preferred_element_type=jnp.float32)
    part_up = jnp.dot(arrived_forward, up_local, preferred_element_type=jnp.float32)
    part_grad = lax.dot_general(
        arrived_backward, down_local, contract_last, preferred_element_type=jnp.float32
    )
    gate_share, up_share = (
        lax.psum_scatter(
            part_gate.astype(jnp.bfloat16), "node", scatter_dimension=1, tiled=True
        ).astype(jnp.float32),
        lax.psum_scatter(
            part_up.astype(jnp.bfloat16), "node", scatter_dimension=1, tiled=True
        ).astype(jnp.float32),
    )
    hidden_share = (jax.nn.silu(gate_share) * up_share).astype(jnp.bfloat16)
    hidden = lax.all_gather(hidden_share, "node", axis=1, tiled=True)
    grad_hidden = lax.psum(part_grad.astype(jnp.bfloat16), "node").astype(jnp.float32)
    grad_gate, grad_up = backward_act(grad_hidden, stored_gate, stored_up)
    result_forward = jnp.dot(hidden, down_local, preferred_element_type=jnp.float32).astype(
        jnp.bfloat16
    )
    result_backward = lax.dot_general(
        grad_gate, gate_local, contract_last, preferred_element_type=jnp.float32
    )
    result_backward = result_backward + lax.dot_general(
        grad_up, up_local, contract_last, preferred_element_type=jnp.float32
    )
    result_backward = result_backward.astype(jnp.bfloat16)
    back_forward, back_backward = (
        lax.all_to_all(
            result_forward.reshape(experts, capacity, width),
            "dev",
            split_axis=0,
            concat_axis=0,
            tiled=True,
        ),
        lax.all_to_all(
            result_backward.reshape(experts, capacity, width),
            "dev",
            split_axis=0,
            concat_axis=0,
            tiled=True,
        ),
    )
    mixed_forward = combine_rows(token_rows, gates_forward[0], back_forward, targets_forward)
    mixed_backward = combine_rows(grad_rows, gates_backward[0], back_backward, targets_backward)
    next_forward = from_behind(mixed_forward[None], "section", 1)
    next_backward = from_behind(mixed_backward[None], "section", -1)
    return (next_forward, next_backward)


CONTRACT_LAST = (((1,), (1,)), ((), ()))
CONTRACT_FIRST = (((0,), (0,)), ((), ()))
VMEM = pl.BlockSpec(memory_space=pltpu.VMEM)
SMEM = pl.BlockSpec(memory_space=pltpu.SMEM)
VMEM_BYTES = 14 << 20
ANY = pl.BlockSpec(memory_space=pl.ANY)


def across(value, axis, mask):
    count = lax.axis_size(axis)
    return lax.ppermute(value, axis, [(source, source ^ mask) for source in range(count)])


def ring_order(count):
    return [0] + list(range(1, count, 2)) + list(range(2, count, 2))[::-1]


def ring_pairs(count, steps):
    order = ring_order(count)
    return [(order[i], order[(i + steps) % count]) for i in range(count)]


def along_ring(value, steps):
    return lax.ppermute(value, "dev", ring_pairs(lax.axis_size("dev"), steps))


def along_ring_and_sections(value, shift):
    count, sections = lax.axis_size("dev"), lax.axis_size("section")
    pairs = [
        (section * count + source, (section + shift) % sections * count + target)
        for section in range(sections)
        for source, target in ring_pairs(count, 1)
    ]
    return lax.ppermute(value, ("section", "dev"), pairs)


def block_behind(expert, count, steps):
    block = 0
    for target, source in ring_pairs(count, -steps):
        block = block + jnp.where(expert == target, source, 0)
    return block


def call(body, place, operands, after, out_shape, scratch, flops):
    def with_after(place_ref, *refs):
        body(place_ref, *refs[: len(operands)], *refs[len(operands) + len(after) :])

    touched = sum(array.size * array.dtype.itemsize for array in operands)
    return pl.pallas_call(
        with_after,
        in_specs=[SMEM] + [VMEM] * len(operands) + [ANY] * len(after),
        out_specs=jax.tree.map(lambda _: VMEM, out_shape),
        scratch_shapes=scratch,
        out_shape=out_shape,
        cost_estimate=pl.CostEstimate(flops=flops, bytes_accessed=touched, transcendentals=0),
        compiler_params=pltpu.CompilerParams(vmem_limit_bytes=VMEM_BYTES),
    )(place, *operands, *after)


def matmul(left, right, dims=(((1,), (0,)), ((), ()))):
    return lax.dot_general(left, right, dims, preferred_element_type=jnp.float32)


def by_owner(place_ref, rows_ref, sorted_rows, nodes):
    rows = rows_ref.shape[0] // nodes
    for mask in range(nodes):
        first = pl.multiple_of((place_ref[0] ^ mask) * rows, rows)
        sorted_rows[mask * rows : (mask + 1) * rows, :] = rows_ref[pl.ds(first, rows), :]


def first_products(place, token_rows, grad_rows, weights, nodes, after):
    (count, width), hidden = token_rows.shape, weights[0].shape[1]
    share = count // nodes

    def body(place_ref, token_ref, grad_ref, gate_ref, up_ref, down_ref, *refs):
        outs, (sorted_tokens, sorted_grads) = refs[:nodes], refs[nodes:]
        by_owner(place_ref, token_ref, sorted_tokens, nodes)
        by_owner(place_ref, grad_ref, sorted_grads, nodes)
        parts = (
            matmul(sorted_tokens[...], gate_ref[...]),
            matmul(sorted_tokens[...], up_ref[...]),
            matmul(sorted_grads[...], down_ref[...], CONTRACT_LAST),
        )
        for index, part in enumerate(parts):
            for mask in range(nodes):
                outs[mask][index] = part[mask * share : (mask + 1) * share].astype(jnp.bfloat16)

    return call(
        body,
        place,
        (token_rows, grad_rows, *weights),
        after,
        [jax.ShapeDtypeStruct((3, share, hidden), jnp.bfloat16)] * nodes,
        [pltpu.VMEM((count, width), jnp.bfloat16)] * 2,
        6 * count * width * hidden,
    )


def activations(place, pieces, after):
    _, share, hidden = pieces[0].shape

    def body(place_ref, *refs):
        piece_refs, out = refs[:-1], refs[-1]
        gate, up, grad = (
            sum(ref[index].astype(jnp.float32) for ref in piece_refs) for index in range(3)
        )
        out[0] = (gate / (1.0 + jnp.exp(-gate)) * up).astype(jnp.bfloat16)
        out[1] = grad.astype(jnp.bfloat16)

    return call(
        body,
        place,
        pieces,
        after,
        jax.ShapeDtypeStruct((2, share, hidden), jnp.bfloat16),
        [],
        16 * share * hidden,
    )


def join(place_ref, piece_refs, index, joined):
    rows = piece_refs[0].shape[1]
    for mask, ref in enumerate(piece_refs):
        first = pl.multiple_of((place_ref[0] ^ mask) * rows, rows)
        joined[pl.ds(first, rows), :] = ref[index]


def weight_column(expert, routes, gates):
    chosen, count = routes.shape
    line = jnp.zeros((1, count), jnp.float32)
    for choice in range(chosen):
        line += jnp.where(routes[choice : choice + 1] == expert, gates[choice : choice + 1], 0.0)
    diagonal = lax.broadcasted_iota(jnp.int32, (count, count), 0) == lax.broadcasted_iota(
        jnp.int32, (count, count), 1
    )
    return jnp.sum(jnp.where(diagonal, line, 0.0), axis=1, keepdims=True)


def slot_selection(expert, routes, capacity):
    chosen, count = routes.shape
    named = jnp.zeros((1, count), jnp.float32)
    for choice in range(chosen):
        named += (routes[choice : choice + 1] == expert).astype(jnp.float32)
    earlier = lax.broadcasted_iota(jnp.int32, (count, count), 0) < lax.broadcasted_iota(
        jnp.int32, (count, count), 1
    )
    rank = matmul(
        jnp.broadcast_to(named, (16, count)).astype(jnp.bfloat16),
        earlier.astype(jnp.float32).astype(jnp.bfloat16),
    )[0:1]
    slot = jnp.where(named > 0, rank, -1.0)
    slots = lax.broadcasted_iota(jnp.int32, (capacity, count), 0).astype(jnp.float32)
    return (slots == slot).astype(jnp.float32).astype(jnp.bfloat16)


def forward_results(place, pieces, w_down, info, added, after):
    nodes, (_, share, hidden), width = len(pieces), pieces[0].shape, w_down.shape[1]
    count, chosen = share * nodes, info.shape[0] // 4

    def body(place_ref, *refs):
        piece_refs, (down_ref, info_ref, added_ref, out, joined) = refs[:nodes], refs[nodes:]
        join(place_ref, piece_refs, 0, joined)
        routes = info_ref[0:chosen].astype(jnp.int32)
        weight = weight_column(place_ref[1], routes, info_ref[chosen : 2 * chosen])
        result = matmul(joined[...], down_ref[...]).astype(jnp.bfloat16).astype(jnp.float32)
        out[...] = (added_ref[...].astype(jnp.float32) + weight * result).astype(jnp.bfloat16)

    return call(
        body,
        place,
        (*pieces, w_down, info, added),
        after,
        jax.ShapeDtypeStruct((count, width), jnp.bfloat16),
        [pltpu.VMEM((count, hidden), jnp.bfloat16)],
        2 * count * width * hidden,
    )


def backward_results(place, pieces, w_gate, w_up, saved_gate, saved_up, info, added, block, after):
    nodes, (_, share, hidden), width = len(pieces), pieces[0].shape, w_gate.shape[0]
    count, chosen = share * nodes, info.shape[0] // 4
    experts = saved_gate.shape[0] // count

    def body(place_ref, *refs):
        piece_refs, refs = refs[:nodes], refs[nodes:]
        gate_ref, up_ref, saved_gate_ref, saved_up_ref, info_ref, added_ref, out, joined = refs
        join(place_ref, piece_refs, 1, joined)
        expert = place_ref[1]
        routes = info_ref[2 * chosen : 3 * chosen].astype(jnp.int32)
        weight = weight_column(expert, routes, info_ref[3 * chosen :])
        select = slot_selection(expert, routes, count)
        first = pl.multiple_of(block_behind(expert, experts, block) * count, count)
        grad_gate, grad_up = backward_act(
            joined[...].astype(jnp.float32),
            matmul(select, saved_gate_ref[pl.ds(first, count), :], CONTRACT_FIRST),
            matmul(select, saved_up_ref[pl.ds(first, count), :], CONTRACT_FIRST),
        )
        result = matmul(grad_gate, gate_ref[...], CONTRACT_LAST)
        result += matmul(grad_up, up_ref[...], CONTRACT_LAST)
        result = result.astype(jnp.bfloat16).astype(jnp.float32)
        out[...] = (added_ref[...].astype(jnp.float32) + weight * result).astype(jnp.bfloat16)

    return call(
        body,
        place,
        (*pieces, w_gate, w_up, saved_gate, saved_up, info, added),
        after,
        jax.ShapeDtypeStruct((count, width), jnp.bfloat16),
        [pltpu.VMEM((count, hidden), jnp.bfloat16)],
        4 * count * width * hidden,
    )


def ring_shards(
    inputs_forward,
    routes_forward,
    gates_forward,
    grads_backward,
    routes_backward,
    gates_backward,
    w_gate,
    w_up,
    w_down,
    saved_gate,
    saved_up,
):
    experts, nodes = lax.axis_size("dev"), lax.axis_size("node")
    place = jnp.stack([lax.axis_index("node"), lax.axis_index("dev")]).astype(jnp.int32)
    weights = (w_gate[0, 0], w_up[0, 0], w_down[0, 0])
    stored_gate, stored_up = saved_gate[0, 0], saved_up[0, 0]

    tokens, grads = [inputs_forward[0]], [grads_backward[0]]
    info = jnp.concatenate(
        [
            routes_forward[0].T.astype(jnp.float32),
            gates_forward[0].T,
            routes_backward[0].T.astype(jnp.float32),
            gates_backward[0].T,
        ]
    )
    for _ in range(1, experts):
        tokens.append(along_ring(tokens[-1], 1))
        grads.append(along_ring(grads[-1], 1))
    infos = [info] + [along_ring(info, step) for step in range(1, experts)]

    pieces, shares = [None] * experts, [None] * experts
    order = []

    def exchange(own):
        return [own[mask] if mask == 0 else across(own[mask], "node", mask) for mask in range(nodes)]

    def first(step):
        own = first_products(place, tokens[step], grads[step], weights, nodes, order[-1:])
        order.append(own[0])
        pieces[step] = exchange(own)

    def middle(step):
        own = activations(place, pieces[step], order[-1:])
        order.append(own)
        shares[step] = exchange([own] * nodes)

    hops = [inputs_forward[0], grads_backward[0]]
    base = [None, None]

    def last(step):
        added = hops
        if step == 1:
            added = [jnp.zeros_like(hops[0]), jnp.zeros_like(hops[1])]
        forward = forward_results(place, shares[step], weights[2], infos[step], added[0], order[-1:])
        order.append(forward)
        backward = backward_results(
            place, shares[step], *weights[:2], stored_gate, stored_up, infos[step], added[1], step, order[-1:]
        )
        order.append(backward)
        if step == 0:
            base[:] = [from_behind(forward, "section", 1), from_behind(backward, "section", -1)]
        elif step < experts - 1:
            hops[:] = [along_ring(forward, 1), along_ring(backward, 1)]
        else:
            hops[:] = [along_ring_and_sections(forward, 1), along_ring_and_sections(backward, -1)]

    for turn in range(experts + 2):
        for act, step in ((first, turn), (last, turn - 2), (middle, turn - 1)):
            if 0 <= step < experts:
                act(step)
    return tuple(
        (own.astype(jnp.float32) + others.astype(jnp.float32)).astype(jnp.bfloat16)[None]
        for own, others in zip(base, hops)
    )


def power_of_two(number):
    return number & (number - 1) == 0


def shards(*args):
    experts, nodes = lax.axis_size("dev"), lax.axis_size("node")
    tokens, capacity = args[0].shape[1], args[9].shape[2] // experts
    if capacity == tokens and experts > 1 and power_of_two(nodes) and tokens % (16 * nodes) == 0:
        return ring_shards(*args)
    return shards_by_slots(*args)


def solution(mesh):
    return jax.shard_map(
        shards,
        mesh=mesh,
        in_specs=(
            P("section", "dev", "node"),
            P("section", "dev", None),
            P("section", "dev", None),
            P("section", "dev", "node"),
            P("section", "dev", None),
            P("section", "dev", None),
            P("section", "dev", "node", None),
            P("section", "dev", "node", None),
            P("section", "dev", None, "node"),
            P("section", "dev", None, None),
            P("section", "dev", None, None),
        ),
        out_specs=(P("section", "dev", "node"), P("section", "dev", "node")),
        check_vma=False,
    )
```

```python
import functools

import jax
import jax.numpy as jnp
from jax import lax
from jax.experimental import pallas as pl
from jax.experimental.pallas import tpu as pltpu
from jax.sharding import PartitionSpec as P


def from_behind(value, axis, steps):
    count = lax.axis_size(axis)
    pairs = [(source, (source + steps) % count) for source in range(count)]
    return lax.ppermute(value, axis, pairs)


def slot_targets(routing, experts, capacity):
    flat = routing.reshape(-1)
    onehot = (flat[:, None] == jnp.arange(experts, dtype=jnp.int32)[None, :]).astype(jnp.int32)
    earlier = jnp.cumsum(onehot, axis=0) - onehot
    return flat * capacity + jnp.sum(earlier * onehot, axis=1)


def pack_rows(token_rows, targets, slot_count, chosen):
    match = (jnp.arange(slot_count, dtype=jnp.int32)[:, None] == targets[None, :]).astype(
        jnp.bfloat16
    )
    select = jnp.sum(match.reshape(slot_count, token_rows.shape[0], chosen), axis=2)
    return jnp.dot(select, token_rows, preferred_element_type=jnp.float32).astype(jnp.bfloat16)


def combine_rows(token_rows, weights_of, returned_rows, targets):
    width = token_rows.shape[1]
    picked = returned_rows.reshape(-1, width)[targets]
    picked = picked.reshape(token_rows.shape[0], weights_of.shape[1], width).astype(jnp.float32)
    mixed = token_rows.astype(jnp.float32) + jnp.sum(weights_of[:, :, None] * picked, axis=1)
    return mixed.astype(jnp.bfloat16)


def backward_act(grad_hidden, stored_gate, stored_up):
    act_gate = stored_gate.astype(jnp.float32)
    act_up = stored_up.astype(jnp.float32)
    squash = jax.nn.sigmoid(act_gate)
    grad_gate = (grad_hidden * act_up * squash * (1.0 + act_gate * (1.0 - squash))).astype(
        jnp.bfloat16
    )
    grad_up = (grad_hidden * act_gate * squash).astype(jnp.bfloat16)
    return (grad_gate, grad_up)


def shards_by_slots(
    inputs_forward,
    routes_forward,
    gates_forward,
    grads_backward,
    routes_backward,
    gates_backward,
    w_gate,
    w_up,
    w_down,
    saved_gate,
    saved_up,
):
    experts = lax.axis_size("dev")
    chosen = routes_forward.shape[2]
    token_rows = inputs_forward[0]
    grad_rows = grads_backward[0]
    slot_total = saved_gate.shape[2]
    capacity = slot_total // experts
    width = token_rows.shape[1]
    targets_forward = slot_targets(routes_forward[0], experts, capacity)
    targets_backward = slot_targets(routes_backward[0], experts, capacity)
    sent_forward = pack_rows(token_rows, targets_forward, slot_total, chosen).reshape(
        experts, capacity, width
    )
    sent_backward = pack_rows(grad_rows, targets_backward, slot_total, chosen).reshape(
        experts, capacity, width
    )
    arrived_forward, arrived_backward = (
        lax.all_to_all(sent_forward, "dev", split_axis=0, concat_axis=0, tiled=True),
        lax.all_to_all(sent_backward, "dev", split_axis=0, concat_axis=0, tiled=True),
    )
    arrived_forward = arrived_forward.reshape(slot_total, width)
    arrived_backward = arrived_backward.reshape(slot_total, width)
    gate_local = w_gate[0, 0]
    up_local = w_up[0, 0]
    down_local = w_down[0, 0]
    stored_gate = saved_gate[0, 0]
    stored_up = saved_up[0, 0]
    contract_last = (((1,), (1,)), ((), ()))
    part_gate = jnp.dot(arrived_forward, gate_local, preferred_element_type=jnp.float32)
    part_up = jnp.dot(arrived_forward, up_local, preferred_element_type=jnp.float32)
    part_grad = lax.dot_general(
        arrived_backward, down_local, contract_last, preferred_element_type=jnp.float32
    )
    gate_share, up_share = (
        lax.psum_scatter(
            part_gate.astype(jnp.bfloat16), "node", scatter_dimension=1, tiled=True
        ).astype(jnp.float32),
        lax.psum_scatter(
            part_up.astype(jnp.bfloat16), "node", scatter_dimension=1, tiled=True
        ).astype(jnp.float32),
    )
    hidden_share = (jax.nn.silu(gate_share) * up_share).astype(jnp.bfloat16)
    hidden = lax.all_gather(hidden_share, "node", axis=1, tiled=True)
    grad_hidden = lax.psum(part_grad.astype(jnp.bfloat16), "node").astype(jnp.float32)
    grad_gate, grad_up = backward_act(grad_hidden, stored_gate, stored_up)
    result_forward = jnp.dot(hidden, down_local, preferred_element_type=jnp.float32).astype(
        jnp.bfloat16
    )
    result_backward = lax.dot_general(
        grad_gate, gate_local, contract_last, preferred_element_type=jnp.float32
    )
    result_backward = result_backward + lax.dot_general(
        grad_up, up_local, contract_last, preferred_element_type=jnp.float32
    )
    result_backward = result_backward.astype(jnp.bfloat16)
    back_forward, back_backward = (
        lax.all_to_all(
            result_forward.reshape(experts, capacity, width),
            "dev",
            split_axis=0,
            concat_axis=0,
            tiled=True,
        ),
        lax.all_to_all(
            result_backward.reshape(experts, capacity, width),
            "dev",
            split_axis=0,
            concat_axis=0,
            tiled=True,
        ),
    )
    mixed_forward = combine_rows(token_rows, gates_forward[0], back_forward, targets_forward)
    mixed_backward = combine_rows(grad_rows, gates_backward[0], back_backward, targets_backward)
    next_forward = from_behind(mixed_forward[None], "section", 1)
    next_backward = from_behind(mixed_backward[None], "section", -1)
    return (next_forward, next_backward)


CONTRACT_LAST = (((1,), (1,)), ((), ()))
CONTRACT_FIRST = (((0,), (0,)), ((), ()))
VMEM = pl.BlockSpec(memory_space=pltpu.VMEM)
SMEM = pl.BlockSpec(memory_space=pltpu.SMEM)
VMEM_BYTES = 14 << 20
CF = 1.0
ANY = pl.BlockSpec(memory_space=pl.ANY)


def across(value, axis, mask):
    count = lax.axis_size(axis)
    return lax.ppermute(value, axis, [(source, source ^ mask) for source in range(count)])


def ring_order(count):
    return [0] + list(range(1, count, 2)) + list(range(2, count, 2))[::-1]


def ring_pairs(count, steps):
    order = ring_order(count)
    return [(order[i], order[(i + steps) % count]) for i in range(count)]


def along_ring(value, steps):
    return lax.ppermute(value, "dev", ring_pairs(lax.axis_size("dev"), steps))


def along_ring_and_sections(value, shift):
    count, sections = lax.axis_size("dev"), lax.axis_size("section")
    pairs = [
        (section * count + source, (section + shift) % sections * count + target)
        for section in range(sections)
        for source, target in ring_pairs(count, 1)
    ]
    return lax.ppermute(value, ("section", "dev"), pairs)


def block_behind(expert, count, steps):
    block = 0
    for target, source in ring_pairs(count, -steps):
        block = block + jnp.where(expert == target, source, 0)
    return block


def call(body, place, operands, after, out_shape, scratch, flops, aliases={}):
    def with_after(place_ref, *refs):
        body(place_ref, *refs[: len(operands)], *refs[len(operands) + len(after) :])

    touched = sum(array.size * array.dtype.itemsize for array in operands)
    return pl.pallas_call(
        with_after,
        in_specs=[SMEM] + [VMEM] * len(operands) + [ANY] * len(after),
        out_specs=jax.tree.map(lambda _: VMEM, out_shape),
        scratch_shapes=scratch,
        out_shape=out_shape,
        input_output_aliases={index + 1: out for index, out in aliases.items()},
        cost_estimate=pl.CostEstimate(flops=int(CF * flops), bytes_accessed=int(CF * touched), transcendentals=0),
        compiler_params=pltpu.CompilerParams(vmem_limit_bytes=VMEM_BYTES),
    )(place, *operands, *after)


def matmul(left, right, dims=(((1,), (0,)), ((), ()))):
    return lax.dot_general(left, right, dims, preferred_element_type=jnp.float32)


def by_owner(place_ref, rows_ref, sorted_rows, nodes):
    rows = sorted_rows.shape[0] // nodes
    for mask in range(nodes):
        first = pl.multiple_of((place_ref[0] ^ mask) * rows, rows)
        sorted_rows[mask * rows : (mask + 1) * rows, :] = rows_ref[pl.ds(first, rows), :]


def first_products(place, token_rows, grad_rows, weights, nodes, planes, after):
    (count, width), hidden = grad_rows.shape, weights[0].shape[1]
    share = count // nodes

    def body(place_ref, token_ref, grad_ref, gate_ref, up_ref, down_ref, *refs):
        outs, (sorted_tokens, sorted_grads) = refs[:nodes], refs[nodes:]
        by_owner(place_ref, token_ref, sorted_tokens, nodes)
        by_owner(place_ref, grad_ref, sorted_grads, nodes)
        parts = (
            matmul(sorted_tokens[...], gate_ref[...]),
            matmul(sorted_tokens[...], up_ref[...]),
            matmul(sorted_grads[...], down_ref[...], CONTRACT_LAST),
        )
        for index, part in enumerate(parts):
            for mask in range(nodes):
                outs[mask][index] = part[mask * share : (mask + 1) * share].astype(jnp.bfloat16)

    return call(
        body,
        place,
        (token_rows, grad_rows, *weights),
        after,
        [jax.ShapeDtypeStruct((planes, share, hidden), jnp.bfloat16)] * nodes,
        [pltpu.VMEM((count, width), jnp.bfloat16)] * 2,
        6 * count * width * hidden,
    )


def activations(place, pieces, filled, after):
    nodes, (_, share, hidden) = len(pieces), pieces[0].shape

    def body(place_ref, *refs):
        piece_refs, outs = refs[:nodes], refs[nodes + len(filled) :]
        gate, up, grad = (
            sum(ref[index].astype(jnp.float32) for ref in piece_refs) for index in range(3)
        )
        act = (gate / (1.0 + jnp.exp(-gate)) * up).astype(jnp.bfloat16)
        grad = grad.astype(jnp.bfloat16)
        for out in outs:
            planes = out.shape[0]
            out[planes - 2] = act
            out[planes - 1] = grad

    shapes = [jax.ShapeDtypeStruct(array.shape, array.dtype) for array in filled]
    return call(
        body,
        place,
        (*pieces, *filled),
        after,
        shapes or [jax.ShapeDtypeStruct((2, share, hidden), jnp.bfloat16)],
        [],
        16 * share * hidden,
        {nodes + index: index for index in range(len(filled))},
    )


def join(place_ref, piece_refs, index, joined):
    planes, rows, _ = piece_refs[0].shape
    for mask, ref in enumerate(piece_refs):
        first = pl.multiple_of((place_ref[0] ^ mask) * rows, rows)
        joined[pl.ds(first, rows), :] = ref[planes - 2 + index]


def with_info(place, rows, routes, gates):
    (count, width), chosen = rows.shape, routes[0].shape[0]
    height = -(-6 * chosen // 16) * 16

    def body(place_ref, rows_ref, *refs):
        infos, out = refs[:-1], refs[-1]
        lines = [ref[...].astype(jnp.float32) for ref in infos[:2]]
        for ref in infos[2:]:
            coarse = ref[...].astype(jnp.bfloat16).astype(jnp.float32)
            lines += [coarse, ref[...] - coarse]
        lines.append(jnp.zeros((height - 6 * chosen, count), jnp.float32))
        out[0:count, :] = rows_ref[...]
        out[count : count + height, :] = jnp.zeros((height, width), jnp.bfloat16)
        out[count : count + height, 0:count] = jnp.concatenate(lines).astype(jnp.bfloat16)

    return call(
        body,
        place,
        (rows, *routes, *gates),
        (),
        jax.ShapeDtypeStruct((count + height, width), jnp.bfloat16),
        [],
        rows.size,
    )


def info_of(ref, count, chosen, which):
    lines = ref[count:, 0:count].astype(jnp.float32)
    routes = lines[which * chosen : (which + 1) * chosen].astype(jnp.int32)
    first = 2 * (which + 1) * chosen
    return routes, lines[first : first + chosen] + lines[first + chosen : first + 2 * chosen]


def weight_column(expert, routes, gates):
    chosen, count = routes.shape
    line = jnp.zeros((1, count), jnp.float32)
    for choice in range(chosen):
        line += jnp.where(routes[choice : choice + 1] == expert, gates[choice : choice + 1], 0.0)
    diagonal = lax.broadcasted_iota(jnp.int32, (count, count), 0) == lax.broadcasted_iota(
        jnp.int32, (count, count), 1
    )
    return jnp.sum(jnp.where(diagonal, line, 0.0), axis=1, keepdims=True)


def slot_selection(expert, routes, capacity):
    chosen, count = routes.shape
    named = jnp.zeros((1, count), jnp.float32)
    for choice in range(chosen):
        named += (routes[choice : choice + 1] == expert).astype(jnp.float32)
    earlier = lax.broadcasted_iota(jnp.int32, (count, count), 0) < lax.broadcasted_iota(
        jnp.int32, (count, count), 1
    )
    rank = matmul(
        jnp.broadcast_to(named, (16, count)).astype(jnp.bfloat16),
        earlier.astype(jnp.float32).astype(jnp.bfloat16),
    )[0:1]
    slot = jnp.where(named > 0, rank, -1.0)
    slots = lax.broadcasted_iota(jnp.int32, (capacity, count), 0).astype(jnp.float32)
    return (slots == slot).astype(jnp.float32).astype(jnp.bfloat16)


def give(out, weight, result, added_refs):
    total = weight * result.astype(jnp.bfloat16).astype(jnp.float32)
    for ref in added_refs:
        total += ref[0 : out.shape[0], :].astype(jnp.float32)
    out[...] = total.astype(jnp.bfloat16)


def forward_results(place, pieces, w_down, info, chosen, added, after):
    nodes, (_, share, hidden), width = len(pieces), pieces[0].shape, w_down.shape[1]
    count = share * nodes

    def body(place_ref, *refs):
        piece_refs, refs = refs[:nodes], refs[nodes:]
        (down_ref, info_ref), added_refs, (out, joined) = refs[:2], refs[2:-2], refs[-2:]
        join(place_ref, piece_refs, 0, joined)
        weight = weight_column(place_ref[1], *info_of(info_ref, count, chosen, 0))
        give(out, weight, matmul(joined[...], down_ref[...]), added_refs)

    return call(
        body,
        place,
        (*pieces, w_down, info, *added),
        after,
        jax.ShapeDtypeStruct((count, width), jnp.bfloat16),
        [pltpu.VMEM((count, hidden), jnp.bfloat16)],
        2 * count * width * hidden,
    )


def backward_results(place, pieces, w_gate, w_up, saved_gate, saved_up, info, chosen, added, block, after):
    nodes, (_, share, hidden), width = len(pieces), pieces[0].shape, w_gate.shape[0]
    count = share * nodes
    experts = saved_gate.shape[0] // count

    def body(place_ref, *refs):
        piece_refs, refs = refs[:nodes], refs[nodes:]
        gate_ref, up_ref, saved_gate_ref, saved_up_ref, info_ref = refs[:5]
        added_refs, (out, joined) = refs[5:-2], refs[-2:]
        join(place_ref, piece_refs, 1, joined)
        expert = place_ref[1]
        routes, gates = info_of(info_ref, count, chosen, 1)
        weight = weight_column(expert, routes, gates)
        select = slot_selection(expert, routes, count)
        first = pl.multiple_of(block_behind(expert, experts, block) * count, count)
        grad_gate, grad_up = backward_act(
            joined[...].astype(jnp.float32),
            matmul(select, saved_gate_ref[pl.ds(first, count), :], CONTRACT_FIRST),
            matmul(select, saved_up_ref[pl.ds(first, count), :], CONTRACT_FIRST),
        )
        result = matmul(grad_gate, gate_ref[...], CONTRACT_LAST)
        result += matmul(grad_up, up_ref[...], CONTRACT_LAST)
        give(out, weight, result, added_refs)

    return call(
        body,
        place,
        (*pieces, w_gate, w_up, saved_gate, saved_up, info, *added),
        after,
        jax.ShapeDtypeStruct((count, width), jnp.bfloat16),
        [pltpu.VMEM((count, hidden), jnp.bfloat16)],
        4 * count * width * hidden,
    )


def ring_shards(
    inputs_forward,
    routes_forward,
    gates_forward,
    grads_backward,
    routes_backward,
    gates_backward,
    w_gate,
    w_up,
    w_down,
    saved_gate,
    saved_up,
):
    experts, nodes = lax.axis_size("dev"), lax.axis_size("node")
    place = jnp.stack([lax.axis_index("node"), lax.axis_index("dev")]).astype(jnp.int32)
    weights = (w_gate[0, 0], w_up[0, 0], w_down[0, 0])
    stored_gate, stored_up = saved_gate[0, 0], saved_up[0, 0]

    chosen = routes_forward.shape[2]
    tokens = [
        with_info(
            place,
            inputs_forward[0],
            (routes_forward[0].T, routes_backward[0].T),
            (gates_forward[0].T, gates_backward[0].T),
        )
    ]
    grads = [grads_backward[0]]
    for _ in range(1, experts):
        tokens.append(along_ring(tokens[-1], 1))
        grads.append(along_ring(grads[-1], 1))

    sent, arrived, done = [None] * (experts + 1), [None] * (experts + 1), []

    def exchange(turn, own):
        sent[turn] = own
        arrived[turn] = [own[0]] + [
            across(own[mask % len(own)], "node", mask) for mask in range(1, nodes)
        ]

    def first(step):
        planes = 3 if step == 0 else 5
        sent[step] = first_products(
            place, tokens[step], grads[step], weights, nodes, planes, done[-1:]
        )
        done.append(sent[step][0])
        if step == 0:
            exchange(0, sent[0])

    def middle(step):
        filled = sent[step + 1] if step + 1 < experts else ()
        own = activations(place, arrived[step], filled, done[-1:])
        done.append(own[0])
        exchange(step + 1, own)

    base, hops = [None, None], [(inputs_forward[0],), (grads_backward[0],)]

    def last(step, *kinds):
        for kind in kinds:
            pieces, added = arrived[step + 1], hops[kind]
            if kind == 0:
                value = forward_results(
                    place, pieces, weights[2], tokens[step], chosen, added, done[-1:]
                )
            else:
                value = backward_results(
                    place, pieces, *weights[:2], stored_gate, stored_up, tokens[step], chosen, added, step, done[-1:]
                )
            done.append(value)
            if step == 0:
                base[kind], hops[kind] = from_behind(value, "section", 1 - 2 * kind), ()
            elif step < experts - 1:
                hops[kind] = (along_ring(value, 1),)
            else:
                hops[kind] = (along_ring_and_sections(value, 1 - 2 * kind),)

    first(0)
    first(1)
    middle(0)
    for turn in range(1, experts - 1):
        if turn >= 2:
            last(turn - 2, 0, 1)
        first(turn + 1)
        middle(turn)
    if experts >= 3:
        last(experts - 3, 0, 1)
    last(experts - 2, 0)
    middle(experts - 1)
    last(experts - 2, 1)
    last(experts - 1, 0, 1)
    return tuple(
        (own.astype(jnp.float32) + others[0].astype(jnp.float32)).astype(jnp.bfloat16)[None]
        for own, others in zip(base, hops)
    )


def power_of_two(number):
    return number & (number - 1) == 0


def shards(*args):
    experts, nodes = lax.axis_size("dev"), lax.axis_size("node")
    tokens, capacity = args[0].shape[1], args[9].shape[2] // experts
    if capacity == tokens and experts > 1 and power_of_two(nodes) and tokens % (16 * nodes) == 0:
        return ring_shards(*args)
    return shards_by_slots(*args)


def solution(mesh):
    return jax.shard_map(
        shards,
        mesh=mesh,
        in_specs=(
            P("section", "dev", "node"),
            P("section", "dev", None),
            P("section", "dev", None),
            P("section", "dev", "node"),
            P("section", "dev", None),
            P("section", "dev", None),
            P("section", "dev", "node", None),
            P("section", "dev", "node", None),
            P("section", "dev", None, "node"),
            P("section", "dev", None, None),
            P("section", "dev", None, None),
        ),
        out_specs=(P("section", "dev", "node"), P("section", "dev", "node")),
        check_vma=False,
    )
```

```python
import functools

import jax
import jax.numpy as jnp
from jax import lax
from jax.experimental import pallas as pl
from jax.experimental.pallas import tpu as pltpu
from jax.sharding import PartitionSpec as P


def from_behind(value, axis, steps):
    count = lax.axis_size(axis)
    pairs = [(source, (source + steps) % count) for source in range(count)]
    return lax.ppermute(value, axis, pairs)


def slot_targets(routing, experts, capacity):
    flat = routing.reshape(-1)
    onehot = (flat[:, None] == jnp.arange(experts, dtype=jnp.int32)[None, :]).astype(jnp.int32)
    earlier = jnp.cumsum(onehot, axis=0) - onehot
    return flat * capacity + jnp.sum(earlier * onehot, axis=1)


def pack_rows(token_rows, targets, slot_count, chosen):
    match = (jnp.arange(slot_count, dtype=jnp.int32)[:, None] == targets[None, :]).astype(
        jnp.bfloat16
    )
    select = jnp.sum(match.reshape(slot_count, token_rows.shape[0], chosen), axis=2)
    return jnp.dot(select, token_rows, preferred_element_type=jnp.float32).astype(jnp.bfloat16)


def combine_rows(token_rows, weights_of, returned_rows, targets):
    width = token_rows.shape[1]
    picked = returned_rows.reshape(-1, width)[targets]
    picked = picked.reshape(token_rows.shape[0], weights_of.shape[1], width).astype(jnp.float32)
    mixed = token_rows.astype(jnp.float32) + jnp.sum(weights_of[:, :, None] * picked, axis=1)
    return mixed.astype(jnp.bfloat16)


def backward_act(grad_hidden, stored_gate, stored_up):
    act_gate = stored_gate.astype(jnp.float32)
    act_up = stored_up.astype(jnp.float32)
    squash = jax.nn.sigmoid(act_gate)
    grad_gate = (grad_hidden * act_up * squash * (1.0 + act_gate * (1.0 - squash))).astype(
        jnp.bfloat16
    )
    grad_up = (grad_hidden * act_gate * squash).astype(jnp.bfloat16)
    return (grad_gate, grad_up)


def shards_by_slots(
    inputs_forward,
    routes_forward,
    gates_forward,
    grads_backward,
    routes_backward,
    gates_backward,
    w_gate,
    w_up,
    w_down,
    saved_gate,
    saved_up,
):
    experts = lax.axis_size("dev")
    chosen = routes_forward.shape[2]
    token_rows = inputs_forward[0]
    grad_rows = grads_backward[0]
    slot_total = saved_gate.shape[2]
    capacity = slot_total // experts
    width = token_rows.shape[1]
    targets_forward = slot_targets(routes_forward[0], experts, capacity)
    targets_backward = slot_targets(routes_backward[0], experts, capacity)
    sent_forward = pack_rows(token_rows, targets_forward, slot_total, chosen).reshape(
        experts, capacity, width
    )
    sent_backward = pack_rows(grad_rows, targets_backward, slot_total, chosen).reshape(
        experts, capacity, width
    )
    arrived_forward, arrived_backward = (
        lax.all_to_all(sent_forward, "dev", split_axis=0, concat_axis=0, tiled=True),
        lax.all_to_all(sent_backward, "dev", split_axis=0, concat_axis=0, tiled=True),
    )
    arrived_forward = arrived_forward.reshape(slot_total, width)
    arrived_backward = arrived_backward.reshape(slot_total, width)
    gate_local = w_gate[0, 0]
    up_local = w_up[0, 0]
    down_local = w_down[0, 0]
    stored_gate = saved_gate[0, 0]
    stored_up = saved_up[0, 0]
    contract_last = (((1,), (1,)), ((), ()))
    part_gate = jnp.dot(arrived_forward, gate_local, preferred_element_type=jnp.float32)
    part_up = jnp.dot(arrived_forward, up_local, preferred_element_type=jnp.float32)
    part_grad = lax.dot_general(
        arrived_backward, down_local, contract_last, preferred_element_type=jnp.float32
    )
    gate_share, up_share = (
        lax.psum_scatter(
            part_gate.astype(jnp.bfloat16), "node", scatter_dimension=1, tiled=True
        ).astype(jnp.float32),
        lax.psum_scatter(
            part_up.astype(jnp.bfloat16), "node", scatter_dimension=1, tiled=True
        ).astype(jnp.float32),
    )
    hidden_share = (jax.nn.silu(gate_share) * up_share).astype(jnp.bfloat16)
    hidden = lax.all_gather(hidden_share, "node", axis=1, tiled=True)
    grad_hidden = lax.psum(part_grad.astype(jnp.bfloat16), "node").astype(jnp.float32)
    grad_gate, grad_up = backward_act(grad_hidden, stored_gate, stored_up)
    result_forward = jnp.dot(hidden, down_local, preferred_element_type=jnp.float32).astype(
        jnp.bfloat16
    )
    result_backward = lax.dot_general(
        grad_gate, gate_local, contract_last, preferred_element_type=jnp.float32
    )
    result_backward = result_backward + lax.dot_general(
        grad_up, up_local, contract_last, preferred_element_type=jnp.float32
    )
    result_backward = result_backward.astype(jnp.bfloat16)
    back_forward, back_backward = (
        lax.all_to_all(
            result_forward.reshape(experts, capacity, width),
            "dev",
            split_axis=0,
            concat_axis=0,
            tiled=True,
        ),
        lax.all_to_all(
            result_backward.reshape(experts, capacity, width),
            "dev",
            split_axis=0,
            concat_axis=0,
            tiled=True,
        ),
    )
    mixed_forward = combine_rows(token_rows, gates_forward[0], back_forward, targets_forward)
    mixed_backward = combine_rows(grad_rows, gates_backward[0], back_backward, targets_backward)
    next_forward = from_behind(mixed_forward[None], "section", 1)
    next_backward = from_behind(mixed_backward[None], "section", -1)
    return (next_forward, next_backward)


CONTRACT_LAST = (((1,), (1,)), ((), ()))
CONTRACT_FIRST = (((0,), (0,)), ((), ()))
VMEM = pl.BlockSpec(memory_space=pltpu.VMEM)
SMEM = pl.BlockSpec(memory_space=pltpu.SMEM)
VMEM_BYTES = 14 << 20
CF = 100.0
WIDE_BYTES = 56 << 20
ANY = pl.BlockSpec(memory_space=pl.ANY)
HBM = pl.BlockSpec(memory_space=pltpu.HBM)


def across(value, axis, mask):
    count = lax.axis_size(axis)
    return lax.ppermute(value, axis, [(source, source ^ mask) for source in range(count)])


def ring_order(count):
    return [0] + list(range(1, count, 2)) + list(range(2, count, 2))[::-1]


def ring_pairs(count, steps):
    order = ring_order(count)
    return [(order[i], order[(i + steps) % count]) for i in range(count)]


def along_ring(value, steps):
    return lax.ppermute(value, "dev", ring_pairs(lax.axis_size("dev"), steps))


def along_ring_and_sections(value, shift):
    count, sections = lax.axis_size("dev"), lax.axis_size("section")
    pairs = [
        (section * count + source, (section + shift) % sections * count + target)
        for section in range(sections)
        for source, target in ring_pairs(count, 1)
    ]
    return lax.ppermute(value, ("section", "dev"), pairs)


def block_behind(expert, count, steps):
    block = 0
    for target, source in ring_pairs(count, -steps):
        block = block + jnp.where(expert == target, source, 0)
    return block


def call(body, place, operands, after, out_shape, scratch, flops, aliases={}):
    def with_after(place_ref, *refs):
        body(place_ref, *refs[: len(operands)], *refs[len(operands) + len(after) :])

    touched = sum(array.size * array.dtype.itemsize for array in operands)
    return pl.pallas_call(
        with_after,
        in_specs=[SMEM] + [VMEM] * len(operands) + [ANY] * len(after),
        out_specs=jax.tree.map(lambda _: VMEM, out_shape),
        scratch_shapes=scratch,
        out_shape=out_shape,
        input_output_aliases={index + 1: out for index, out in aliases.items()},
        cost_estimate=pl.CostEstimate(flops=int(CF * flops), bytes_accessed=int(CF * touched), transcendentals=0),
        compiler_params=pltpu.CompilerParams(vmem_limit_bytes=VMEM_BYTES),
    )(place, *operands, *after)


def matmul(left, right, dims=(((1,), (0,)), ((), ()))):
    return lax.dot_general(left, right, dims, preferred_element_type=jnp.float32)


def by_owner(place_ref, rows_ref, sorted_rows, nodes):
    rows = sorted_rows.shape[0] // nodes
    for mask in range(nodes):
        first = pl.multiple_of((place_ref[0] ^ mask) * rows, rows)
        sorted_rows[mask * rows : (mask + 1) * rows, :] = rows_ref[pl.ds(first, rows), :]


def first_products(place, token_rows, grad_rows, weights, nodes, planes, after):
    (count, width), hidden = grad_rows.shape, weights[0].shape[1]
    share = count // nodes

    def body(place_ref, token_ref, grad_ref, gate_ref, up_ref, down_ref, *refs):
        outs, (sorted_tokens, sorted_grads) = refs[:nodes], refs[nodes:]
        by_owner(place_ref, token_ref, sorted_tokens, nodes)
        by_owner(place_ref, grad_ref, sorted_grads, nodes)
        parts = (
            matmul(sorted_tokens[...], gate_ref[...]),
            matmul(sorted_tokens[...], up_ref[...]),
            matmul(sorted_grads[...], down_ref[...], CONTRACT_LAST),
        )
        for index, part in enumerate(parts):
            for mask in range(nodes):
                outs[mask][index] = part[mask * share : (mask + 1) * share].astype(jnp.bfloat16)

    return call(
        body,
        place,
        (token_rows, grad_rows, *weights),
        after,
        [jax.ShapeDtypeStruct((planes, share, hidden), jnp.bfloat16)] * nodes,
        [pltpu.VMEM((count, width), jnp.bfloat16)] * 2,
        6 * count * width * hidden,
    )


def activations(place, pieces, filled, after):
    nodes, (_, share, hidden) = len(pieces), pieces[0].shape

    def body(place_ref, *refs):
        piece_refs, outs = refs[:nodes], refs[nodes + len(filled) :]
        gate, up, grad = (
            sum(ref[index].astype(jnp.float32) for ref in piece_refs) for index in range(3)
        )
        act = (gate / (1.0 + jnp.exp(-gate)) * up).astype(jnp.bfloat16)
        grad = grad.astype(jnp.bfloat16)
        for out in outs:
            planes = out.shape[0]
            out[planes - 2] = act
            out[planes - 1] = grad

    shapes = [jax.ShapeDtypeStruct(array.shape, array.dtype) for array in filled]
    return call(
        body,
        place,
        (*pieces, *filled),
        after,
        shapes or [jax.ShapeDtypeStruct((2, share, hidden), jnp.bfloat16)],
        [],
        16 * share * hidden,
        {nodes + index: index for index in range(len(filled))},
    )


def join(place_ref, piece_refs, index, joined):
    planes, rows, _ = piece_refs[0].shape
    for mask, ref in enumerate(piece_refs):
        first = pl.multiple_of((place_ref[0] ^ mask) * rows, rows)
        joined[pl.ds(first, rows), :] = ref[planes - 2 + index]


def copied(sources, targets, sems):
    copies = [
        pltpu.make_async_copy(source, target, sems.at[index])
        for index, (source, target) in enumerate(zip(sources, targets))
    ]
    for copy in copies:
        copy.start()
    return copies


def with_info(rows, routes, gates):
    (count, width), chosen = rows.shape, routes[0].shape[0]
    height = -(-6 * chosen // 16) * 16
    small = (*routes, *gates)

    def body(*refs):
        inputs, out, held, sems = refs[:5], refs[5], refs[6:10], refs[10]
        targets = (out.at[pl.ds(0, count)], *held)
        for copy in copied(inputs, targets, sems):
            copy.wait()
        lines = [ref[...].astype(jnp.float32) for ref in held[:2]]
        for ref in held[2:]:
            coarse = ref[...].astype(jnp.bfloat16).astype(jnp.float32)
            lines += [coarse, ref[...] - coarse]
        lines.append(jnp.zeros((height - 6 * chosen, count), jnp.float32))
        out[count:, :] = jnp.zeros((height, width), jnp.bfloat16)
        out[count:, 0:count] = jnp.concatenate(lines).astype(jnp.bfloat16)

    return pl.pallas_call(
        body,
        in_specs=[HBM] * 5,
        out_specs=VMEM,
        out_shape=jax.ShapeDtypeStruct((count + height, width), jnp.bfloat16),
        scratch_shapes=[pltpu.VMEM(value.shape, value.dtype) for value in small]
        + [pltpu.SemaphoreType.DMA((5,))],
        compiler_params=pltpu.CompilerParams(vmem_limit_bytes=WIDE_BYTES),
    )(rows, *small)


def opening_products(place, token_rows, grad_rows, weights, nodes):
    (count, width), hidden = grad_rows.shape, weights[0].shape[1]
    share = count // nodes
    operands = (token_rows, weights[0], weights[1], grad_rows, weights[2])
    cuts = 4

    def body(place_ref, *refs):
        inputs, pieces, held = refs[:5], refs[5 : 5 + nodes], refs[5 + nodes : 10 + nodes]
        sorted_rows, sems = refs[10 + nodes :]

        def pieces_of(ref):
            rows = ref.shape[0] // cuts
            return [ref.at[pl.ds(cut * rows, rows)] for cut in range(cuts)]

        parts = [
            copied(pieces_of(source), pieces_of(target), sems.at[index])
            for index, (source, target) in enumerate(zip(inputs, held))
        ]

        def wait(index):
            for copy in parts[index]:
                copy.wait()

        def give(index, part):
            for mask in range(nodes):
                pieces[mask][index] = part[mask * share : (mask + 1) * share].astype(jnp.bfloat16)

        wait(0)
        by_owner(place_ref, held[0], sorted_rows, nodes)
        for index in (0, 1):
            wait(index + 1)
            give(index, matmul(sorted_rows[...], held[index + 1][...]))
        wait(3)
        by_owner(place_ref, held[3], sorted_rows, nodes)
        wait(4)
        give(2, matmul(sorted_rows[...], held[4][...], CONTRACT_LAST))

    return pl.pallas_call(
        body,
        in_specs=[SMEM] + [HBM] * 5,
        out_specs=[VMEM] * nodes,
        out_shape=[jax.ShapeDtypeStruct((3, share, hidden), jnp.bfloat16)] * nodes,
        scratch_shapes=[pltpu.VMEM(value.shape, value.dtype) for value in operands]
        + [pltpu.VMEM((count, width), jnp.bfloat16), pltpu.SemaphoreType.DMA((5, cuts))],
        cost_estimate=pl.CostEstimate(
            flops=int(CF * 6 * count * width * hidden),
            bytes_accessed=int(CF * 6 * width * hidden),
            transcendentals=0,
        ),
        compiler_params=pltpu.CompilerParams(vmem_limit_bytes=WIDE_BYTES),
    )(place, *operands)


def info_of(ref, count, chosen, which):
    lines = ref[count:, 0:count].astype(jnp.float32)
    routes = lines[which * chosen : (which + 1) * chosen].astype(jnp.int32)
    first = 2 * (which + 1) * chosen
    return routes, lines[first : first + chosen] + lines[first + chosen : first + 2 * chosen]


def weight_column(expert, routes, gates):
    chosen, count = routes.shape
    line = jnp.zeros((1, count), jnp.float32)
    for choice in range(chosen):
        line += jnp.where(routes[choice : choice + 1] == expert, gates[choice : choice + 1], 0.0)
    diagonal = lax.broadcasted_iota(jnp.int32, (count, count), 0) == lax.broadcasted_iota(
        jnp.int32, (count, count), 1
    )
    return jnp.sum(jnp.where(diagonal, line, 0.0), axis=1, keepdims=True)


def slot_selection(expert, routes, capacity):
    chosen, count = routes.shape
    named = jnp.zeros((1, count), jnp.float32)
    for choice in range(chosen):
        named += (routes[choice : choice + 1] == expert).astype(jnp.float32)
    earlier = lax.broadcasted_iota(jnp.int32, (count, count), 0) < lax.broadcasted_iota(
        jnp.int32, (count, count), 1
    )
    rank = matmul(
        jnp.broadcast_to(named, (16, count)).astype(jnp.bfloat16),
        earlier.astype(jnp.float32).astype(jnp.bfloat16),
    )[0:1]
    slot = jnp.where(named > 0, rank, -1.0)
    slots = lax.broadcasted_iota(jnp.int32, (capacity, count), 0).astype(jnp.float32)
    return (slots == slot).astype(jnp.float32).astype(jnp.bfloat16)


def give(out, weight, result, added_refs):
    total = weight * result.astype(jnp.bfloat16).astype(jnp.float32)
    for ref in added_refs:
        total += ref[0 : out.shape[0], :].astype(jnp.float32)
    out[...] = total.astype(jnp.bfloat16)


def forward_results(place, pieces, w_down, info, chosen, added, after):
    nodes, (_, share, hidden), width = len(pieces), pieces[0].shape, w_down.shape[1]
    count = share * nodes

    def body(place_ref, *refs):
        piece_refs, refs = refs[:nodes], refs[nodes:]
        (down_ref, info_ref), added_refs, (out, joined) = refs[:2], refs[2:-2], refs[-2:]
        join(place_ref, piece_refs, 0, joined)
        weight = weight_column(place_ref[1], *info_of(info_ref, count, chosen, 0))
        give(out, weight, matmul(joined[...], down_ref[...]), added_refs)

    return call(
        body,
        place,
        (*pieces, w_down, info, *added),
        after,
        jax.ShapeDtypeStruct((count, width), jnp.bfloat16),
        [pltpu.VMEM((count, hidden), jnp.bfloat16)],
        2 * count * width * hidden,
    )


def backward_results(place, pieces, w_gate, w_up, saved_gate, saved_up, info, chosen, added, block, after):
    nodes, (_, share, hidden), width = len(pieces), pieces[0].shape, w_gate.shape[0]
    count = share * nodes
    experts = saved_gate.shape[0] // count

    def body(place_ref, *refs):
        piece_refs, refs = refs[:nodes], refs[nodes:]
        gate_ref, up_ref, saved_gate_ref, saved_up_ref, info_ref = refs[:5]
        added_refs, (out, joined) = refs[5:-2], refs[-2:]
        join(place_ref, piece_refs, 1, joined)
        expert = place_ref[1]
        routes, gates = info_of(info_ref, count, chosen, 1)
        weight = weight_column(expert, routes, gates)
        select = slot_selection(expert, routes, count)
        first = pl.multiple_of(block_behind(expert, experts, block) * count, count)
        grad_gate, grad_up = backward_act(
            joined[...].astype(jnp.float32),
            matmul(select, saved_gate_ref[pl.ds(first, count), :], CONTRACT_FIRST),
            matmul(select, saved_up_ref[pl.ds(first, count), :], CONTRACT_FIRST),
        )
        result = matmul(grad_gate, gate_ref[...], CONTRACT_LAST)
        result += matmul(grad_up, up_ref[...], CONTRACT_LAST)
        give(out, weight, result, added_refs)

    return call(
        body,
        place,
        (*pieces, w_gate, w_up, saved_gate, saved_up, info, *added),
        after,
        jax.ShapeDtypeStruct((count, width), jnp.bfloat16),
        [pltpu.VMEM((count, hidden), jnp.bfloat16)],
        4 * count * width * hidden,
    )


def ring_shards(
    inputs_forward,
    routes_forward,
    gates_forward,
    grads_backward,
    routes_backward,
    gates_backward,
    w_gate,
    w_up,
    w_down,
    saved_gate,
    saved_up,
):
    experts, nodes = lax.axis_size("dev"), lax.axis_size("node")
    place = jnp.stack([lax.axis_index("node"), lax.axis_index("dev")]).astype(jnp.int32)
    weights = (w_gate[0, 0], w_up[0, 0], w_down[0, 0])
    stored_gate, stored_up = saved_gate[0, 0], saved_up[0, 0]

    chosen = routes_forward.shape[2]
    tokens = [
        with_info(
            inputs_forward[0],
            (routes_forward[0].T, routes_backward[0].T),
            (gates_forward[0].T, gates_backward[0].T),
        )
    ]
    grads = [grads_backward[0]]
    for _ in range(1, experts):
        tokens.append(along_ring(tokens[-1], 1))
        grads.append(along_ring(grads[-1], 1))

    sent, arrived, done = [None] * (experts + 1), [None] * (experts + 1), []

    def exchange(turn, own):
        sent[turn] = own
        arrived[turn] = [own[0]] + [
            across(own[mask % len(own)], "node", mask) for mask in range(1, nodes)
        ]

    def first(step):
        if step == 0:
            sent[0] = opening_products(
                place, inputs_forward[0], grads_backward[0], weights, nodes
            )
        else:
            sent[step] = first_products(
                place, tokens[step], grads[step], weights, nodes, 5, done[-1:]
            )
        done.append(sent[step][0])
        if step == 0:
            exchange(0, sent[0])

    def middle(step):
        filled = sent[step + 1] if step + 1 < experts else ()
        own = activations(place, arrived[step], filled, done[-1:])
        done.append(own[0])
        exchange(step + 1, own)

    base, hops = [None, None], [(inputs_forward[0],), (grads_backward[0],)]

    def last(step, *kinds):
        for kind in kinds:
            pieces, added = arrived[step + 1], hops[kind]
            if kind == 0:
                value = forward_results(
                    place, pieces, weights[2], tokens[step], chosen, added, done[-1:]
                )
            else:
                value = backward_results(
                    place, pieces, *weights[:2], stored_gate, stored_up, tokens[step], chosen, added, step, done[-1:]
                )
            done.append(value)
            if step == 0:
                base[kind], hops[kind] = from_behind(value, "section", 1 - 2 * kind), ()
            elif step < experts - 1:
                hops[kind] = (along_ring(value, 1),)
            else:
                hops[kind] = (along_ring_and_sections(value, 1 - 2 * kind),)

    first(0)
    first(1)
    middle(0)
    for turn in range(1, experts - 1):
        if turn >= 2:
            last(turn - 2, 0, 1)
        first(turn + 1)
        middle(turn)
    if experts >= 3:
        last(experts - 3, 0, 1)
    last(experts - 2, 0)
    middle(experts - 1)
    last(experts - 2, 1)
    last(experts - 1, 0, 1)
    return tuple(
        (own.astype(jnp.float32) + others[0].astype(jnp.float32)).astype(jnp.bfloat16)[None]
        for own, others in zip(base, hops)
    )


def power_of_two(number):
    return number & (number - 1) == 0


def shards(*args):
    experts, nodes = lax.axis_size("dev"), lax.axis_size("node")
    tokens, capacity = args[0].shape[1], args[9].shape[2] // experts
    if capacity == tokens and experts > 1 and power_of_two(nodes) and tokens % (16 * nodes) == 0:
        return ring_shards(*args)
    return shards_by_slots(*args)


def solution(mesh):
    return jax.shard_map(
        shards,
        mesh=mesh,
        in_specs=(
            P("section", "dev", "node"),
            P("section", "dev", None),
            P("section", "dev", None),
            P("section", "dev", "node"),
            P("section", "dev", None),
            P("section", "dev", None),
            P("section", "dev", "node", None),
            P("section", "dev", "node", None),
            P("section", "dev", None, "node"),
            P("section", "dev", None, None),
            P("section", "dev", None, None),
        ),
        out_specs=(P("section", "dev", "node"), P("section", "dev", "node")),
        check_vma=False,
    )
```

```python
import functools

import jax
import jax.numpy as jnp
from jax import lax
from jax.experimental import pallas as pl
from jax.experimental.pallas import tpu as pltpu
from jax.sharding import PartitionSpec as P


def from_behind(value, axis, steps):
    count = lax.axis_size(axis)
    pairs = [(source, (source + steps) % count) for source in range(count)]
    return lax.ppermute(value, axis, pairs)


def slot_targets(routing, experts, capacity):
    flat = routing.reshape(-1)
    onehot = (flat[:, None] == jnp.arange(experts, dtype=jnp.int32)[None, :]).astype(jnp.int32)
    earlier = jnp.cumsum(onehot, axis=0) - onehot
    return flat * capacity + jnp.sum(earlier * onehot, axis=1)


def pack_rows(token_rows, targets, slot_count, chosen):
    match = (jnp.arange(slot_count, dtype=jnp.int32)[:, None] == targets[None, :]).astype(
        jnp.bfloat16
    )
    select = jnp.sum(match.reshape(slot_count, token_rows.shape[0], chosen), axis=2)
    return jnp.dot(select, token_rows, preferred_element_type=jnp.float32).astype(jnp.bfloat16)


def combine_rows(token_rows, weights_of, returned_rows, targets):
    width = token_rows.shape[1]
    picked = returned_rows.reshape(-1, width)[targets]
    picked = picked.reshape(token_rows.shape[0], weights_of.shape[1], width).astype(jnp.float32)
    mixed = token_rows.astype(jnp.float32) + jnp.sum(weights_of[:, :, None] * picked, axis=1)
    return mixed.astype(jnp.bfloat16)


def backward_act(grad_hidden, stored_gate, stored_up):
    act_gate = stored_gate.astype(jnp.float32)
    act_up = stored_up.astype(jnp.float32)
    squash = jax.nn.sigmoid(act_gate)
    grad_gate = (grad_hidden * act_up * squash * (1.0 + act_gate * (1.0 - squash))).astype(
        jnp.bfloat16
    )
    grad_up = (grad_hidden * act_gate * squash).astype(jnp.bfloat16)
    return (grad_gate, grad_up)


def shards_by_slots(
    inputs_forward,
    routes_forward,
    gates_forward,
    grads_backward,
    routes_backward,
    gates_backward,
    w_gate,
    w_up,
    w_down,
    saved_gate,
    saved_up,
):
    experts = lax.axis_size("dev")
    chosen = routes_forward.shape[2]
    token_rows = inputs_forward[0]
    grad_rows = grads_backward[0]
    slot_total = saved_gate.shape[2]
    capacity = slot_total // experts
    width = token_rows.shape[1]
    targets_forward = slot_targets(routes_forward[0], experts, capacity)
    targets_backward = slot_targets(routes_backward[0], experts, capacity)
    sent_forward = pack_rows(token_rows, targets_forward, slot_total, chosen).reshape(
        experts, capacity, width
    )
    sent_backward = pack_rows(grad_rows, targets_backward, slot_total, chosen).reshape(
        experts, capacity, width
    )
    arrived_forward, arrived_backward = (
        lax.all_to_all(sent_forward, "dev", split_axis=0, concat_axis=0, tiled=True),
        lax.all_to_all(sent_backward, "dev", split_axis=0, concat_axis=0, tiled=True),
    )
    arrived_forward = arrived_forward.reshape(slot_total, width)
    arrived_backward = arrived_backward.reshape(slot_total, width)
    gate_local = w_gate[0, 0]
    up_local = w_up[0, 0]
    down_local = w_down[0, 0]
    stored_gate = saved_gate[0, 0]
    stored_up = saved_up[0, 0]
    contract_last = (((1,), (1,)), ((), ()))
    part_gate = jnp.dot(arrived_forward, gate_local, preferred_element_type=jnp.float32)
    part_up = jnp.dot(arrived_forward, up_local, preferred_element_type=jnp.float32)
    part_grad = lax.dot_general(
        arrived_backward, down_local, contract_last, preferred_element_type=jnp.float32
    )
    gate_share, up_share = (
        lax.psum_scatter(
            part_gate.astype(jnp.bfloat16), "node", scatter_dimension=1, tiled=True
        ).astype(jnp.float32),
        lax.psum_scatter(
            part_up.astype(jnp.bfloat16), "node", scatter_dimension=1, tiled=True
        ).astype(jnp.float32),
    )
    hidden_share = (jax.nn.silu(gate_share) * up_share).astype(jnp.bfloat16)
    hidden = lax.all_gather(hidden_share, "node", axis=1, tiled=True)
    grad_hidden = lax.psum(part_grad.astype(jnp.bfloat16), "node").astype(jnp.float32)
    grad_gate, grad_up = backward_act(grad_hidden, stored_gate, stored_up)
    result_forward = jnp.dot(hidden, down_local, preferred_element_type=jnp.float32).astype(
        jnp.bfloat16
    )
    result_backward = lax.dot_general(
        grad_gate, gate_local, contract_last, preferred_element_type=jnp.float32
    )
    result_backward = result_backward + lax.dot_general(
        grad_up, up_local, contract_last, preferred_element_type=jnp.float32
    )
    result_backward = result_backward.astype(jnp.bfloat16)
    back_forward, back_backward = (
        lax.all_to_all(
            result_forward.reshape(experts, capacity, width),
            "dev",
            split_axis=0,
            concat_axis=0,
            tiled=True,
        ),
        lax.all_to_all(
            result_backward.reshape(experts, capacity, width),
            "dev",
            split_axis=0,
            concat_axis=0,
            tiled=True,
        ),
    )
    mixed_forward = combine_rows(token_rows, gates_forward[0], back_forward, targets_forward)
    mixed_backward = combine_rows(grad_rows, gates_backward[0], back_backward, targets_backward)
    next_forward = from_behind(mixed_forward[None], "section", 1)
    next_backward = from_behind(mixed_backward[None], "section", -1)
    return (next_forward, next_backward)


CONTRACT_LAST = (((1,), (1,)), ((), ()))
CONTRACT_FIRST = (((0,), (0,)), ((), ()))
VMEM = pl.BlockSpec(memory_space=pltpu.VMEM)
SMEM = pl.BlockSpec(memory_space=pltpu.SMEM)
VMEM_BYTES = 14 << 20
CF = 1.0
SUM_COST = 1e10
WIDE_BYTES = 56 << 20
ANY = pl.BlockSpec(memory_space=pl.ANY)
HBM = pl.BlockSpec(memory_space=pltpu.HBM)


def across(value, axis, mask):
    count = lax.axis_size(axis)
    return lax.ppermute(value, axis, [(source, source ^ mask) for source in range(count)])


def ring_order(count):
    return [0] + list(range(1, count, 2)) + list(range(2, count, 2))[::-1]


def ring_pairs(count, steps):
    order = ring_order(count)
    return [(order[i], order[(i + steps) % count]) for i in range(count)]


def along_ring(value, steps):
    return lax.ppermute(value, "dev", ring_pairs(lax.axis_size("dev"), steps))


def along_ring_and_sections(value, steps, shift):
    count, sections = lax.axis_size("dev"), lax.axis_size("section")
    pairs = [
        (section * count + source, (section + shift) % sections * count + target)
        for section in range(sections)
        for source, target in ring_pairs(count, steps)
    ]
    return lax.ppermute(value, ("section", "dev"), pairs)


def block_behind(expert, count, steps):
    block = 0
    for target, source in ring_pairs(count, -steps):
        block = block + jnp.where(expert == target, source, 0)
    return block


def call(body, place, operands, after, out_shape, scratch, flops, aliases={}):
    def with_after(place_ref, *refs):
        body(place_ref, *refs[: len(operands)], *refs[len(operands) + len(after) :])

    touched = sum(array.size * array.dtype.itemsize for array in operands)
    return pl.pallas_call(
        with_after,
        in_specs=[SMEM] + [VMEM] * len(operands) + [ANY] * len(after),
        out_specs=jax.tree.map(lambda _: VMEM, out_shape),
        scratch_shapes=scratch,
        out_shape=out_shape,
        input_output_aliases={index + 1: out for index, out in aliases.items()},
        cost_estimate=pl.CostEstimate(flops=int(CF * flops), bytes_accessed=int(CF * touched), transcendentals=0),
        compiler_params=pltpu.CompilerParams(vmem_limit_bytes=VMEM_BYTES),
    )(place, *operands, *after)


def matmul(left, right, dims=(((1,), (0,)), ((), ()))):
    return lax.dot_general(left, right, dims, preferred_element_type=jnp.float32)


def by_owner(place_ref, rows_ref, sorted_rows, nodes):
    rows = sorted_rows.shape[0] // nodes
    for mask in range(nodes):
        first = pl.multiple_of((place_ref[0] ^ mask) * rows, rows)
        sorted_rows[mask * rows : (mask + 1) * rows, :] = rows_ref[pl.ds(first, rows), :]


def first_products(place, token_rows, grad_rows, weights, nodes, planes, after):
    (count, width), hidden = grad_rows.shape, weights[0].shape[1]
    share = count // nodes

    def body(place_ref, token_ref, grad_ref, gate_ref, up_ref, down_ref, *refs):
        outs, (sorted_tokens, sorted_grads) = refs[:nodes], refs[nodes:]
        by_owner(place_ref, token_ref, sorted_tokens, nodes)
        by_owner(place_ref, grad_ref, sorted_grads, nodes)
        parts = (
            matmul(sorted_tokens[...], gate_ref[...]),
            matmul(sorted_tokens[...], up_ref[...]),
            matmul(sorted_grads[...], down_ref[...], CONTRACT_LAST),
        )
        for index, part in enumerate(parts):
            for mask in range(nodes):
                outs[mask][index] = part[mask * share : (mask + 1) * share].astype(jnp.bfloat16)

    return call(
        body,
        place,
        (token_rows, grad_rows, *weights),
        after,
        [jax.ShapeDtypeStruct((planes, share, hidden), jnp.bfloat16)] * nodes,
        [pltpu.VMEM((count, width), jnp.bfloat16)] * 2,
        6 * count * width * hidden,
    )


def activations(place, pieces, filled, after):
    nodes, (_, share, hidden) = len(pieces), pieces[0].shape

    def body(place_ref, *refs):
        piece_refs, outs = refs[:nodes], refs[nodes + len(filled) :]
        gate, up, grad = (
            sum(ref[index].astype(jnp.float32) for ref in piece_refs) for index in range(3)
        )
        act = (gate / (1.0 + jnp.exp(-gate)) * up).astype(jnp.bfloat16)
        grad = grad.astype(jnp.bfloat16)
        for out in outs:
            planes = out.shape[0]
            out[planes - 2] = act
            out[planes - 1] = grad

    shapes = [jax.ShapeDtypeStruct(array.shape, array.dtype) for array in filled]
    return call(
        body,
        place,
        (*pieces, *filled),
        after,
        shapes or [jax.ShapeDtypeStruct((2, share, hidden), jnp.bfloat16)],
        [],
        16 * share * hidden,
        {nodes + index: index for index in range(len(filled))},
    )


def join(place_ref, piece_refs, index, joined):
    planes, rows, _ = piece_refs[0].shape
    for mask, ref in enumerate(piece_refs):
        first = pl.multiple_of((place_ref[0] ^ mask) * rows, rows)
        joined[pl.ds(first, rows), :] = ref[planes - 2 + index]


def copied(sources, targets, sems):
    copies = [
        pltpu.make_async_copy(source, target, sems.at[index])
        for index, (source, target) in enumerate(zip(sources, targets))
    ]
    for copy in copies:
        copy.start()
    return copies


def with_info(rows, routes, gates):
    (count, width), chosen = rows.shape, routes[0].shape[0]
    height = -(-6 * chosen // 16) * 16
    small = (*routes, *gates)

    def body(*refs):
        inputs, out, held, sems = refs[:5], refs[5], refs[6:10], refs[10]
        targets = (out.at[pl.ds(0, count)], *held)
        for copy in copied(inputs, targets, sems):
            copy.wait()
        lines = [ref[...].astype(jnp.float32) for ref in held[:2]]
        for ref in held[2:]:
            coarse = ref[...].astype(jnp.bfloat16).astype(jnp.float32)
            lines += [coarse, ref[...] - coarse]
        lines.append(jnp.zeros((height - 6 * chosen, count), jnp.float32))
        out[count:, :] = jnp.zeros((height, width), jnp.bfloat16)
        out[count:, 0:count] = jnp.concatenate(lines).astype(jnp.bfloat16)

    return pl.pallas_call(
        body,
        in_specs=[HBM] * 5,
        out_specs=VMEM,
        out_shape=jax.ShapeDtypeStruct((count + height, width), jnp.bfloat16),
        scratch_shapes=[pltpu.VMEM(value.shape, value.dtype) for value in small]
        + [pltpu.SemaphoreType.DMA((5,))],
        compiler_params=pltpu.CompilerParams(vmem_limit_bytes=WIDE_BYTES),
    )(rows, *small)


def opening_products(place, token_rows, grad_rows, weights, nodes):
    (count, width), hidden = grad_rows.shape, weights[0].shape[1]
    share = count // nodes
    operands = (token_rows, weights[0], weights[1], grad_rows, weights[2])
    cuts = 4

    def body(place_ref, *refs):
        inputs, pieces, held = refs[:5], refs[5 : 5 + nodes], refs[5 + nodes : 10 + nodes]
        sorted_rows, sems = refs[10 + nodes :]

        def pieces_of(ref):
            rows = ref.shape[0] // cuts
            return [ref.at[pl.ds(cut * rows, rows)] for cut in range(cuts)]

        parts = [
            copied(pieces_of(source), pieces_of(target), sems.at[index])
            for index, (source, target) in enumerate(zip(inputs, held))
        ]

        def wait(index):
            for copy in parts[index]:
                copy.wait()

        def give(index, part):
            for mask in range(nodes):
                pieces[mask][index] = part[mask * share : (mask + 1) * share].astype(jnp.bfloat16)

        wait(0)
        by_owner(place_ref, held[0], sorted_rows, nodes)
        for index in (0, 1):
            wait(index + 1)
            give(index, matmul(sorted_rows[...], held[index + 1][...]))
        wait(3)
        by_owner(place_ref, held[3], sorted_rows, nodes)
        wait(4)
        give(2, matmul(sorted_rows[...], held[4][...], CONTRACT_LAST))

    return pl.pallas_call(
        body,
        in_specs=[SMEM] + [HBM] * 5,
        out_specs=[VMEM] * nodes,
        out_shape=[jax.ShapeDtypeStruct((3, share, hidden), jnp.bfloat16)] * nodes,
        scratch_shapes=[pltpu.VMEM(value.shape, value.dtype) for value in operands]
        + [pltpu.VMEM((count, width), jnp.bfloat16), pltpu.SemaphoreType.DMA((5, cuts))],
        cost_estimate=pl.CostEstimate(
            flops=int(CF * 6 * count * width * hidden),
            bytes_accessed=int(CF * 6 * width * hidden),
            transcendentals=0,
        ),
        compiler_params=pltpu.CompilerParams(vmem_limit_bytes=WIDE_BYTES),
    )(place, *operands)


def info_of(ref, count, chosen, which):
    lines = ref[count:, 0:count].astype(jnp.float32)
    routes = lines[which * chosen : (which + 1) * chosen].astype(jnp.int32)
    first = 2 * (which + 1) * chosen
    return routes, lines[first : first + chosen] + lines[first + chosen : first + 2 * chosen]


def weight_column(expert, routes, gates):
    chosen, count = routes.shape
    line = jnp.zeros((1, count), jnp.float32)
    for choice in range(chosen):
        line += jnp.where(routes[choice : choice + 1] == expert, gates[choice : choice + 1], 0.0)
    diagonal = lax.broadcasted_iota(jnp.int32, (count, count), 0) == lax.broadcasted_iota(
        jnp.int32, (count, count), 1
    )
    return jnp.sum(jnp.where(diagonal, line, 0.0), axis=1, keepdims=True)


def slot_selection(expert, routes, capacity):
    chosen, count = routes.shape
    named = jnp.zeros((1, count), jnp.float32)
    for choice in range(chosen):
        named += (routes[choice : choice + 1] == expert).astype(jnp.float32)
    earlier = lax.broadcasted_iota(jnp.int32, (count, count), 0) < lax.broadcasted_iota(
        jnp.int32, (count, count), 1
    )
    rank = matmul(
        jnp.broadcast_to(named, (16, count)).astype(jnp.bfloat16),
        earlier.astype(jnp.float32).astype(jnp.bfloat16),
    )[0:1]
    slot = jnp.where(named > 0, rank, -1.0)
    slots = lax.broadcasted_iota(jnp.int32, (capacity, count), 0).astype(jnp.float32)
    return (slots == slot).astype(jnp.float32).astype(jnp.bfloat16)


def give(out, weight, result, added_refs):
    total = weight * result.astype(jnp.bfloat16).astype(jnp.float32)
    for ref in added_refs:
        total += ref[0 : out.shape[0], :].astype(jnp.float32)
    out[...] = total.astype(jnp.bfloat16)


def forward_results(place, pieces, w_down, info, chosen, added, after):
    nodes, (_, share, hidden), width = len(pieces), pieces[0].shape, w_down.shape[1]
    count = share * nodes

    def body(place_ref, *refs):
        piece_refs, refs = refs[:nodes], refs[nodes:]
        (down_ref, info_ref), added_refs, (out, joined) = refs[:2], refs[2:-2], refs[-2:]
        join(place_ref, piece_refs, 0, joined)
        weight = weight_column(place_ref[1], *info_of(info_ref, count, chosen, 0))
        give(out, weight, matmul(joined[...], down_ref[...]), added_refs)

    return call(
        body,
        place,
        (*pieces, w_down, info, *added),
        after,
        jax.ShapeDtypeStruct((count, width), jnp.bfloat16),
        [pltpu.VMEM((count, hidden), jnp.bfloat16)],
        2 * count * width * hidden,
    )


def backward_results(place, pieces, w_gate, w_up, saved_gate, saved_up, info, chosen, added, block, after):
    nodes, (_, share, hidden), width = len(pieces), pieces[0].shape, w_gate.shape[0]
    count = share * nodes
    experts = saved_gate.shape[0] // count

    def body(place_ref, *refs):
        piece_refs, refs = refs[:nodes], refs[nodes:]
        gate_ref, up_ref, saved_gate_ref, saved_up_ref, info_ref = refs[:5]
        added_refs, (out, joined) = refs[5:-2], refs[-2:]
        join(place_ref, piece_refs, 1, joined)
        expert = place_ref[1]
        routes, gates = info_of(info_ref, count, chosen, 1)
        weight = weight_column(expert, routes, gates)
        select = slot_selection(expert, routes, count)
        first = pl.multiple_of(block_behind(expert, experts, block) * count, count)
        grad_gate, grad_up = backward_act(
            joined[...].astype(jnp.float32),
            matmul(select, saved_gate_ref[pl.ds(first, count), :], CONTRACT_FIRST),
            matmul(select, saved_up_ref[pl.ds(first, count), :], CONTRACT_FIRST),
        )
        result = matmul(grad_gate, gate_ref[...], CONTRACT_LAST)
        result += matmul(grad_up, up_ref[...], CONTRACT_LAST)
        give(out, weight, result, added_refs)

    return call(
        body,
        place,
        (*pieces, w_gate, w_up, saved_gate, saved_up, info, *added),
        after,
        jax.ShapeDtypeStruct((count, width), jnp.bfloat16),
        [pltpu.VMEM((count, hidden), jnp.bfloat16)],
        4 * count * width * hidden,
    )


def sum_rows(values, after):
    def body(*refs):
        total = sum(ref[...].astype(jnp.float32) for ref in refs[: len(values)])
        refs[-1][...] = total

    return pl.pallas_call(
        body,
        in_specs=[VMEM] * len(values) + [ANY] * len(after),
        out_specs=VMEM,
        out_shape=jax.ShapeDtypeStruct(values[0].shape, jnp.float32),
        cost_estimate=pl.CostEstimate(
            flops=int(SUM_COST), bytes_accessed=int(SUM_COST / 100), transcendentals=0
        ),
        compiler_params=pltpu.CompilerParams(vmem_limit_bytes=VMEM_BYTES),
    )(*values, *after)


def ring_shards(
    inputs_forward,
    routes_forward,
    gates_forward,
    grads_backward,
    routes_backward,
    gates_backward,
    w_gate,
    w_up,
    w_down,
    saved_gate,
    saved_up,
):
    experts, nodes = lax.axis_size("dev"), lax.axis_size("node")
    place = jnp.stack([lax.axis_index("node"), lax.axis_index("dev")]).astype(jnp.int32)
    weights = (w_gate[0, 0], w_up[0, 0], w_down[0, 0])
    stored_gate, stored_up = saved_gate[0, 0], saved_up[0, 0]

    chosen = routes_forward.shape[2]
    tokens = [
        with_info(
            inputs_forward[0],
            (routes_forward[0].T, routes_backward[0].T),
            (gates_forward[0].T, gates_backward[0].T),
        )
    ]
    grads = [grads_backward[0]]
    for _ in range(1, experts):
        tokens.append(along_ring(tokens[-1], 1))
        grads.append(along_ring(grads[-1], 1))

    sent, parts, acts = [None] * experts, [None] * experts, [None] * experts
    done = []

    def exchange(own):
        return [own[0]] + [across(own[mask % len(own)], "node", mask) for mask in range(1, nodes)]

    def first(step, *after):
        if step == 0:
            sent[0] = opening_products(
                place, inputs_forward[0], grads_backward[0], weights, nodes
            )
        else:
            sent[step] = first_products(
                place, tokens[step], grads[step], weights, nodes, 3 if step == 1 else 5, (*done[-1:], *after)
            )
        done.append(sent[step][0])
        if step < 2:
            parts[step] = exchange(sent[step])

    def middle(step, *after):
        joint = 0 < step < experts - 1
        own = activations(place, parts[step], sent[step + 1] if joint else (), (*done[-1:], *after))
        done.append(own[0])
        acts[step] = exchange(own)
        if joint:
            parts[step + 1] = acts[step]

    sums, hops = [[], []], [(), ()]

    def last(step, kind, *after):
        shift = 1 - 2 * kind
        added = (inputs_forward[0], grads_backward[0])[kind : kind + 1] if step == 0 else ()
        if step >= 2:
            added = hops[kind]
        if kind == 0:
            value = forward_results(
                place, acts[step], weights[2], tokens[step], chosen, added, (*done[-1:], *after)
            )
        else:
            value = backward_results(
                place, acts[step], *weights[:2], stored_gate, stored_up, tokens[step], chosen, added, step, (*done[-1:], *after)
            )
        done.append(value)
        if step == 0:
            sums[kind].append(from_behind(value, "section", shift))
        elif step == 1:
            sums[kind].append(along_ring_and_sections(value, -1, shift))
        elif step < experts - 1:
            hops[kind] = (along_ring(value, 1),)
        else:
            sums[kind].append(along_ring_and_sections(value, 1, shift))

    first(0)
    first(1)
    for step in range(1, experts - 1):
        first(step + 1, *(parts[0][1:] if step == 1 else ()))
        middle(step)
        if step >= 2:
            last(step - 1, 0)
            last(step - 1, 1)
    middle(experts - 1)
    if experts > 2:
        last(experts - 2, 0)
        last(experts - 2, 1, *[values[0] for values in sums if values])
    middle(0, *acts[experts - 1][1:])
    for step in (experts - 1, 0):
        last(step, 0)
        last(step, 1)
    totals = []
    for values in sums:
        totals.append(sum_rows(values[:-1], done[-1:]))
        done.append(totals[-1])
    return tuple(
        (total.astype(jnp.float32) + values[-1].astype(jnp.float32)).astype(jnp.bfloat16)[None]
        for total, values in zip(totals, sums)
    )


def power_of_two(number):
    return number & (number - 1) == 0


def shards(*args):
    experts, nodes = lax.axis_size("dev"), lax.axis_size("node")
    tokens, capacity = args[0].shape[1], args[9].shape[2] // experts
    if capacity == tokens and experts > 1 and power_of_two(nodes) and tokens % (16 * nodes) == 0:
        return ring_shards(*args)
    return shards_by_slots(*args)


def solution(mesh):
    return jax.shard_map(
        shards,
        mesh=mesh,
        in_specs=(
            P("section", "dev", "node"),
            P("section", "dev", None),
            P("section", "dev", None),
            P("section", "dev", "node"),
            P("section", "dev", None),
            P("section", "dev", None),
            P("section", "dev", "node", None),
            P("section", "dev", "node", None),
            P("section", "dev", None, "node"),
            P("section", "dev", None, None),
            P("section", "dev", None, None),
        ),
        out_specs=(P("section", "dev", "node"), P("section", "dev", "node")),
        check_vma=False,
    )
```

```python
import functools

import jax
import jax.numpy as jnp
from jax import lax
from jax.experimental import pallas as pl
from jax.experimental.pallas import tpu as pltpu
from jax.sharding import PartitionSpec as P


def from_behind(value, axis, steps):
    count = lax.axis_size(axis)
    pairs = [(source, (source + steps) % count) for source in range(count)]
    return lax.ppermute(value, axis, pairs)


def slot_targets(routing, experts, capacity):
    flat = routing.reshape(-1)
    onehot = (flat[:, None] == jnp.arange(experts, dtype=jnp.int32)[None, :]).astype(jnp.int32)
    earlier = jnp.cumsum(onehot, axis=0) - onehot
    return flat * capacity + jnp.sum(earlier * onehot, axis=1)


def pack_rows(token_rows, targets, slot_count, chosen):
    match = (jnp.arange(slot_count, dtype=jnp.int32)[:, None] == targets[None, :]).astype(
        jnp.bfloat16
    )
    select = jnp.sum(match.reshape(slot_count, token_rows.shape[0], chosen), axis=2)
    return jnp.dot(select, token_rows, preferred_element_type=jnp.float32).astype(jnp.bfloat16)


def combine_rows(token_rows, weights_of, returned_rows, targets):
    width = token_rows.shape[1]
    picked = returned_rows.reshape(-1, width)[targets]
    picked = picked.reshape(token_rows.shape[0], weights_of.shape[1], width).astype(jnp.float32)
    mixed = token_rows.astype(jnp.float32) + jnp.sum(weights_of[:, :, None] * picked, axis=1)
    return mixed.astype(jnp.bfloat16)


def backward_act(grad_hidden, stored_gate, stored_up):
    act_gate = stored_gate.astype(jnp.float32)
    act_up = stored_up.astype(jnp.float32)
    squash = jax.nn.sigmoid(act_gate)
    grad_gate = (grad_hidden * act_up * squash * (1.0 + act_gate * (1.0 - squash))).astype(
        jnp.bfloat16
    )
    grad_up = (grad_hidden * act_gate * squash).astype(jnp.bfloat16)
    return (grad_gate, grad_up)


def shards_by_slots(
    inputs_forward,
    routes_forward,
    gates_forward,
    grads_backward,
    routes_backward,
    gates_backward,
    w_gate,
    w_up,
    w_down,
    saved_gate,
    saved_up,
):
    experts = lax.axis_size("dev")
    chosen = routes_forward.shape[2]
    token_rows = inputs_forward[0]
    grad_rows = grads_backward[0]
    slot_total = saved_gate.shape[2]
    capacity = slot_total // experts
    width = token_rows.shape[1]
    targets_forward = slot_targets(routes_forward[0], experts, capacity)
    targets_backward = slot_targets(routes_backward[0], experts, capacity)
    sent_forward = pack_rows(token_rows, targets_forward, slot_total, chosen).reshape(
        experts, capacity, width
    )
    sent_backward = pack_rows(grad_rows, targets_backward, slot_total, chosen).reshape(
        experts, capacity, width
    )
    arrived_forward, arrived_backward = (
        lax.all_to_all(sent_forward, "dev", split_axis=0, concat_axis=0, tiled=True),
        lax.all_to_all(sent_backward, "dev", split_axis=0, concat_axis=0, tiled=True),
    )
    arrived_forward = arrived_forward.reshape(slot_total, width)
    arrived_backward = arrived_backward.reshape(slot_total, width)
    gate_local = w_gate[0, 0]
    up_local = w_up[0, 0]
    down_local = w_down[0, 0]
    stored_gate = saved_gate[0, 0]
    stored_up = saved_up[0, 0]
    contract_last = (((1,), (1,)), ((), ()))
    part_gate = jnp.dot(arrived_forward, gate_local, preferred_element_type=jnp.float32)
    part_up = jnp.dot(arrived_forward, up_local, preferred_element_type=jnp.float32)
    part_grad = lax.dot_general(
        arrived_backward, down_local, contract_last, preferred_element_type=jnp.float32
    )
    gate_share, up_share = (
        lax.psum_scatter(
            part_gate.astype(jnp.bfloat16), "node", scatter_dimension=1, tiled=True
        ).astype(jnp.float32),
        lax.psum_scatter(
            part_up.astype(jnp.bfloat16), "node", scatter_dimension=1, tiled=True
        ).astype(jnp.float32),
    )
    hidden_share = (jax.nn.silu(gate_share) * up_share).astype(jnp.bfloat16)
    hidden = lax.all_gather(hidden_share, "node", axis=1, tiled=True)
    grad_hidden = lax.psum(part_grad.astype(jnp.bfloat16), "node").astype(jnp.float32)
    grad_gate, grad_up = backward_act(grad_hidden, stored_gate, stored_up)
    result_forward = jnp.dot(hidden, down_local, preferred_element_type=jnp.float32).astype(
        jnp.bfloat16
    )
    result_backward = lax.dot_general(
        grad_gate, gate_local, contract_last, preferred_element_type=jnp.float32
    )
    result_backward = result_backward + lax.dot_general(
        grad_up, up_local, contract_last, preferred_element_type=jnp.float32
    )
    result_backward = result_backward.astype(jnp.bfloat16)
    back_forward, back_backward = (
        lax.all_to_all(
            result_forward.reshape(experts, capacity, width),
            "dev",
            split_axis=0,
            concat_axis=0,
            tiled=True,
        ),
        lax.all_to_all(
            result_backward.reshape(experts, capacity, width),
            "dev",
            split_axis=0,
            concat_axis=0,
            tiled=True,
        ),
    )
    mixed_forward = combine_rows(token_rows, gates_forward[0], back_forward, targets_forward)
    mixed_backward = combine_rows(grad_rows, gates_backward[0], back_backward, targets_backward)
    next_forward = from_behind(mixed_forward[None], "section", 1)
    next_backward = from_behind(mixed_backward[None], "section", -1)
    return (next_forward, next_backward)


CONTRACT_LAST = (((1,), (1,)), ((), ()))
CONTRACT_FIRST = (((0,), (0,)), ((), ()))
VMEM = pl.BlockSpec(memory_space=pltpu.VMEM)
SMEM = pl.BlockSpec(memory_space=pltpu.SMEM)
VMEM_BYTES = 14 << 20
CF = 1.0
SUM_COST = 1e10
SPACE_COST = 10**10
INFO_COST = 10**6
WIDE_BYTES = 56 << 20
ANY = pl.BlockSpec(memory_space=pl.ANY)
HBM = pl.BlockSpec(memory_space=pltpu.HBM)


def across(value, axis, mask):
    count = lax.axis_size(axis)
    return lax.ppermute(value, axis, [(source, source ^ mask) for source in range(count)])


def ring_order(count):
    return [0] + list(range(1, count, 2)) + list(range(2, count, 2))[::-1]


def ring_pairs(count, steps):
    order = ring_order(count)
    return [(order[i], order[(i + steps) % count]) for i in range(count)]


def along_ring(value, steps):
    return lax.ppermute(value, "dev", ring_pairs(lax.axis_size("dev"), steps))


def along_ring_and_sections(value, steps, shift):
    count, sections = lax.axis_size("dev"), lax.axis_size("section")
    pairs = [
        (section * count + source, (section + shift) % sections * count + target)
        for section in range(sections)
        for source, target in ring_pairs(count, steps)
    ]
    return lax.ppermute(value, ("section", "dev"), pairs)


def block_behind(expert, count, steps):
    block = 0
    for target, source in ring_pairs(count, -steps):
        block = block + jnp.where(expert == target, source, 0)
    return block


def call(body, place, operands, after, out_shape, scratch, flops, aliases={}):
    def with_after(place_ref, *refs):
        body(place_ref, *refs[: len(operands)], *refs[len(operands) + len(after) :])

    touched = sum(array.size * array.dtype.itemsize for array in operands)
    return pl.pallas_call(
        with_after,
        in_specs=[SMEM] + [VMEM] * len(operands) + [ANY] * len(after),
        out_specs=jax.tree.map(lambda _: VMEM, out_shape),
        scratch_shapes=scratch,
        out_shape=out_shape,
        input_output_aliases={index + 1: out for index, out in aliases.items()},
        cost_estimate=pl.CostEstimate(flops=int(CF * flops), bytes_accessed=int(CF * touched), transcendentals=0),
        compiler_params=pltpu.CompilerParams(vmem_limit_bytes=VMEM_BYTES),
    )(place, *operands, *after)


def matmul(left, right, dims=(((1,), (0,)), ((), ()))):
    return lax.dot_general(left, right, dims, preferred_element_type=jnp.float32)


def by_owner(place_ref, rows_ref, sorted_rows, nodes):
    rows = sorted_rows.shape[0] // nodes
    for mask in range(nodes):
        first = pl.multiple_of((place_ref[0] ^ mask) * rows, rows)
        sorted_rows[mask * rows : (mask + 1) * rows, :] = rows_ref[pl.ds(first, rows), :]


def first_products(place, token_rows, grad_rows, weights, nodes, planes, after):
    (count, width), hidden = grad_rows.shape, weights[0].shape[1]
    share = count // nodes

    def body(place_ref, token_ref, grad_ref, gate_ref, up_ref, down_ref, *refs):
        outs, (sorted_tokens, sorted_grads) = refs[:nodes], refs[nodes:]
        by_owner(place_ref, token_ref, sorted_tokens, nodes)
        by_owner(place_ref, grad_ref, sorted_grads, nodes)
        parts = (
            matmul(sorted_tokens[...], gate_ref[...]),
            matmul(sorted_tokens[...], up_ref[...]),
            matmul(sorted_grads[...], down_ref[...], CONTRACT_LAST),
        )
        for index, part in enumerate(parts):
            for mask in range(nodes):
                outs[mask][index] = part[mask * share : (mask + 1) * share].astype(jnp.bfloat16)

    return call(
        body,
        place,
        (token_rows, grad_rows, *weights),
        after,
        [jax.ShapeDtypeStruct((planes, share, hidden), jnp.bfloat16)] * nodes,
        [pltpu.VMEM((count, width), jnp.bfloat16)] * 2,
        6 * count * width * hidden,
    )


def activations(place, pieces, filled, after):
    nodes, (_, share, hidden) = len(pieces), pieces[0].shape

    def body(place_ref, *refs):
        piece_refs, outs = refs[:nodes], refs[nodes + len(filled) :]
        gate, up, grad = (
            sum(ref[index].astype(jnp.float32) for ref in piece_refs) for index in range(3)
        )
        act = (gate / (1.0 + jnp.exp(-gate)) * up).astype(jnp.bfloat16)
        grad = grad.astype(jnp.bfloat16)
        for out in outs:
            planes = out.shape[0]
            out[planes - 2] = act
            out[planes - 1] = grad

    shapes = [jax.ShapeDtypeStruct(array.shape, array.dtype) for array in filled]
    return call(
        body,
        place,
        (*pieces, *filled),
        after,
        shapes or [jax.ShapeDtypeStruct((2, share, hidden), jnp.bfloat16)],
        [],
        16 * share * hidden,
        {nodes + index: index for index in range(len(filled))},
    )


def join(place_ref, piece_refs, index, joined):
    planes, rows, _ = piece_refs[0].shape
    for mask, ref in enumerate(piece_refs):
        first = pl.multiple_of((place_ref[0] ^ mask) * rows, rows)
        joined[pl.ds(first, rows), :] = ref[planes - 2 + index]


def copied(sources, targets, sems):
    copies = [
        pltpu.make_async_copy(source, target, sems.at[index])
        for index, (source, target) in enumerate(zip(sources, targets))
    ]
    for copy in copies:
        copy.start()
    return copies


def with_info(rows, routes, gates, after):
    (count, width), chosen = rows.shape, routes[0].shape[0]
    height = -(-6 * chosen // 16) * 16
    small = (*routes, *gates)

    def body(rows_ref, *refs):
        infos, out = refs[:4], refs[-1]
        lines = [ref[...].astype(jnp.float32) for ref in infos[:2]]
        for ref in infos[2:]:
            coarse = ref[...].astype(jnp.bfloat16).astype(jnp.float32)
            lines += [coarse, ref[...] - coarse]
        lines.append(jnp.zeros((height - 6 * chosen, count), jnp.float32))
        out[0:count, :] = rows_ref[...]
        out[count:, :] = jnp.zeros((height, width), jnp.bfloat16)
        out[count:, 0:count] = jnp.concatenate(lines).astype(jnp.bfloat16)

    return pl.pallas_call(
        body,
        in_specs=[VMEM] * 5 + [ANY] * len(after),
        out_specs=VMEM,
        out_shape=jax.ShapeDtypeStruct((count + height, width), jnp.bfloat16),
        cost_estimate=pl.CostEstimate(flops=INFO_COST, bytes_accessed=INFO_COST // 100, transcendentals=0),
        compiler_params=pltpu.CompilerParams(vmem_limit_bytes=4 << 20),
    )(rows, *small, *after)


def marker():
    def body(out):
        out[...] = jnp.zeros_like(out)

    return pl.pallas_call(
        body,
        out_specs=VMEM,
        out_shape=jax.ShapeDtypeStruct((8, 128), jnp.float32),
        cost_estimate=pl.CostEstimate(flops=SPACE_COST, bytes_accessed=SPACE_COST // 100, transcendentals=0),
        compiler_params=pltpu.CompilerParams(vmem_limit_bytes=1 << 20),
    )()


def opening_products(place, token_rows, grad_rows, weights, nodes):
    (count, width), hidden = grad_rows.shape, weights[0].shape[1]
    share = count // nodes
    operands = (token_rows, weights[0], weights[1], grad_rows, weights[2])
    cuts = 4

    def body(place_ref, *refs):
        inputs, pieces, held = refs[:5], refs[5 : 5 + nodes], refs[5 + nodes : 10 + nodes]
        sorted_rows, sems = refs[10 + nodes :]

        def pieces_of(ref):
            rows = ref.shape[0] // cuts
            return [ref.at[pl.ds(cut * rows, rows)] for cut in range(cuts)]

        parts = [
            copied(pieces_of(source), pieces_of(target), sems.at[index])
            for index, (source, target) in enumerate(zip(inputs, held))
        ]

        def wait(index):
            for copy in parts[index]:
                copy.wait()

        def give(index, part):
            for mask in range(nodes):
                pieces[mask][index] = part[mask * share : (mask + 1) * share].astype(jnp.bfloat16)

        wait(0)
        by_owner(place_ref, held[0], sorted_rows, nodes)
        for index in (0, 1):
            wait(index + 1)
            give(index, matmul(sorted_rows[...], held[index + 1][...]))
        wait(3)
        by_owner(place_ref, held[3], sorted_rows, nodes)
        wait(4)
        give(2, matmul(sorted_rows[...], held[4][...], CONTRACT_LAST))

    return pl.pallas_call(
        body,
        in_specs=[SMEM] + [HBM] * 5,
        out_specs=[VMEM] * nodes,
        out_shape=[jax.ShapeDtypeStruct((3, share, hidden), jnp.bfloat16)] * nodes,
        scratch_shapes=[pltpu.VMEM(value.shape, value.dtype) for value in operands]
        + [pltpu.VMEM((count, width), jnp.bfloat16), pltpu.SemaphoreType.DMA((5, cuts))],
        cost_estimate=pl.CostEstimate(
            flops=int(CF * 6 * count * width * hidden),
            bytes_accessed=int(CF * 6 * width * hidden),
            transcendentals=0,
        ),
        compiler_params=pltpu.CompilerParams(vmem_limit_bytes=WIDE_BYTES),
    )(place, *operands)


def info_of(ref, count, chosen, which):
    lines = ref[count:, 0:count].astype(jnp.float32)
    routes = lines[which * chosen : (which + 1) * chosen].astype(jnp.int32)
    first = 2 * (which + 1) * chosen
    return routes, lines[first : first + chosen] + lines[first + chosen : first + 2 * chosen]


def weight_column(expert, routes, gates):
    chosen, count = routes.shape
    line = jnp.zeros((1, count), jnp.float32)
    for choice in range(chosen):
        line += jnp.where(routes[choice : choice + 1] == expert, gates[choice : choice + 1], 0.0)
    diagonal = lax.broadcasted_iota(jnp.int32, (count, count), 0) == lax.broadcasted_iota(
        jnp.int32, (count, count), 1
    )
    return jnp.sum(jnp.where(diagonal, line, 0.0), axis=1, keepdims=True)


def slot_selection(expert, routes, capacity):
    chosen, count = routes.shape
    named = jnp.zeros((1, count), jnp.float32)
    for choice in range(chosen):
        named += (routes[choice : choice + 1] == expert).astype(jnp.float32)
    earlier = lax.broadcasted_iota(jnp.int32, (count, count), 0) < lax.broadcasted_iota(
        jnp.int32, (count, count), 1
    )
    rank = matmul(
        jnp.broadcast_to(named, (16, count)).astype(jnp.bfloat16),
        earlier.astype(jnp.float32).astype(jnp.bfloat16),
    )[0:1]
    slot = jnp.where(named > 0, rank, -1.0)
    slots = lax.broadcasted_iota(jnp.int32, (capacity, count), 0).astype(jnp.float32)
    return (slots == slot).astype(jnp.float32).astype(jnp.bfloat16)


def give(out, weight, result, added_refs):
    total = weight * result.astype(jnp.bfloat16).astype(jnp.float32)
    for ref in added_refs:
        total += ref[0 : out.shape[0], :].astype(jnp.float32)
    out[...] = total.astype(jnp.bfloat16)


def forward_results(place, pieces, w_down, info, chosen, added, after):
    nodes, (_, share, hidden), width = len(pieces), pieces[0].shape, w_down.shape[1]
    count = share * nodes

    def body(place_ref, *refs):
        piece_refs, refs = refs[:nodes], refs[nodes:]
        (down_ref, info_ref), added_refs, (out, joined) = refs[:2], refs[2:-2], refs[-2:]
        join(place_ref, piece_refs, 0, joined)
        weight = weight_column(place_ref[1], *info_of(info_ref, count, chosen, 0))
        give(out, weight, matmul(joined[...], down_ref[...]), added_refs)

    return call(
        body,
        place,
        (*pieces, w_down, info, *added),
        after,
        jax.ShapeDtypeStruct((count, width), jnp.bfloat16),
        [pltpu.VMEM((count, hidden), jnp.bfloat16)],
        2 * count * width * hidden,
    )


def backward_factors(place, saved_gate, saved_up, info, chosen, count, block, after):
    slots, hidden = saved_gate.shape
    experts = slots // count

    def body(place_ref, saved_gate_ref, saved_up_ref, info_ref, gate_out, up_out):
        routes, _ = info_of(info_ref, count, chosen, 1)
        select = slot_selection(place_ref[1], routes, count)
        first = pl.multiple_of(block_behind(place_ref[1], experts, block) * count, count)
        act_gate = matmul(select, saved_gate_ref[pl.ds(first, count), :], CONTRACT_FIRST)
        act_up = matmul(select, saved_up_ref[pl.ds(first, count), :], CONTRACT_FIRST)
        squash = 1.0 / (1.0 + jnp.exp(-act_gate))
        gate_out[...] = act_up * squash * (1.0 + act_gate * (1.0 - squash))
        up_out[...] = act_gate * squash

    return call(
        body,
        place,
        (saved_gate, saved_up, info),
        after,
        [jax.ShapeDtypeStruct((count, hidden), jnp.float32)] * 2,
        [],
        4 * count * count * hidden,
    )


def backward_results(place, pieces, w_gate, w_up, factors, info, chosen, added, after):
    nodes, (_, share, hidden), width = len(pieces), pieces[0].shape, w_gate.shape[0]
    count = share * nodes

    def body(place_ref, *refs):
        piece_refs, refs = refs[:nodes], refs[nodes:]
        gate_ref, up_ref, gate_factor, up_factor, info_ref = refs[:5]
        added_refs, (out, joined) = refs[5:-2], refs[-2:]
        join(place_ref, piece_refs, 1, joined)
        weight = weight_column(place_ref[1], *info_of(info_ref, count, chosen, 1))
        grad_hidden = joined[...].astype(jnp.float32)
        grad_gate = (grad_hidden * gate_factor[...]).astype(jnp.bfloat16)
        grad_up = (grad_hidden * up_factor[...]).astype(jnp.bfloat16)
        result = matmul(grad_gate, gate_ref[...], CONTRACT_LAST)
        result += matmul(grad_up, up_ref[...], CONTRACT_LAST)
        give(out, weight, result, added_refs)

    return call(
        body,
        place,
        (*pieces, w_gate, w_up, *factors, info, *added),
        after,
        jax.ShapeDtypeStruct((count, width), jnp.bfloat16),
        [pltpu.VMEM((count, hidden), jnp.bfloat16)],
        4 * count * width * hidden,
    )


def sum_rows(values, after):
    def body(*refs):
        total = sum(ref[...].astype(jnp.float32) for ref in refs[: len(values)])
        refs[-1][...] = total

    return pl.pallas_call(
        body,
        in_specs=[VMEM] * len(values) + [ANY] * len(after),
        out_specs=VMEM,
        out_shape=jax.ShapeDtypeStruct(values[0].shape, jnp.float32),
        cost_estimate=pl.CostEstimate(
            flops=int(SUM_COST), bytes_accessed=int(SUM_COST / 100), transcendentals=0
        ),
        compiler_params=pltpu.CompilerParams(vmem_limit_bytes=VMEM_BYTES),
    )(*values, *after)


def ring_shards(
    inputs_forward,
    routes_forward,
    gates_forward,
    grads_backward,
    routes_backward,
    gates_backward,
    w_gate,
    w_up,
    w_down,
    saved_gate,
    saved_up,
):
    experts, nodes = lax.axis_size("dev"), lax.axis_size("node")
    place = jnp.stack([lax.axis_index("node"), lax.axis_index("dev")]).astype(jnp.int32)
    weights = (w_gate[0, 0], w_up[0, 0], w_down[0, 0])
    stored_gate, stored_up = saved_gate[0, 0], saved_up[0, 0]

    chosen = routes_forward.shape[2]
    tokens = [
        with_info(
            inputs_forward[0],
            (routes_forward[0].T, routes_backward[0].T),
            (gates_forward[0].T, gates_backward[0].T),
            (marker(),),
        )
    ]
    grads = [grads_backward[0]]
    for _ in range(1, experts):
        tokens.append(along_ring(tokens[-1], 1))
        grads.append(along_ring(grads[-1], 1))

    count = grads_backward.shape[1]
    sent, parts, acts = [None] * experts, [None] * experts, [None] * experts
    done = []

    def exchange(own):
        return [own[0]] + [across(own[mask % len(own)], "node", mask) for mask in range(1, nodes)]

    factors = [None] * experts

    def prepare(step):
        factors[step] = backward_factors(
            place, stored_gate, stored_up, tokens[step], chosen, count, step, done[-1:]
        )
        done.append(factors[step][0])

    def first(step, *after):
        sent[step] = first_products(
            place, tokens[step], grads[step], weights, nodes, 5 if step > 1 else 3, (*done[-1:], *after)
        )
        done.append(sent[step][0])
        if step < 2:
            parts[step] = exchange(sent[step])

    def middle(step, *after):
        joint = 0 < step < experts - 1
        own = activations(place, parts[step], sent[step + 1] if joint else (), (*done[-1:], *after))
        done.append(own[0])
        acts[step] = exchange(own)
        if joint:
            parts[step + 1] = acts[step]

    sums, hops = [[], []], [(), ()]

    def last(step, kind, *after):
        shift = 1 - 2 * kind
        added = (inputs_forward[0], grads_backward[0])[kind : kind + 1] if step == 0 else ()
        if step >= 2:
            added = hops[kind]
        if kind == 0:
            value = forward_results(
                place, acts[step], weights[2], tokens[step], chosen, added, (*done[-1:], *after)
            )
        else:
            value = backward_results(
                place, acts[step], *weights[:2], factors[step], tokens[step], chosen, added, (*done[-1:], *after)
            )
        done.append(value)
        if step == 0:
            sums[kind].append(from_behind(value, "section", shift))
        elif step == 1:
            sums[kind].append(along_ring_and_sections(value, -1, shift))
        elif step < experts - 1:
            hops[kind] = (along_ring(value, 1),)
        else:
            sums[kind].append(along_ring_and_sections(value, 1, shift))

    first(0)
    first(1)
    for step in range(1, experts - 1):
        first(step + 1, *(parts[0][1:] if step == 1 else ()))
        prepare(step)
        middle(step)
        if step >= 2:
            last(step - 1, 0)
            last(step - 1, 1)
    prepare(experts - 1)
    prepare(0)
    middle(experts - 1)
    if experts > 2:
        last(experts - 2, 0)
        last(experts - 2, 1, *[values[0] for values in sums if values])
    middle(0, *acts[experts - 1][1:])
    for step in (experts - 1, 0):
        last(step, 0)
        last(step, 1)
    outs = []
    for values in sums:
        total = sum_rows(values[:-1], (*done[-1:], *outs)) + values[-1].astype(jnp.float32)
        outs.append(total.astype(jnp.bfloat16))
    return tuple(out[None] for out in outs)


def power_of_two(number):
    return number & (number - 1) == 0


def shards(*args):
    experts, nodes = lax.axis_size("dev"), lax.axis_size("node")
    tokens, capacity = args[0].shape[1], args[9].shape[2] // experts
    if capacity == tokens and experts > 1 and power_of_two(nodes) and tokens % (16 * nodes) == 0:
        return ring_shards(*args)
    return shards_by_slots(*args)


def solution(mesh):
    return jax.shard_map(
        shards,
        mesh=mesh,
        in_specs=(
            P("section", "dev", "node"),
            P("section", "dev", None),
            P("section", "dev", None),
            P("section", "dev", "node"),
            P("section", "dev", None),
            P("section", "dev", None),
            P("section", "dev", "node", None),
            P("section", "dev", "node", None),
            P("section", "dev", None, "node"),
            P("section", "dev", None, None),
            P("section", "dev", None, None),
        ),
        out_specs=(P("section", "dev", "node"), P("section", "dev", "node")),
        check_vma=False,
    )
```

```python
import functools

import jax
import jax.numpy as jnp
from jax import lax
from jax.experimental import pallas as pl
from jax.experimental.pallas import tpu as pltpu
from jax.sharding import PartitionSpec as P


def from_behind(value, axis, steps):
    count = lax.axis_size(axis)
    pairs = [(source, (source + steps) % count) for source in range(count)]
    return lax.ppermute(value, axis, pairs)


def slot_targets(routing, experts, capacity):
    flat = routing.reshape(-1)
    onehot = (flat[:, None] == jnp.arange(experts, dtype=jnp.int32)[None, :]).astype(jnp.int32)
    earlier = jnp.cumsum(onehot, axis=0) - onehot
    return flat * capacity + jnp.sum(earlier * onehot, axis=1)


def pack_rows(token_rows, targets, slot_count, chosen):
    match = (jnp.arange(slot_count, dtype=jnp.int32)[:, None] == targets[None, :]).astype(
        jnp.bfloat16
    )
    select = jnp.sum(match.reshape(slot_count, token_rows.shape[0], chosen), axis=2)
    return jnp.dot(select, token_rows, preferred_element_type=jnp.float32).astype(jnp.bfloat16)


def combine_rows(token_rows, weights_of, returned_rows, targets):
    width = token_rows.shape[1]
    picked = returned_rows.reshape(-1, width)[targets]
    picked = picked.reshape(token_rows.shape[0], weights_of.shape[1], width).astype(jnp.float32)
    mixed = token_rows.astype(jnp.float32) + jnp.sum(weights_of[:, :, None] * picked, axis=1)
    return mixed.astype(jnp.bfloat16)


def backward_act(grad_hidden, stored_gate, stored_up):
    act_gate = stored_gate.astype(jnp.float32)
    act_up = stored_up.astype(jnp.float32)
    squash = jax.nn.sigmoid(act_gate)
    grad_gate = (grad_hidden * act_up * squash * (1.0 + act_gate * (1.0 - squash))).astype(
        jnp.bfloat16
    )
    grad_up = (grad_hidden * act_gate * squash).astype(jnp.bfloat16)
    return (grad_gate, grad_up)


def shards_by_slots(
    inputs_forward,
    routes_forward,
    gates_forward,
    grads_backward,
    routes_backward,
    gates_backward,
    w_gate,
    w_up,
    w_down,
    saved_gate,
    saved_up,
):
    experts = lax.axis_size("dev")
    chosen = routes_forward.shape[2]
    token_rows = inputs_forward[0]
    grad_rows = grads_backward[0]
    slot_total = saved_gate.shape[2]
    capacity = slot_total // experts
    width = token_rows.shape[1]
    targets_forward = slot_targets(routes_forward[0], experts, capacity)
    targets_backward = slot_targets(routes_backward[0], experts, capacity)
    sent_forward = pack_rows(token_rows, targets_forward, slot_total, chosen).reshape(
        experts, capacity, width
    )
    sent_backward = pack_rows(grad_rows, targets_backward, slot_total, chosen).reshape(
        experts, capacity, width
    )
    arrived_forward, arrived_backward = (
        lax.all_to_all(sent_forward, "dev", split_axis=0, concat_axis=0, tiled=True),
        lax.all_to_all(sent_backward, "dev", split_axis=0, concat_axis=0, tiled=True),
    )
    arrived_forward = arrived_forward.reshape(slot_total, width)
    arrived_backward = arrived_backward.reshape(slot_total, width)
    gate_local = w_gate[0, 0]
    up_local = w_up[0, 0]
    down_local = w_down[0, 0]
    stored_gate = saved_gate[0, 0]
    stored_up = saved_up[0, 0]
    contract_last = (((1,), (1,)), ((), ()))
    part_gate = jnp.dot(arrived_forward, gate_local, preferred_element_type=jnp.float32)
    part_up = jnp.dot(arrived_forward, up_local, preferred_element_type=jnp.float32)
    part_grad = lax.dot_general(
        arrived_backward, down_local, contract_last, preferred_element_type=jnp.float32
    )
    gate_share, up_share = (
        lax.psum_scatter(
            part_gate.astype(jnp.bfloat16), "node", scatter_dimension=1, tiled=True
        ).astype(jnp.float32),
        lax.psum_scatter(
            part_up.astype(jnp.bfloat16), "node", scatter_dimension=1, tiled=True
        ).astype(jnp.float32),
    )
    hidden_share = (jax.nn.silu(gate_share) * up_share).astype(jnp.bfloat16)
    hidden = lax.all_gather(hidden_share, "node", axis=1, tiled=True)
    grad_hidden = lax.psum(part_grad.astype(jnp.bfloat16), "node").astype(jnp.float32)
    grad_gate, grad_up = backward_act(grad_hidden, stored_gate, stored_up)
    result_forward = jnp.dot(hidden, down_local, preferred_element_type=jnp.float32).astype(
        jnp.bfloat16
    )
    result_backward = lax.dot_general(
        grad_gate, gate_local, contract_last, preferred_element_type=jnp.float32
    )
    result_backward = result_backward + lax.dot_general(
        grad_up, up_local, contract_last, preferred_element_type=jnp.float32
    )
    result_backward = result_backward.astype(jnp.bfloat16)
    back_forward, back_backward = (
        lax.all_to_all(
            result_forward.reshape(experts, capacity, width),
            "dev",
            split_axis=0,
            concat_axis=0,
            tiled=True,
        ),
        lax.all_to_all(
            result_backward.reshape(experts, capacity, width),
            "dev",
            split_axis=0,
            concat_axis=0,
            tiled=True,
        ),
    )
    mixed_forward = combine_rows(token_rows, gates_forward[0], back_forward, targets_forward)
    mixed_backward = combine_rows(grad_rows, gates_backward[0], back_backward, targets_backward)
    next_forward = from_behind(mixed_forward[None], "section", 1)
    next_backward = from_behind(mixed_backward[None], "section", -1)
    return (next_forward, next_backward)


CONTRACT_LAST = (((1,), (1,)), ((), ()))
CONTRACT_FIRST = (((0,), (0,)), ((), ()))
VMEM = pl.BlockSpec(memory_space=pltpu.VMEM)
SMEM = pl.BlockSpec(memory_space=pltpu.SMEM)
VMEM_BYTES = 14 << 20
CF = 1.0
SUM_COST = 1e10
SPACE_COST = 10**10
INFO_COST = 10**6
WIDE_BYTES = 56 << 20
ANY = pl.BlockSpec(memory_space=pl.ANY)
HBM = pl.BlockSpec(memory_space=pltpu.HBM)


def across(value, axis, mask):
    count = lax.axis_size(axis)
    return lax.ppermute(value, axis, [(source, source ^ mask) for source in range(count)])


def ring_order(count):
    return [0] + list(range(1, count, 2)) + list(range(2, count, 2))[::-1]


def ring_pairs(count, steps):
    order = ring_order(count)
    return [(order[i], order[(i + steps) % count]) for i in range(count)]


def along_ring(value, steps):
    return lax.ppermute(value, "dev", ring_pairs(lax.axis_size("dev"), steps))


def along_ring_and_sections(value, steps, shift):
    count, sections = lax.axis_size("dev"), lax.axis_size("section")
    pairs = [
        (section * count + source, (section + shift) % sections * count + target)
        for section in range(sections)
        for source, target in ring_pairs(count, steps)
    ]
    return lax.ppermute(value, ("section", "dev"), pairs)


def block_behind(expert, count, steps):
    block = 0
    for target, source in ring_pairs(count, -steps):
        block = block + jnp.where(expert == target, source, 0)
    return block


def call(body, place, operands, after, out_shape, scratch, flops, aliases={}):
    def with_after(place_ref, *refs):
        body(place_ref, *refs[: len(operands)], *refs[len(operands) + len(after) :])

    touched = sum(array.size * array.dtype.itemsize for array in operands)
    return pl.pallas_call(
        with_after,
        in_specs=[SMEM] + [VMEM] * len(operands) + [ANY] * len(after),
        out_specs=jax.tree.map(lambda _: VMEM, out_shape),
        scratch_shapes=scratch,
        out_shape=out_shape,
        input_output_aliases={index + 1: out for index, out in aliases.items()},
        cost_estimate=pl.CostEstimate(flops=int(CF * flops), bytes_accessed=int(CF * touched), transcendentals=0),
        compiler_params=pltpu.CompilerParams(vmem_limit_bytes=VMEM_BYTES),
    )(place, *operands, *after)


def matmul(left, right, dims=(((1,), (0,)), ((), ()))):
    return lax.dot_general(left, right, dims, preferred_element_type=jnp.float32)


def by_owner(place_ref, rows_ref, sorted_rows, nodes):
    rows = sorted_rows.shape[0] // nodes
    for mask in range(nodes):
        first = pl.multiple_of((place_ref[0] ^ mask) * rows, rows)
        sorted_rows[mask * rows : (mask + 1) * rows, :] = rows_ref[pl.ds(first, rows), :]


def first_products(place, token_rows, grad_rows, weights, nodes, planes, after):
    (count, width), hidden = token_rows.shape, weights[0].shape[1]
    share = count // nodes

    def body(place_ref, token_ref, grad_ref, gate_ref, up_ref, down_ref, *refs):
        outs, (sorted_tokens, sorted_grads) = refs[:nodes], refs[nodes:]
        by_owner(place_ref, token_ref, sorted_tokens, nodes)
        by_owner(place_ref, grad_ref, sorted_grads, nodes)
        parts = (
            matmul(sorted_tokens[...], gate_ref[...]),
            matmul(sorted_tokens[...], up_ref[...]),
            matmul(sorted_grads[...], down_ref[...], CONTRACT_LAST),
        )
        for index, part in enumerate(parts):
            for mask in range(nodes):
                outs[mask][index] = part[mask * share : (mask + 1) * share].astype(jnp.bfloat16)

    return call(
        body,
        place,
        (token_rows, grad_rows, *weights),
        after,
        [jax.ShapeDtypeStruct((planes, share, hidden), jnp.bfloat16)] * nodes,
        [pltpu.VMEM((count, width), jnp.bfloat16)] * 2,
        6 * count * width * hidden,
    )


def activations(place, pieces, filled, after, extra=()):
    nodes, (_, share, hidden) = len(pieces), pieces[0].shape

    def body(place_ref, *refs):
        piece_refs, extra_refs = refs[:nodes], refs[nodes + len(filled) :][: len(extra)]
        outs = refs[nodes + len(filled) + len(extra) :]
        gate, up, grad = (
            sum(ref[index].astype(jnp.float32) for ref in piece_refs) for index in range(3)
        )
        act = (gate / (1.0 + jnp.exp(-gate)) * up).astype(jnp.bfloat16)
        grad = grad.astype(jnp.bfloat16)
        for out in outs:
            start = 3 if filled else 0
            out[start] = act
            out[start + 1] = grad
            for index, ref in enumerate(extra_refs):
                out[start + 2 + index] = ref[1]

    shapes = [jax.ShapeDtypeStruct(array.shape, array.dtype) for array in filled]
    return call(
        body,
        place,
        (*pieces, *filled, *extra),
        after,
        shapes or [jax.ShapeDtypeStruct((2 + len(extra), share, hidden), jnp.bfloat16)],
        [],
        16 * share * hidden,
        {nodes + index: index for index in range(len(filled))},
    )


def first_plane(place, planes, after):
    def body(place_ref, planes_ref, out):
        out[0] = planes_ref[0]

    shape = (1, *planes.shape[1:])
    return call(body, place, (planes,), after, jax.ShapeDtypeStruct(shape, planes.dtype), [], 0)


def join(place_ref, piece_refs, index, joined):
    rows = piece_refs[0].shape[1]
    for mask, ref in enumerate(piece_refs):
        first = pl.multiple_of((place_ref[0] ^ mask) * rows, rows)
        joined[pl.ds(first, rows), :] = ref[index]


def copied(sources, targets, sems):
    copies = [
        pltpu.make_async_copy(source, target, sems.at[index])
        for index, (source, target) in enumerate(zip(sources, targets))
    ]
    for copy in copies:
        copy.start()
    return copies


def with_info(rows, routes, gates, after):
    (count, width), chosen = rows.shape, routes[0].shape[0]
    height = -(-6 * chosen // 16) * 16
    small = (*routes, *gates)

    def body(rows_ref, *refs):
        infos, out = refs[:4], refs[-1]
        lines = [ref[...].astype(jnp.float32) for ref in infos[:2]]
        for ref in infos[2:]:
            coarse = ref[...].astype(jnp.bfloat16).astype(jnp.float32)
            lines += [coarse, ref[...] - coarse]
        lines.append(jnp.zeros((height - 6 * chosen, count), jnp.float32))
        out[0:count, :] = rows_ref[...]
        out[count:, :] = jnp.zeros((height, width), jnp.bfloat16)
        out[count:, 0:count] = jnp.concatenate(lines).astype(jnp.bfloat16)

    return pl.pallas_call(
        body,
        in_specs=[VMEM] * 5 + [ANY] * len(after),
        out_specs=VMEM,
        out_shape=jax.ShapeDtypeStruct((count + height, width), jnp.bfloat16),
        cost_estimate=pl.CostEstimate(flops=INFO_COST, bytes_accessed=INFO_COST // 100, transcendentals=0),
        compiler_params=pltpu.CompilerParams(vmem_limit_bytes=4 << 20),
    )(rows, *small, *after)


def marker():
    def body(out):
        out[...] = jnp.zeros_like(out)

    return pl.pallas_call(
        body,
        out_specs=VMEM,
        out_shape=jax.ShapeDtypeStruct((8, 128), jnp.float32),
        cost_estimate=pl.CostEstimate(flops=SPACE_COST, bytes_accessed=SPACE_COST // 100, transcendentals=0),
        compiler_params=pltpu.CompilerParams(vmem_limit_bytes=1 << 20),
    )()


def opening_products(place, token_rows, grad_rows, weights, nodes):
    (count, width), hidden = grad_rows.shape, weights[0].shape[1]
    share = count // nodes
    operands = (token_rows, weights[0], weights[1], grad_rows, weights[2])
    cuts = 4

    def body(place_ref, *refs):
        inputs, pieces, held = refs[:5], refs[5 : 5 + nodes], refs[5 + nodes : 10 + nodes]
        sorted_rows, sems = refs[10 + nodes :]

        def pieces_of(ref):
            rows = ref.shape[0] // cuts
            return [ref.at[pl.ds(cut * rows, rows)] for cut in range(cuts)]

        parts = [
            copied(pieces_of(source), pieces_of(target), sems.at[index])
            for index, (source, target) in enumerate(zip(inputs, held))
        ]

        def wait(index):
            for copy in parts[index]:
                copy.wait()

        def give(index, part):
            for mask in range(nodes):
                pieces[mask][index] = part[mask * share : (mask + 1) * share].astype(jnp.bfloat16)

        wait(0)
        by_owner(place_ref, held[0], sorted_rows, nodes)
        for index in (0, 1):
            wait(index + 1)
            give(index, matmul(sorted_rows[...], held[index + 1][...]))
        wait(3)
        by_owner(place_ref, held[3], sorted_rows, nodes)
        wait(4)
        give(2, matmul(sorted_rows[...], held[4][...], CONTRACT_LAST))

    return pl.pallas_call(
        body,
        in_specs=[SMEM] + [HBM] * 5,
        out_specs=[VMEM] * nodes,
        out_shape=[jax.ShapeDtypeStruct((3, share, hidden), jnp.bfloat16)] * nodes,
        scratch_shapes=[pltpu.VMEM(value.shape, value.dtype) for value in operands]
        + [pltpu.VMEM((count, width), jnp.bfloat16), pltpu.SemaphoreType.DMA((5, cuts))],
        cost_estimate=pl.CostEstimate(
            flops=int(CF * 6 * count * width * hidden),
            bytes_accessed=int(CF * 6 * width * hidden),
            transcendentals=0,
        ),
        compiler_params=pltpu.CompilerParams(vmem_limit_bytes=WIDE_BYTES),
    )(place, *operands)


def info_of(ref, count, chosen, which):
    lines = ref[count:, 0:count].astype(jnp.float32)
    routes = lines[which * chosen : (which + 1) * chosen].astype(jnp.int32)
    first = 2 * (which + 1) * chosen
    return routes, lines[first : first + chosen] + lines[first + chosen : first + 2 * chosen]


def weight_column(expert, routes, gates):
    chosen, count = routes.shape
    line = jnp.zeros((1, count), jnp.float32)
    for choice in range(chosen):
        line += jnp.where(routes[choice : choice + 1] == expert, gates[choice : choice + 1], 0.0)
    diagonal = lax.broadcasted_iota(jnp.int32, (count, count), 0) == lax.broadcasted_iota(
        jnp.int32, (count, count), 1
    )
    return jnp.sum(jnp.where(diagonal, line, 0.0), axis=1, keepdims=True)


def slot_selection(expert, routes, capacity):
    chosen, count = routes.shape
    named = jnp.zeros((1, count), jnp.float32)
    for choice in range(chosen):
        named += (routes[choice : choice + 1] == expert).astype(jnp.float32)
    earlier = lax.broadcasted_iota(jnp.int32, (count, count), 0) < lax.broadcasted_iota(
        jnp.int32, (count, count), 1
    )
    rank = matmul(
        jnp.broadcast_to(named, (16, count)).astype(jnp.bfloat16),
        earlier.astype(jnp.float32).astype(jnp.bfloat16),
    )[0:1]
    slot = jnp.where(named > 0, rank, -1.0)
    slots = lax.broadcasted_iota(jnp.int32, (capacity, count), 0).astype(jnp.float32)
    return (slots == slot).astype(jnp.float32).astype(jnp.bfloat16)


def give(out, weight, result, added_refs):
    total = weight * result.astype(jnp.bfloat16).astype(jnp.float32)
    for ref in added_refs:
        total += ref[0 : out.shape[0], :].astype(jnp.float32)
    out[...] = total.astype(jnp.bfloat16)


def forward_results(place, pieces, plane, w_down, info, chosen, added, after):
    nodes, (_, share, hidden), width = len(pieces), pieces[0].shape, w_down.shape[1]
    count = share * nodes

    def body(place_ref, *refs):
        piece_refs, refs = refs[:nodes], refs[nodes:]
        (down_ref, info_ref), added_refs, (out, joined) = refs[:2], refs[2:-2], refs[-2:]
        join(place_ref, piece_refs, plane, joined)
        weight = weight_column(place_ref[1], *info_of(info_ref, count, chosen, 0))
        give(out, weight, matmul(joined[...], down_ref[...]), added_refs)

    return call(
        body,
        place,
        (*pieces, w_down, info, *added),
        after,
        jax.ShapeDtypeStruct((count, width), jnp.bfloat16),
        [pltpu.VMEM((count, hidden), jnp.bfloat16)],
        2 * count * width * hidden,
    )


def backward_factors(place, saved_gate, saved_up, info, chosen, count, block, after):
    slots, hidden = saved_gate.shape
    experts = slots // count

    def body(place_ref, saved_gate_ref, saved_up_ref, info_ref, gate_out, up_out):
        routes, _ = info_of(info_ref, count, chosen, 1)
        select = slot_selection(place_ref[1], routes, count)
        first = pl.multiple_of(block_behind(place_ref[1], experts, block) * count, count)
        act_gate = matmul(select, saved_gate_ref[pl.ds(first, count), :], CONTRACT_FIRST)
        act_up = matmul(select, saved_up_ref[pl.ds(first, count), :], CONTRACT_FIRST)
        squash = 1.0 / (1.0 + jnp.exp(-act_gate))
        gate_out[...] = act_up * squash * (1.0 + act_gate * (1.0 - squash))
        up_out[...] = act_gate * squash

    return call(
        body,
        place,
        (saved_gate, saved_up, info),
        after,
        [jax.ShapeDtypeStruct((count, hidden), jnp.float32)] * 2,
        [],
        4 * count * count * hidden,
    )


def backward_results(place, pieces, plane, w_gate, w_up, factors, info, chosen, added, after):
    nodes, (_, share, hidden), width = len(pieces), pieces[0].shape, w_gate.shape[0]
    count = share * nodes

    def body(place_ref, *refs):
        piece_refs, refs = refs[:nodes], refs[nodes:]
        gate_ref, up_ref, gate_factor, up_factor, info_ref = refs[:5]
        added_refs, (out, joined) = refs[5:-2], refs[-2:]
        join(place_ref, piece_refs, plane, joined)
        weight = weight_column(place_ref[1], *info_of(info_ref, count, chosen, 1))
        grad_hidden = joined[...].astype(jnp.float32)
        grad_gate = (grad_hidden * gate_factor[...]).astype(jnp.bfloat16)
        grad_up = (grad_hidden * up_factor[...]).astype(jnp.bfloat16)
        result = matmul(grad_gate, gate_ref[...], CONTRACT_LAST)
        result += matmul(grad_up, up_ref[...], CONTRACT_LAST)
        give(out, weight, result, added_refs)

    return call(
        body,
        place,
        (*pieces, w_gate, w_up, *factors, info, *added),
        after,
        jax.ShapeDtypeStruct((count, width), jnp.bfloat16),
        [pltpu.VMEM((count, hidden), jnp.bfloat16)],
        4 * count * width * hidden,
    )


def sum_rows(values, after):
    def body(*refs):
        total = sum(ref[...].astype(jnp.float32) for ref in refs[: len(values)])
        refs[-1][...] = total

    return pl.pallas_call(
        body,
        in_specs=[VMEM] * len(values) + [ANY] * len(after),
        out_specs=VMEM,
        out_shape=jax.ShapeDtypeStruct(values[0].shape, jnp.float32),
        cost_estimate=pl.CostEstimate(
            flops=int(SUM_COST), bytes_accessed=int(SUM_COST / 100), transcendentals=0
        ),
        compiler_params=pltpu.CompilerParams(vmem_limit_bytes=VMEM_BYTES),
    )(*values, *after)


def ring_shards(
    inputs_forward,
    routes_forward,
    gates_forward,
    grads_backward,
    routes_backward,
    gates_backward,
    w_gate,
    w_up,
    w_down,
    saved_gate,
    saved_up,
):
    experts, nodes = lax.axis_size("dev"), lax.axis_size("node")
    place = jnp.stack([lax.axis_index("node"), lax.axis_index("dev")]).astype(jnp.int32)
    weights = (w_gate[0, 0], w_up[0, 0], w_down[0, 0])
    stored_gate, stored_up = saved_gate[0, 0], saved_up[0, 0]

    chosen = routes_forward.shape[2]
    tokens = [inputs_forward[0]]
    grads = [
        with_info(
            grads_backward[0],
            (routes_forward[0].T, routes_backward[0].T),
            (gates_forward[0].T, gates_backward[0].T),
            (marker(),),
        )
    ]
    for _ in range(1, experts):
        tokens.append(along_ring(tokens[-1], 1))
        grads.append(along_ring(grads[-1], 1))

    count = grads_backward.shape[1]
    sent, parts = [None] * experts, [None] * experts
    acts = [None] * experts, [None] * experts
    done = []

    def exchange(own):
        return [own[0]] + [across(own[mask % len(own)], "node", mask) for mask in range(1, nodes)]

    factors = [None] * experts

    def prepare(step):
        factors[step] = backward_factors(
            place, stored_gate, stored_up, grads[step], chosen, count, step, done[-1:]
        )
        done.append(factors[step][0])

    def first(step, *after):
        sent[step] = first_products(
            place, tokens[step], grads[step], weights, nodes, 5 if step > 1 else 3, (*done[-1:], *after)
        )
        done.append(sent[step][0])
        if step < 2:
            parts[step] = exchange(sent[step])

    def middle(step, *after):
        joint = 0 < step < experts - 1
        filled, extra = (sent[step + 1], ()) if joint else ((), (own_acts,))
        own = activations(place, parts[step], filled, (*done[-1:], *after), extra)
        done.append(own[0])
        arrived = exchange(own)
        plane = 3 if joint else 0
        acts[0][step], acts[1][step] = (arrived, plane), (arrived, plane + 1)
        if joint:
            parts[step + 1] = arrived
        else:
            acts[1][0] = (arrived, plane + 2)

    sums, hops, base = [[], []], [(), ()], [None, None]

    def last(step, kind, *after):
        shift = 1 - 2 * kind
        added = (inputs_forward[0], grads_backward[0])[kind : kind + 1] if step == 0 else ()
        if step >= 2:
            added = hops[kind]
        if kind == 0:
            value = forward_results(
                place, *acts[0][step], weights[2], grads[step], chosen, added, (*done[-1:], *after)
            )
        else:
            value = backward_results(
                place, *acts[1][step], *weights[:2], factors[step], grads[step], chosen, added, (*done[-1:], *after)
            )
        done.append(value)
        if step == 0:
            base[kind] = from_behind(value, "section", shift)
        elif step == 1:
            sums[kind].append(along_ring_and_sections(value, -1, shift))
        elif step < experts - 1:
            hops[kind] = (along_ring(value, 1),)
        else:
            sums[kind].append(along_ring_and_sections(value, 1, shift))

    first(0)
    first(1)
    own_acts = activations(place, parts[0], (), done[-1:])[0]
    done.append(own_acts)
    for step in range(1, experts - 1):
        first(step + 1)
        prepare(step)
        middle(step)
        if step >= 2:
            last(step - 1, 0)
            last(step - 1, 1)
    prepare(experts - 1)
    prepare(0)
    middle(experts - 1)
    if experts > 2:
        last(experts - 2, 0)
        last(experts - 2, 1, *[values[0] for values in sums if values])
    last(experts - 1, 0)
    own_plane = first_plane(place, own_acts, (*done[-1:], *acts[0][experts - 1][0][1:]))
    done.append(own_plane)
    acts[0][0] = (exchange([own_plane]), 0)
    last(experts - 1, 1)
    last(0, 1)
    last(0, 0)
    outs = []
    for values, own in zip(sums, base):
        total = sum_rows(values, (*done[-1:], *outs)) + own.astype(jnp.float32)
        outs.append(total.astype(jnp.bfloat16))
    return tuple(out[None] for out in outs)


def power_of_two(number):
    return number & (number - 1) == 0


def shards(*args):
    experts, nodes = lax.axis_size("dev"), lax.axis_size("node")
    tokens, capacity = args[0].shape[1], args[9].shape[2] // experts
    if capacity == tokens and experts > 1 and power_of_two(nodes) and tokens % (16 * nodes) == 0:
        return ring_shards(*args)
    return shards_by_slots(*args)


def solution(mesh):
    return jax.shard_map(
        shards,
        mesh=mesh,
        in_specs=(
            P("section", "dev", "node"),
            P("section", "dev", None),
            P("section", "dev", None),
            P("section", "dev", "node"),
            P("section", "dev", None),
            P("section", "dev", None),
            P("section", "dev", "node", None),
            P("section", "dev", "node", None),
            P("section", "dev", None, "node"),
            P("section", "dev", None, None),
            P("section", "dev", None, None),
        ),
        out_specs=(P("section", "dev", "node"), P("section", "dev", "node")),
        check_vma=False,
    )
```

```python
import functools

import jax
import jax.numpy as jnp
from jax import lax
from jax.experimental import pallas as pl
from jax.experimental.pallas import tpu as pltpu
from jax.sharding import PartitionSpec as P


def from_behind(value, axis, steps):
    count = lax.axis_size(axis)
    pairs = [(source, (source + steps) % count) for source in range(count)]
    return lax.ppermute(value, axis, pairs)


def slot_targets(routing, experts, capacity):
    flat = routing.reshape(-1)
    onehot = (flat[:, None] == jnp.arange(experts, dtype=jnp.int32)[None, :]).astype(jnp.int32)
    earlier = jnp.cumsum(onehot, axis=0) - onehot
    return flat * capacity + jnp.sum(earlier * onehot, axis=1)


def pack_rows(token_rows, targets, slot_count, chosen):
    match = (jnp.arange(slot_count, dtype=jnp.int32)[:, None] == targets[None, :]).astype(
        jnp.bfloat16
    )
    select = jnp.sum(match.reshape(slot_count, token_rows.shape[0], chosen), axis=2)
    return jnp.dot(select, token_rows, preferred_element_type=jnp.float32).astype(jnp.bfloat16)


def combine_rows(token_rows, weights_of, returned_rows, targets):
    width = token_rows.shape[1]
    picked = returned_rows.reshape(-1, width)[targets]
    picked = picked.reshape(token_rows.shape[0], weights_of.shape[1], width).astype(jnp.float32)
    mixed = token_rows.astype(jnp.float32) + jnp.sum(weights_of[:, :, None] * picked, axis=1)
    return mixed.astype(jnp.bfloat16)


def backward_act(grad_hidden, stored_gate, stored_up):
    act_gate = stored_gate.astype(jnp.float32)
    act_up = stored_up.astype(jnp.float32)
    squash = jax.nn.sigmoid(act_gate)
    grad_gate = (grad_hidden * act_up * squash * (1.0 + act_gate * (1.0 - squash))).astype(
        jnp.bfloat16
    )
    grad_up = (grad_hidden * act_gate * squash).astype(jnp.bfloat16)
    return (grad_gate, grad_up)


def shards_by_slots(
    inputs_forward,
    routes_forward,
    gates_forward,
    grads_backward,
    routes_backward,
    gates_backward,
    w_gate,
    w_up,
    w_down,
    saved_gate,
    saved_up,
):
    experts = lax.axis_size("dev")
    chosen = routes_forward.shape[2]
    token_rows = inputs_forward[0]
    grad_rows = grads_backward[0]
    slot_total = saved_gate.shape[2]
    capacity = slot_total // experts
    width = token_rows.shape[1]
    targets_forward = slot_targets(routes_forward[0], experts, capacity)
    targets_backward = slot_targets(routes_backward[0], experts, capacity)
    sent_forward = pack_rows(token_rows, targets_forward, slot_total, chosen).reshape(
        experts, capacity, width
    )
    sent_backward = pack_rows(grad_rows, targets_backward, slot_total, chosen).reshape(
        experts, capacity, width
    )
    arrived_forward, arrived_backward = (
        lax.all_to_all(sent_forward, "dev", split_axis=0, concat_axis=0, tiled=True),
        lax.all_to_all(sent_backward, "dev", split_axis=0, concat_axis=0, tiled=True),
    )
    arrived_forward = arrived_forward.reshape(slot_total, width)
    arrived_backward = arrived_backward.reshape(slot_total, width)
    gate_local = w_gate[0, 0]
    up_local = w_up[0, 0]
    down_local = w_down[0, 0]
    stored_gate = saved_gate[0, 0]
    stored_up = saved_up[0, 0]
    contract_last = (((1,), (1,)), ((), ()))
    part_gate = jnp.dot(arrived_forward, gate_local, preferred_element_type=jnp.float32)
    part_up = jnp.dot(arrived_forward, up_local, preferred_element_type=jnp.float32)
    part_grad = lax.dot_general(
        arrived_backward, down_local, contract_last, preferred_element_type=jnp.float32
    )
    gate_share, up_share = (
        lax.psum_scatter(
            part_gate.astype(jnp.bfloat16), "node", scatter_dimension=1, tiled=True
        ).astype(jnp.float32),
        lax.psum_scatter(
            part_up.astype(jnp.bfloat16), "node", scatter_dimension=1, tiled=True
        ).astype(jnp.float32),
    )
    hidden_share = (jax.nn.silu(gate_share) * up_share).astype(jnp.bfloat16)
    hidden = lax.all_gather(hidden_share, "node", axis=1, tiled=True)
    grad_hidden = lax.psum(part_grad.astype(jnp.bfloat16), "node").astype(jnp.float32)
    grad_gate, grad_up = backward_act(grad_hidden, stored_gate, stored_up)
    result_forward = jnp.dot(hidden, down_local, preferred_element_type=jnp.float32).astype(
        jnp.bfloat16
    )
    result_backward = lax.dot_general(
        grad_gate, gate_local, contract_last, preferred_element_type=jnp.float32
    )
    result_backward = result_backward + lax.dot_general(
        grad_up, up_local, contract_last, preferred_element_type=jnp.float32
    )
    result_backward = result_backward.astype(jnp.bfloat16)
    back_forward, back_backward = (
        lax.all_to_all(
            result_forward.reshape(experts, capacity, width),
            "dev",
            split_axis=0,
            concat_axis=0,
            tiled=True,
        ),
        lax.all_to_all(
            result_backward.reshape(experts, capacity, width),
            "dev",
            split_axis=0,
            concat_axis=0,
            tiled=True,
        ),
    )
    mixed_forward = combine_rows(token_rows, gates_forward[0], back_forward, targets_forward)
    mixed_backward = combine_rows(grad_rows, gates_backward[0], back_backward, targets_backward)
    next_forward = from_behind(mixed_forward[None], "section", 1)
    next_backward = from_behind(mixed_backward[None], "section", -1)
    return (next_forward, next_backward)


CONTRACT_LAST = (((1,), (1,)), ((), ()))
PLAIN = (((1,), (0,)), ((), ()))
CONTRACT_FIRST = (((0,), (0,)), ((), ()))
VMEM = pl.BlockSpec(memory_space=pltpu.VMEM)
SMEM = pl.BlockSpec(memory_space=pltpu.SMEM)
VMEM_BYTES = 14 << 20
CF = 1.0
TURN_DOWN = True
SUM_COST = 1e10
SPACE_COST = 10**10
INFO_COST = 10**6
WIDE_BYTES = 56 << 20
ANY = pl.BlockSpec(memory_space=pl.ANY)
HBM = pl.BlockSpec(memory_space=pltpu.HBM)


def across(value, axis, mask):
    count = lax.axis_size(axis)
    return lax.ppermute(value, axis, [(source, source ^ mask) for source in range(count)])


def ring_order(count):
    return [0] + list(range(1, count, 2)) + list(range(2, count, 2))[::-1]


def ring_pairs(count, steps):
    order = ring_order(count)
    return [(order[i], order[(i + steps) % count]) for i in range(count)]


def along_ring(value, steps):
    return lax.ppermute(value, "dev", ring_pairs(lax.axis_size("dev"), steps))


def along_ring_and_sections(value, steps, shift):
    count, sections = lax.axis_size("dev"), lax.axis_size("section")
    pairs = [
        (section * count + source, (section + shift) % sections * count + target)
        for section in range(sections)
        for source, target in ring_pairs(count, steps)
    ]
    return lax.ppermute(value, ("section", "dev"), pairs)


def block_behind(expert, count, steps):
    block = 0
    for target, source in ring_pairs(count, -steps):
        block = block + jnp.where(expert == target, source, 0)
    return block


def call(body, place, operands, after, out_shape, scratch, flops, aliases={}):
    def with_after(place_ref, *refs):
        body(place_ref, *refs[: len(operands)], *refs[len(operands) + len(after) :])

    touched = sum(array.size * array.dtype.itemsize for array in operands)
    return pl.pallas_call(
        with_after,
        in_specs=[SMEM] + [VMEM] * len(operands) + [ANY] * len(after),
        out_specs=jax.tree.map(lambda _: VMEM, out_shape),
        scratch_shapes=scratch,
        out_shape=out_shape,
        input_output_aliases={index + 1: out for index, out in aliases.items()},
        cost_estimate=pl.CostEstimate(flops=int(CF * flops), bytes_accessed=int(CF * touched), transcendentals=0),
        compiler_params=pltpu.CompilerParams(vmem_limit_bytes=VMEM_BYTES),
    )(place, *operands, *after)


def matmul(left, right, dims=(((1,), (0,)), ((), ()))):
    return lax.dot_general(left, right, dims, preferred_element_type=jnp.float32)


def by_owner(place_ref, rows_ref, sorted_rows, nodes):
    rows = sorted_rows.shape[0] // nodes
    for mask in range(nodes):
        first = pl.multiple_of((place_ref[0] ^ mask) * rows, rows)
        sorted_rows[mask * rows : (mask + 1) * rows, :] = rows_ref[pl.ds(first, rows), :]


def first_products(place, token_rows, grad_rows, weights, dims, nodes, planes, after):
    (count, width), hidden = token_rows.shape, weights[0].shape[1]
    share = count // nodes

    def body(place_ref, token_ref, grad_ref, gate_ref, up_ref, down_ref, *refs):
        outs, (sorted_tokens, sorted_grads) = refs[:nodes], refs[nodes:]
        by_owner(place_ref, token_ref, sorted_tokens, nodes)
        by_owner(place_ref, grad_ref, sorted_grads, nodes)
        parts = (
            matmul(sorted_tokens[...], gate_ref[...]),
            matmul(sorted_tokens[...], up_ref[...]),
            matmul(sorted_grads[...], down_ref[...], dims),
        )
        for index, part in enumerate(parts):
            for mask in range(nodes):
                outs[mask][index] = part[mask * share : (mask + 1) * share].astype(jnp.bfloat16)

    return call(
        body,
        place,
        (token_rows, grad_rows, *weights),
        after,
        [jax.ShapeDtypeStruct((planes, share, hidden), jnp.bfloat16)] * nodes,
        [pltpu.VMEM((count, width), jnp.bfloat16)] * 2,
        6 * count * width * hidden,
    )


def transposed(place, weight, after):
    def body(place_ref, weight_ref, out):
        out[...] = weight_ref[...].T

    shape = jax.ShapeDtypeStruct(weight.shape[::-1], weight.dtype)
    return call(body, place, (weight,), after, shape, [], 0)


def activations(place, pieces, filled, after, extra=()):
    nodes, (_, share, hidden) = len(pieces), pieces[0].shape

    def body(place_ref, *refs):
        piece_refs, extra_refs = refs[:nodes], refs[nodes + len(filled) :][: len(extra)]
        outs = refs[nodes + len(filled) + len(extra) :]
        gate, up, grad = (
            sum(ref[index].astype(jnp.float32) for ref in piece_refs) for index in range(3)
        )
        act = (gate / (1.0 + jnp.exp(-gate)) * up).astype(jnp.bfloat16)
        grad = grad.astype(jnp.bfloat16)
        for out in outs:
            start = 3 if filled else 0
            out[start] = act
            out[start + 1] = grad
            for index, ref in enumerate(extra_refs):
                out[start + 2 + index] = ref[1]

    shapes = [jax.ShapeDtypeStruct(array.shape, array.dtype) for array in filled]
    return call(
        body,
        place,
        (*pieces, *filled, *extra),
        after,
        shapes or [jax.ShapeDtypeStruct((2 + len(extra), share, hidden), jnp.bfloat16)],
        [],
        16 * share * hidden,
        {nodes + index: index for index in range(len(filled))},
    )


def first_plane(place, planes, after):
    def body(place_ref, planes_ref, out):
        out[0] = planes_ref[0]

    shape = (1, *planes.shape[1:])
    return call(body, place, (planes,), after, jax.ShapeDtypeStruct(shape, planes.dtype), [], 0)


def join(place_ref, piece_refs, index, joined):
    rows = piece_refs[0].shape[1]
    for mask, ref in enumerate(piece_refs):
        first = pl.multiple_of((place_ref[0] ^ mask) * rows, rows)
        joined[pl.ds(first, rows), :] = ref[index]


def copied(sources, targets, sems):
    copies = [
        pltpu.make_async_copy(source, target, sems.at[index])
        for index, (source, target) in enumerate(zip(sources, targets))
    ]
    for copy in copies:
        copy.start()
    return copies


def with_info(rows, routes, gates, after):
    (count, width), chosen = rows.shape, routes[0].shape[0]
    height = -(-6 * chosen // 16) * 16
    small = (*routes, *gates)

    def body(rows_ref, *refs):
        infos, out = refs[:4], refs[-1]
        lines = [ref[...].astype(jnp.float32) for ref in infos[:2]]
        for ref in infos[2:]:
            coarse = ref[...].astype(jnp.bfloat16).astype(jnp.float32)
            lines += [coarse, ref[...] - coarse]
        lines.append(jnp.zeros((height - 6 * chosen, count), jnp.float32))
        out[0:count, :] = rows_ref[...]
        out[count:, :] = jnp.zeros((height, width), jnp.bfloat16)
        out[count:, 0:count] = jnp.concatenate(lines).astype(jnp.bfloat16)

    return pl.pallas_call(
        body,
        in_specs=[VMEM] * 5 + [ANY] * len(after),
        out_specs=VMEM,
        out_shape=jax.ShapeDtypeStruct((count + height, width), jnp.bfloat16),
        cost_estimate=pl.CostEstimate(flops=INFO_COST, bytes_accessed=INFO_COST // 100, transcendentals=0),
        compiler_params=pltpu.CompilerParams(vmem_limit_bytes=4 << 20),
    )(rows, *small, *after)


def marker():
    def body(out):
        out[...] = jnp.zeros_like(out)

    return pl.pallas_call(
        body,
        out_specs=VMEM,
        out_shape=jax.ShapeDtypeStruct((8, 128), jnp.float32),
        cost_estimate=pl.CostEstimate(flops=SPACE_COST, bytes_accessed=SPACE_COST // 100, transcendentals=0),
        compiler_params=pltpu.CompilerParams(vmem_limit_bytes=1 << 20),
    )()


def opening_products(place, token_rows, grad_rows, weights, nodes):
    (count, width), hidden = grad_rows.shape, weights[0].shape[1]
    share = count // nodes
    operands = (token_rows, weights[0], weights[1], grad_rows, weights[2])
    cuts = 4

    def body(place_ref, *refs):
        inputs, pieces, held = refs[:5], refs[5 : 5 + nodes], refs[5 + nodes : 10 + nodes]
        sorted_rows, sems = refs[10 + nodes :]

        def pieces_of(ref):
            rows = ref.shape[0] // cuts
            return [ref.at[pl.ds(cut * rows, rows)] for cut in range(cuts)]

        parts = [
            copied(pieces_of(source), pieces_of(target), sems.at[index])
            for index, (source, target) in enumerate(zip(inputs, held))
        ]

        def wait(index):
            for copy in parts[index]:
                copy.wait()

        def give(index, part):
            for mask in range(nodes):
                pieces[mask][index] = part[mask * share : (mask + 1) * share].astype(jnp.bfloat16)

        wait(0)
        by_owner(place_ref, held[0], sorted_rows, nodes)
        for index in (0, 1):
            wait(index + 1)
            give(index, matmul(sorted_rows[...], held[index + 1][...]))
        wait(3)
        by_owner(place_ref, held[3], sorted_rows, nodes)
        wait(4)
        give(2, matmul(sorted_rows[...], held[4][...], CONTRACT_LAST))

    return pl.pallas_call(
        body,
        in_specs=[SMEM] + [HBM] * 5,
        out_specs=[VMEM] * nodes,
        out_shape=[jax.ShapeDtypeStruct((3, share, hidden), jnp.bfloat16)] * nodes,
        scratch_shapes=[pltpu.VMEM(value.shape, value.dtype) for value in operands]
        + [pltpu.VMEM((count, width), jnp.bfloat16), pltpu.SemaphoreType.DMA((5, cuts))],
        cost_estimate=pl.CostEstimate(
            flops=int(CF * 6 * count * width * hidden),
            bytes_accessed=int(CF * 6 * width * hidden),
            transcendentals=0,
        ),
        compiler_params=pltpu.CompilerParams(vmem_limit_bytes=WIDE_BYTES),
    )(place, *operands)


def info_of(ref, count, chosen, which):
    lines = ref[count:, 0:count].astype(jnp.float32)
    routes = lines[which * chosen : (which + 1) * chosen].astype(jnp.int32)
    first = 2 * (which + 1) * chosen
    return routes, lines[first : first + chosen] + lines[first + chosen : first + 2 * chosen]


def weight_column(expert, routes, gates):
    chosen, count = routes.shape
    line = jnp.zeros((1, count), jnp.float32)
    for choice in range(chosen):
        line += jnp.where(routes[choice : choice + 1] == expert, gates[choice : choice + 1], 0.0)
    diagonal = lax.broadcasted_iota(jnp.int32, (count, count), 0) == lax.broadcasted_iota(
        jnp.int32, (count, count), 1
    )
    return jnp.sum(jnp.where(diagonal, line, 0.0), axis=1, keepdims=True)


def slot_selection(expert, routes, capacity):
    chosen, count = routes.shape
    named = jnp.zeros((1, count), jnp.float32)
    for choice in range(chosen):
        named += (routes[choice : choice + 1] == expert).astype(jnp.float32)
    earlier = lax.broadcasted_iota(jnp.int32, (count, count), 0) < lax.broadcasted_iota(
        jnp.int32, (count, count), 1
    )
    rank = matmul(
        jnp.broadcast_to(named, (16, count)).astype(jnp.bfloat16),
        earlier.astype(jnp.float32).astype(jnp.bfloat16),
    )[0:1]
    slot = jnp.where(named > 0, rank, -1.0)
    slots = lax.broadcasted_iota(jnp.int32, (capacity, count), 0).astype(jnp.float32)
    return (slots == slot).astype(jnp.float32).astype(jnp.bfloat16)


def give(out, weight, result, added_refs):
    total = weight * result.astype(jnp.bfloat16).astype(jnp.float32)
    for ref in added_refs:
        total += ref[0 : out.shape[0], :].astype(jnp.float32)
    out[...] = total.astype(jnp.bfloat16)


def forward_results(place, pieces, plane, w_down, info, chosen, added, after):
    nodes, (_, share, hidden), width = len(pieces), pieces[0].shape, w_down.shape[1]
    count = share * nodes

    def body(place_ref, *refs):
        piece_refs, refs = refs[:nodes], refs[nodes:]
        (down_ref, info_ref), added_refs, (out, joined) = refs[:2], refs[2:-2], refs[-2:]
        join(place_ref, piece_refs, plane, joined)
        weight = weight_column(place_ref[1], *info_of(info_ref, count, chosen, 0))
        give(out, weight, matmul(joined[...], down_ref[...]), added_refs)

    return call(
        body,
        place,
        (*pieces, w_down, info, *added),
        after,
        jax.ShapeDtypeStruct((count, width), jnp.bfloat16),
        [pltpu.VMEM((count, hidden), jnp.bfloat16)],
        2 * count * width * hidden,
    )


def backward_factors(place, saved_gate, saved_up, info, chosen, count, block, after):
    slots, hidden = saved_gate.shape
    experts = slots // count

    def body(place_ref, saved_gate_ref, saved_up_ref, info_ref, gate_out, up_out):
        routes, _ = info_of(info_ref, count, chosen, 1)
        select = slot_selection(place_ref[1], routes, count)
        first = pl.multiple_of(block_behind(place_ref[1], experts, block) * count, count)
        act_gate = matmul(select, saved_gate_ref[pl.ds(first, count), :], CONTRACT_FIRST)
        act_up = matmul(select, saved_up_ref[pl.ds(first, count), :], CONTRACT_FIRST)
        squash = 1.0 / (1.0 + jnp.exp(-act_gate))
        gate_out[...] = act_up * squash * (1.0 + act_gate * (1.0 - squash))
        up_out[...] = act_gate * squash

    return call(
        body,
        place,
        (saved_gate, saved_up, info),
        after,
        [jax.ShapeDtypeStruct((count, hidden), jnp.float32)] * 2,
        [],
        4 * count * count * hidden,
    )


def backward_results(place, pieces, plane, w_gate, w_up, factors, info, chosen, added, after):
    nodes, (_, share, hidden), width = len(pieces), pieces[0].shape, w_gate.shape[1]
    count = share * nodes

    def body(place_ref, *refs):
        piece_refs, refs = refs[:nodes], refs[nodes:]
        gate_ref, up_ref, gate_factor, up_factor, info_ref = refs[:5]
        added_refs, (out, joined) = refs[5:-2], refs[-2:]
        join(place_ref, piece_refs, plane, joined)
        weight = weight_column(place_ref[1], *info_of(info_ref, count, chosen, 1))
        grad_hidden = joined[...].astype(jnp.float32)
        grad_gate = (grad_hidden * gate_factor[...]).astype(jnp.bfloat16)
        grad_up = (grad_hidden * up_factor[...]).astype(jnp.bfloat16)
        result = matmul(grad_gate, gate_ref[...])
        result += matmul(grad_up, up_ref[...])
        give(out, weight, result, added_refs)

    return call(
        body,
        place,
        (*pieces, w_gate, w_up, *factors, info, *added),
        after,
        jax.ShapeDtypeStruct((count, width), jnp.bfloat16),
        [pltpu.VMEM((count, hidden), jnp.bfloat16)],
        4 * count * width * hidden,
    )


def sum_rows(values, after):
    def body(*refs):
        total = sum(ref[...].astype(jnp.float32) for ref in refs[: len(values)])
        refs[-1][...] = total

    return pl.pallas_call(
        body,
        in_specs=[VMEM] * len(values) + [ANY] * len(after),
        out_specs=VMEM,
        out_shape=jax.ShapeDtypeStruct(values[0].shape, jnp.float32),
        cost_estimate=pl.CostEstimate(
            flops=int(SUM_COST), bytes_accessed=int(SUM_COST / 100), transcendentals=0
        ),
        compiler_params=pltpu.CompilerParams(vmem_limit_bytes=VMEM_BYTES),
    )(*values, *after)


def ring_shards(
    inputs_forward,
    routes_forward,
    gates_forward,
    grads_backward,
    routes_backward,
    gates_backward,
    w_gate,
    w_up,
    w_down,
    saved_gate,
    saved_up,
):
    experts, nodes = lax.axis_size("dev"), lax.axis_size("node")
    place = jnp.stack([lax.axis_index("node"), lax.axis_index("dev")]).astype(jnp.int32)
    weights = (w_gate[0, 0], w_up[0, 0], w_down[0, 0])
    stored_gate, stored_up = saved_gate[0, 0], saved_up[0, 0]

    chosen = routes_forward.shape[2]
    tokens = [inputs_forward[0]]
    grads = [
        with_info(
            grads_backward[0],
            (routes_forward[0].T, routes_backward[0].T),
            (gates_forward[0].T, gates_backward[0].T),
            (marker(),),
        )
    ]
    for _ in range(1, experts):
        tokens.append(along_ring(tokens[-1], 1))
        grads.append(along_ring(grads[-1], 1))

    count = grads_backward.shape[1]
    sent, parts = [None] * experts, [None] * experts
    acts = [None] * experts, [None] * experts
    done = []

    def exchange(own):
        arrived = [across(own[mask % len(own)], "node", mask) for mask in range(nodes - 1, 0, -1)]
        return [own[0]] + arrived[::-1]

    factors = [None] * experts

    def prepare(step):
        factors[step] = backward_factors(
            place, stored_gate, stored_up, grads[step], chosen, count, step, done[-1:]
        )
        done.append(factors[step][0])

    first_weights = [weights, CONTRACT_LAST]
    turned = [None, None]

    def turn(index):
        value = transposed(place, weights[index], done[-1:])
        done.append(value)
        return value

    def first(step, *after):
        sent[step] = first_products(
            place, tokens[step], grads[step], first_weights[0], first_weights[1], nodes, 5 if step > 1 else 3, (*done[-1:], *after)
        )
        done.append(sent[step][0])
        if step < 2:
            parts[step] = exchange(sent[step])

    def middle(step, *after):
        joint = 0 < step < experts - 1
        filled, extra = (sent[step + 1], ()) if joint else ((), (own_acts,))
        own = activations(place, parts[step], filled, (*done[-1:], *after), extra)
        done.append(own[0])
        arrived = exchange(own)
        plane = 3 if joint else 0
        acts[0][step], acts[1][step] = (arrived, plane), (arrived, plane + 1)
        if joint:
            parts[step + 1] = arrived
        else:
            acts[1][0] = (arrived, plane + 2)

    sums, hops, base = [[], []], [(), ()], [None, None]

    def last(step, kind, *after):
        shift = 1 - 2 * kind
        added = (inputs_forward[0], grads_backward[0])[kind : kind + 1] if step == 0 else ()
        if step >= 2:
            added = hops[kind]
        if kind == 0:
            value = forward_results(
                place, *acts[0][step], weights[2], grads[step], chosen, added, (*done[-1:], *after)
            )
        else:
            value = backward_results(
                place, *acts[1][step], *turned, factors[step], grads[step], chosen, added, (*done[-1:], *after)
            )
        done.append(value)
        if step == 0:
            base[kind] = from_behind(value, "section", shift)
        elif step == 1:
            sums[kind].append(along_ring_and_sections(value, -1, shift))
        elif step < experts - 1:
            hops[kind] = (along_ring(value, 1),)
        else:
            sums[kind].append(along_ring_and_sections(value, 1, shift))

    first(0)
    if TURN_DOWN:
        first_weights[:] = (*weights[:2], turn(2)), PLAIN
    first(1)
    own_acts = activations(place, parts[0], (), done[-1:])[0]
    done.append(own_acts)
    for step in range(1, experts - 1):
        if step == experts - 2:
            turned[:] = turn(0), turn(1)
        first(step + 1)
        prepare(step)
        middle(step)
        if step >= 2:
            last(step - 1, 0)
            last(step - 1, 1)
    prepare(experts - 1)
    prepare(0)
    middle(experts - 1)
    if experts > 2:
        last(experts - 2, 0)
        last(experts - 2, 1, *[values[0] for values in sums if values])
    last(experts - 1, 0)
    own_plane = first_plane(place, own_acts, (*done[-1:], *acts[0][experts - 1][0][1:]))
    done.append(own_plane)
    acts[0][0] = (exchange([own_plane]), 0)
    last(experts - 1, 1)
    last(0, 0)
    last(0, 1)
    outs = []
    for values, own in zip(sums, base):
        total = sum(value.astype(jnp.float32) for value in (sum_rows(values[-1:], (*done[-1:], *outs)), *values[:-1], own))
        outs.append(total.astype(jnp.bfloat16))
    return tuple(out[None] for out in outs)


def power_of_two(number):
    return number & (number - 1) == 0


def shards(*args):
    experts, nodes = lax.axis_size("dev"), lax.axis_size("node")
    tokens, capacity = args[0].shape[1], args[9].shape[2] // experts
    if capacity == tokens and experts > 1 and power_of_two(nodes) and tokens % (16 * nodes) == 0:
        return ring_shards(*args)
    return shards_by_slots(*args)


def solution(mesh):
    return jax.shard_map(
        shards,
        mesh=mesh,
        in_specs=(
            P("section", "dev", "node"),
            P("section", "dev", None),
            P("section", "dev", None),
            P("section", "dev", "node"),
            P("section", "dev", None),
            P("section", "dev", None),
            P("section", "dev", "node", None),
            P("section", "dev", "node", None),
            P("section", "dev", None, "node"),
            P("section", "dev", None, None),
            P("section", "dev", None, None),
        ),
        out_specs=(P("section", "dev", "node"), P("section", "dev", "node")),
        check_vma=False,
    )
```

```python
import functools

import jax
import jax.numpy as jnp
from jax import lax
from jax.experimental import pallas as pl
from jax.experimental.pallas import tpu as pltpu
from jax.sharding import PartitionSpec as P


def from_behind(value, axis, steps):
    count = lax.axis_size(axis)
    pairs = [(source, (source + steps) % count) for source in range(count)]
    return lax.ppermute(value, axis, pairs)


def slot_targets(routing, experts, capacity):
    flat = routing.reshape(-1)
    onehot = (flat[:, None] == jnp.arange(experts, dtype=jnp.int32)[None, :]).astype(jnp.int32)
    earlier = jnp.cumsum(onehot, axis=0) - onehot
    return flat * capacity + jnp.sum(earlier * onehot, axis=1)


def pack_rows(token_rows, targets, slot_count, chosen):
    match = (jnp.arange(slot_count, dtype=jnp.int32)[:, None] == targets[None, :]).astype(
        jnp.bfloat16
    )
    select = jnp.sum(match.reshape(slot_count, token_rows.shape[0], chosen), axis=2)
    return jnp.dot(select, token_rows, preferred_element_type=jnp.float32).astype(jnp.bfloat16)


def combine_rows(token_rows, weights_of, returned_rows, targets):
    width = token_rows.shape[1]
    picked = returned_rows.reshape(-1, width)[targets]
    picked = picked.reshape(token_rows.shape[0], weights_of.shape[1], width).astype(jnp.float32)
    mixed = token_rows.astype(jnp.float32) + jnp.sum(weights_of[:, :, None] * picked, axis=1)
    return mixed.astype(jnp.bfloat16)


def backward_act(grad_hidden, stored_gate, stored_up):
    act_gate = stored_gate.astype(jnp.float32)
    act_up = stored_up.astype(jnp.float32)
    squash = jax.nn.sigmoid(act_gate)
    grad_gate = (grad_hidden * act_up * squash * (1.0 + act_gate * (1.0 - squash))).astype(
        jnp.bfloat16
    )
    grad_up = (grad_hidden * act_gate * squash).astype(jnp.bfloat16)
    return (grad_gate, grad_up)


def shards_by_slots(
    inputs_forward,
    routes_forward,
    gates_forward,
    grads_backward,
    routes_backward,
    gates_backward,
    w_gate,
    w_up,
    w_down,
    saved_gate,
    saved_up,
):
    experts = lax.axis_size("dev")
    chosen = routes_forward.shape[2]
    token_rows = inputs_forward[0]
    grad_rows = grads_backward[0]
    slot_total = saved_gate.shape[2]
    capacity = slot_total // experts
    width = token_rows.shape[1]
    targets_forward = slot_targets(routes_forward[0], experts, capacity)
    targets_backward = slot_targets(routes_backward[0], experts, capacity)
    sent_forward = pack_rows(token_rows, targets_forward, slot_total, chosen).reshape(
        experts, capacity, width
    )
    sent_backward = pack_rows(grad_rows, targets_backward, slot_total, chosen).reshape(
        experts, capacity, width
    )
    arrived_forward, arrived_backward = (
        lax.all_to_all(sent_forward, "dev", split_axis=0, concat_axis=0, tiled=True),
        lax.all_to_all(sent_backward, "dev", split_axis=0, concat_axis=0, tiled=True),
    )
    arrived_forward = arrived_forward.reshape(slot_total, width)
    arrived_backward = arrived_backward.reshape(slot_total, width)
    gate_local = w_gate[0, 0]
    up_local = w_up[0, 0]
    down_local = w_down[0, 0]
    stored_gate = saved_gate[0, 0]
    stored_up = saved_up[0, 0]
    contract_last = (((1,), (1,)), ((), ()))
    part_gate = jnp.dot(arrived_forward, gate_local, preferred_element_type=jnp.float32)
    part_up = jnp.dot(arrived_forward, up_local, preferred_element_type=jnp.float32)
    part_grad = lax.dot_general(
        arrived_backward, down_local, contract_last, preferred_element_type=jnp.float32
    )
    gate_share, up_share = (
        lax.psum_scatter(
            part_gate.astype(jnp.bfloat16), "node", scatter_dimension=1, tiled=True
        ).astype(jnp.float32),
        lax.psum_scatter(
            part_up.astype(jnp.bfloat16), "node", scatter_dimension=1, tiled=True
        ).astype(jnp.float32),
    )
    hidden_share = (jax.nn.silu(gate_share) * up_share).astype(jnp.bfloat16)
    hidden = lax.all_gather(hidden_share, "node", axis=1, tiled=True)
    grad_hidden = lax.psum(part_grad.astype(jnp.bfloat16), "node").astype(jnp.float32)
    grad_gate, grad_up = backward_act(grad_hidden, stored_gate, stored_up)
    result_forward = jnp.dot(hidden, down_local, preferred_element_type=jnp.float32).astype(
        jnp.bfloat16
    )
    result_backward = lax.dot_general(
        grad_gate, gate_local, contract_last, preferred_element_type=jnp.float32
    )
    result_backward = result_backward + lax.dot_general(
        grad_up, up_local, contract_last, preferred_element_type=jnp.float32
    )
    result_backward = result_backward.astype(jnp.bfloat16)
    back_forward, back_backward = (
        lax.all_to_all(
            result_forward.reshape(experts, capacity, width),
            "dev",
            split_axis=0,
            concat_axis=0,
            tiled=True,
        ),
        lax.all_to_all(
            result_backward.reshape(experts, capacity, width),
            "dev",
            split_axis=0,
            concat_axis=0,
            tiled=True,
        ),
    )
    mixed_forward = combine_rows(token_rows, gates_forward[0], back_forward, targets_forward)
    mixed_backward = combine_rows(grad_rows, gates_backward[0], back_backward, targets_backward)
    next_forward = from_behind(mixed_forward[None], "section", 1)
    next_backward = from_behind(mixed_backward[None], "section", -1)
    return (next_forward, next_backward)


CONTRACT_LAST = (((1,), (1,)), ((), ()))
PLAIN = (((1,), (0,)), ((), ()))
CONTRACT_FIRST = (((0,), (0,)), ((), ()))
VMEM = pl.BlockSpec(memory_space=pltpu.VMEM)
SMEM = pl.BlockSpec(memory_space=pltpu.SMEM)
VMEM_BYTES = 14 << 20
SUM_COST = 1e10
SPACE_COST = 10**10
INFO_COST = 10**6
ANY = pl.BlockSpec(memory_space=pl.ANY)


def across(value, axis, mask):
    count = lax.axis_size(axis)
    return lax.ppermute(value, axis, [(source, source ^ mask) for source in range(count)])


def ring_order(count):
    return [0] + list(range(1, count, 2)) + list(range(2, count, 2))[::-1]


def ring_pairs(count, steps):
    order = ring_order(count)
    return [(order[i], order[(i + steps) % count]) for i in range(count)]


def along_ring(value, steps):
    return lax.ppermute(value, "dev", ring_pairs(lax.axis_size("dev"), steps))


def along_ring_and_sections(value, steps, shift):
    count, sections = lax.axis_size("dev"), lax.axis_size("section")
    pairs = [
        (section * count + source, (section + shift) % sections * count + target)
        for section in range(sections)
        for source, target in ring_pairs(count, steps)
    ]
    return lax.ppermute(value, ("section", "dev"), pairs)


def block_behind(expert, count, steps):
    block = 0
    for target, source in ring_pairs(count, -steps):
        block = block + jnp.where(expert == target, source, 0)
    return block


def call(body, place, operands, after, out_shape, scratch, flops, aliases={}):
    def with_after(place_ref, *refs):
        body(place_ref, *refs[: len(operands)], *refs[len(operands) + len(after) :])

    touched = sum(array.size * array.dtype.itemsize for array in operands)
    return pl.pallas_call(
        with_after,
        in_specs=[SMEM] + [VMEM] * len(operands) + [ANY] * len(after),
        out_specs=jax.tree.map(lambda _: VMEM, out_shape),
        scratch_shapes=scratch,
        out_shape=out_shape,
        input_output_aliases={index + 1: out for index, out in aliases.items()},
        cost_estimate=pl.CostEstimate(flops=flops, bytes_accessed=touched, transcendentals=0),
        compiler_params=pltpu.CompilerParams(vmem_limit_bytes=VMEM_BYTES),
    )(place, *operands, *after)


def matmul(left, right, dims=(((1,), (0,)), ((), ()))):
    return lax.dot_general(left, right, dims, preferred_element_type=jnp.float32)


def by_owner(place_ref, rows_ref, sorted_rows, nodes):
    rows = sorted_rows.shape[0] // nodes
    for mask in range(nodes):
        first = pl.multiple_of((place_ref[0] ^ mask) * rows, rows)
        sorted_rows[mask * rows : (mask + 1) * rows, :] = rows_ref[pl.ds(first, rows), :]


def first_products(place, token_rows, grad_rows, weights, dims, nodes, planes, after):
    (count, width), hidden = token_rows.shape, weights[0].shape[1]
    share = count // nodes

    def body(place_ref, token_ref, grad_ref, gate_ref, up_ref, down_ref, *refs):
        outs, (sorted_tokens, sorted_grads) = refs[:nodes], refs[nodes:]
        by_owner(place_ref, token_ref, sorted_tokens, nodes)
        by_owner(place_ref, grad_ref, sorted_grads, nodes)
        parts = (
            matmul(sorted_tokens[...], gate_ref[...]),
            matmul(sorted_tokens[...], up_ref[...]),
            matmul(sorted_grads[...], down_ref[...], dims),
        )
        for index, part in enumerate(parts):
            for mask in range(nodes):
                outs[mask][index] = part[mask * share : (mask + 1) * share].astype(jnp.bfloat16)

    return call(
        body,
        place,
        (token_rows, grad_rows, *weights),
        after,
        [jax.ShapeDtypeStruct((planes, share, hidden), jnp.bfloat16)] * nodes,
        [pltpu.VMEM((count, width), jnp.bfloat16)] * 2,
        6 * count * width * hidden,
    )


def transposed(place, weight, after):
    def body(place_ref, weight_ref, out):
        out[...] = weight_ref[...].T

    shape = jax.ShapeDtypeStruct(weight.shape[::-1], weight.dtype)
    return call(body, place, (weight,), after, shape, [], 0)


def activations(place, pieces, filled, after, extra=()):
    nodes, (_, share, hidden) = len(pieces), pieces[0].shape

    def body(place_ref, *refs):
        piece_refs, extra_refs = refs[:nodes], refs[nodes + len(filled) :][: len(extra)]
        outs = refs[nodes + len(filled) + len(extra) :]
        gate, up, grad = (
            sum(ref[index].astype(jnp.float32) for ref in piece_refs) for index in range(3)
        )
        act = (gate / (1.0 + jnp.exp(-gate)) * up).astype(jnp.bfloat16)
        grad = grad.astype(jnp.bfloat16)
        for out in outs:
            start = 3 if filled else 0
            out[start] = act
            out[start + 1] = grad
            for index, ref in enumerate(extra_refs):
                out[start + 2 + index] = ref[1]

    shapes = [jax.ShapeDtypeStruct(array.shape, array.dtype) for array in filled]
    return call(
        body,
        place,
        (*pieces, *filled, *extra),
        after,
        shapes or [jax.ShapeDtypeStruct((2 + len(extra), share, hidden), jnp.bfloat16)],
        [],
        16 * share * hidden,
        {nodes + index: index for index in range(len(filled))},
    )


def first_plane(place, planes, after):
    def body(place_ref, planes_ref, out):
        out[0] = planes_ref[0]

    shape = (1, *planes.shape[1:])
    return call(body, place, (planes,), after, jax.ShapeDtypeStruct(shape, planes.dtype), [], 0)


def join(place_ref, piece_refs, index, joined):
    rows = piece_refs[0].shape[1]
    for mask, ref in enumerate(piece_refs):
        first = pl.multiple_of((place_ref[0] ^ mask) * rows, rows)
        joined[pl.ds(first, rows), :] = ref[index]


def with_info(rows, routes, gates, after):
    (count, width), chosen = rows.shape, routes[0].shape[0]
    height = -(-6 * chosen // 16) * 16
    small = (*routes, *gates)

    def body(rows_ref, *refs):
        infos, out = refs[:4], refs[-1]
        lines = [ref[...].astype(jnp.float32) for ref in infos[:2]]
        for ref in infos[2:]:
            coarse = ref[...].astype(jnp.bfloat16).astype(jnp.float32)
            lines += [coarse, ref[...] - coarse]
        lines.append(jnp.zeros((height - 6 * chosen, count), jnp.float32))
        out[0:count, :] = rows_ref[...]
        out[count:, :] = jnp.zeros((height, width), jnp.bfloat16)
        out[count:, 0:count] = jnp.concatenate(lines).astype(jnp.bfloat16)

    return pl.pallas_call(
        body,
        in_specs=[VMEM] * 5 + [ANY] * len(after),
        out_specs=VMEM,
        out_shape=jax.ShapeDtypeStruct((count + height, width), jnp.bfloat16),
        cost_estimate=pl.CostEstimate(flops=INFO_COST, bytes_accessed=INFO_COST // 100, transcendentals=0),
        compiler_params=pltpu.CompilerParams(vmem_limit_bytes=4 << 20),
    )(rows, *small, *after)


def marker():
    def body(out):
        out[...] = jnp.zeros_like(out)

    return pl.pallas_call(
        body,
        out_specs=VMEM,
        out_shape=jax.ShapeDtypeStruct((8, 128), jnp.float32),
        cost_estimate=pl.CostEstimate(flops=SPACE_COST, bytes_accessed=SPACE_COST // 100, transcendentals=0),
        compiler_params=pltpu.CompilerParams(vmem_limit_bytes=1 << 20),
    )()


def info_of(ref, count, chosen, which):
    lines = ref[count:, 0:count].astype(jnp.float32)
    routes = lines[which * chosen : (which + 1) * chosen].astype(jnp.int32)
    first = 2 * (which + 1) * chosen
    return routes, lines[first : first + chosen] + lines[first + chosen : first + 2 * chosen]


def weight_column(expert, routes, gates):
    chosen, count = routes.shape
    line = jnp.zeros((1, count), jnp.float32)
    for choice in range(chosen):
        line += jnp.where(routes[choice : choice + 1] == expert, gates[choice : choice + 1], 0.0)
    diagonal = lax.broadcasted_iota(jnp.int32, (count, count), 0) == lax.broadcasted_iota(
        jnp.int32, (count, count), 1
    )
    return jnp.sum(jnp.where(diagonal, line, 0.0), axis=1, keepdims=True)


def slot_selection(expert, routes, capacity):
    chosen, count = routes.shape
    named = jnp.zeros((1, count), jnp.float32)
    for choice in range(chosen):
        named += (routes[choice : choice + 1] == expert).astype(jnp.float32)
    earlier = lax.broadcasted_iota(jnp.int32, (count, count), 0) < lax.broadcasted_iota(
        jnp.int32, (count, count), 1
    )
    rank = matmul(
        jnp.broadcast_to(named, (16, count)).astype(jnp.bfloat16),
        earlier.astype(jnp.float32).astype(jnp.bfloat16),
    )[0:1]
    slot = jnp.where(named > 0, rank, -1.0)
    slots = lax.broadcasted_iota(jnp.int32, (capacity, count), 0).astype(jnp.float32)
    return (slots == slot).astype(jnp.float32).astype(jnp.bfloat16)


def give(out, weight, result, added_refs):
    total = weight * result.astype(jnp.bfloat16).astype(jnp.float32)
    for ref in added_refs:
        total += ref[0 : out.shape[0], :].astype(jnp.float32)
    out[...] = total.astype(jnp.bfloat16)


def forward_results(place, pieces, plane, w_down, info, chosen, added, after):
    nodes, (_, share, hidden), width = len(pieces), pieces[0].shape, w_down.shape[1]
    count = share * nodes

    def body(place_ref, *refs):
        piece_refs, refs = refs[:nodes], refs[nodes:]
        (down_ref, info_ref), added_refs, (out, joined) = refs[:2], refs[2:-2], refs[-2:]
        join(place_ref, piece_refs, plane, joined)
        weight = weight_column(place_ref[1], *info_of(info_ref, count, chosen, 0))
        give(out, weight, matmul(joined[...], down_ref[...]), added_refs)

    return call(
        body,
        place,
        (*pieces, w_down, info, *added),
        after,
        jax.ShapeDtypeStruct((count, width), jnp.bfloat16),
        [pltpu.VMEM((count, hidden), jnp.bfloat16)],
        2 * count * width * hidden,
    )


def backward_factors(place, saved_gate, saved_up, info, chosen, count, block, after):
    slots, hidden = saved_gate.shape
    experts = slots // count

    def body(place_ref, saved_gate_ref, saved_up_ref, info_ref, gate_out, up_out):
        routes, _ = info_of(info_ref, count, chosen, 1)
        select = slot_selection(place_ref[1], routes, count)
        first = pl.multiple_of(block_behind(place_ref[1], experts, block) * count, count)
        act_gate = matmul(select, saved_gate_ref[pl.ds(first, count), :], CONTRACT_FIRST)
        act_up = matmul(select, saved_up_ref[pl.ds(first, count), :], CONTRACT_FIRST)
        squash = 1.0 / (1.0 + jnp.exp(-act_gate))
        gate_out[...] = act_up * squash * (1.0 + act_gate * (1.0 - squash))
        up_out[...] = act_gate * squash

    return call(
        body,
        place,
        (saved_gate, saved_up, info),
        after,
        [jax.ShapeDtypeStruct((count, hidden), jnp.float32)] * 2,
        [],
        4 * count * count * hidden,
    )


def backward_results(place, pieces, plane, w_gate, w_up, factors, info, chosen, added, after):
    nodes, (_, share, hidden), width = len(pieces), pieces[0].shape, w_gate.shape[1]
    count = share * nodes

    def body(place_ref, *refs):
        piece_refs, refs = refs[:nodes], refs[nodes:]
        gate_ref, up_ref, gate_factor, up_factor, info_ref = refs[:5]
        added_refs, (out, joined) = refs[5:-2], refs[-2:]
        join(place_ref, piece_refs, plane, joined)
        weight = weight_column(place_ref[1], *info_of(info_ref, count, chosen, 1))
        grad_hidden = joined[...].astype(jnp.float32)
        grad_gate = (grad_hidden * gate_factor[...]).astype(jnp.bfloat16)
        grad_up = (grad_hidden * up_factor[...]).astype(jnp.bfloat16)
        result = matmul(grad_gate, gate_ref[...])
        result += matmul(grad_up, up_ref[...])
        give(out, weight, result, added_refs)

    return call(
        body,
        place,
        (*pieces, w_gate, w_up, *factors, info, *added),
        after,
        jax.ShapeDtypeStruct((count, width), jnp.bfloat16),
        [pltpu.VMEM((count, hidden), jnp.bfloat16)],
        4 * count * width * hidden,
    )


def sum_rows(values, after):
    def body(*refs):
        total = sum(ref[...].astype(jnp.float32) for ref in refs[: len(values)])
        refs[-1][...] = total

    return pl.pallas_call(
        body,
        in_specs=[VMEM] * len(values) + [ANY] * len(after),
        out_specs=VMEM,
        out_shape=jax.ShapeDtypeStruct(values[0].shape, jnp.float32),
        cost_estimate=pl.CostEstimate(
            flops=int(SUM_COST), bytes_accessed=int(SUM_COST / 100), transcendentals=0
        ),
        compiler_params=pltpu.CompilerParams(vmem_limit_bytes=VMEM_BYTES),
    )(*values, *after)


def ring_shards(
    inputs_forward,
    routes_forward,
    gates_forward,
    grads_backward,
    routes_backward,
    gates_backward,
    w_gate,
    w_up,
    w_down,
    saved_gate,
    saved_up,
):
    experts, nodes = lax.axis_size("dev"), lax.axis_size("node")
    place = jnp.stack([lax.axis_index("node"), lax.axis_index("dev")]).astype(jnp.int32)
    weights = (w_gate[0, 0], w_up[0, 0], w_down[0, 0])
    stored_gate, stored_up = saved_gate[0, 0], saved_up[0, 0]

    chosen = routes_forward.shape[2]
    tokens = [inputs_forward[0]]
    grads = [
        with_info(
            grads_backward[0],
            (routes_forward[0].T, routes_backward[0].T),
            (gates_forward[0].T, gates_backward[0].T),
            (marker(),),
        )
    ]
    for _ in range(1, experts):
        tokens.append(along_ring(tokens[-1], 1))
        grads.append(along_ring(grads[-1], 1))

    count = grads_backward.shape[1]
    sent, parts = [None] * experts, [None] * experts
    acts = [None] * experts, [None] * experts
    done = []

    def exchange(own):
        arrived = [across(own[mask % len(own)], "node", mask) for mask in range(nodes - 1, 0, -1)]
        return [own[0]] + arrived[::-1]

    factors = [None] * experts

    def prepare(step):
        factors[step] = backward_factors(
            place, stored_gate, stored_up, grads[step], chosen, count, step, done[-1:]
        )
        done.append(factors[step][0])

    first_weights = [weights, CONTRACT_LAST]
    turned = [None, None]

    def turn(index):
        value = transposed(place, weights[index], done[-1:])
        done.append(value)
        return value

    def first(step, *after):
        sent[step] = first_products(
            place, tokens[step], grads[step], first_weights[0], first_weights[1], nodes, 5 if step > 1 else 3, (*done[-1:], *after)
        )
        done.append(sent[step][0])
        if step < 2:
            parts[step] = exchange(sent[step])

    def middle(step, *after):
        joint = 0 < step < experts - 1
        filled, extra = (sent[step + 1], ()) if joint else ((), (own_acts,))
        own = activations(place, parts[step], filled, (*done[-1:], *after), extra)
        done.append(own[0])
        arrived = exchange(own)
        plane = 3 if joint else 0
        acts[0][step], acts[1][step] = (arrived, plane), (arrived, plane + 1)
        if joint:
            parts[step + 1] = arrived
        else:
            acts[1][0] = (arrived, plane + 2)

    sums, hops, base = [[], []], [(), ()], [None, None]

    def last(step, kind, *after):
        shift = 1 - 2 * kind
        added = (inputs_forward[0], grads_backward[0])[kind : kind + 1] if step == 0 else ()
        if step >= 2:
            added = hops[kind]
        if kind == 0:
            value = forward_results(
                place, *acts[0][step], weights[2], grads[step], chosen, added, (*done[-1:], *after)
            )
        else:
            value = backward_results(
                place, *acts[1][step], *turned, factors[step], grads[step], chosen, added, (*done[-1:], *after)
            )
        done.append(value)
        if step == 0:
            base[kind] = from_behind(value, "section", shift)
        elif step == 1:
            sums[kind].append(along_ring_and_sections(value, -1, shift))
        elif step < experts - 1:
            hops[kind] = (along_ring(value, 1),)
        else:
            sums[kind].append(along_ring_and_sections(value, 1, shift))

    first(0)
    first_weights[:] = (*weights[:2], turn(2)), PLAIN
    first(1)
    own_acts = activations(place, parts[0], (), done[-1:])[0]
    done.append(own_acts)
    for step in range(1, experts - 1):
        if step == experts - 2:
            turned[:] = turn(0), turn(1)
        first(step + 1)
        prepare(step)
        middle(step)
        if step >= 2:
            last(step - 1, 0)
            last(step - 1, 1)
    prepare(experts - 1)
    prepare(0)
    middle(experts - 1)
    if experts > 2:
        last(experts - 2, 0)
        last(experts - 2, 1, *[values[0] for values in sums if values])
    last(experts - 1, 0)
    own_plane = first_plane(place, own_acts, (*done[-1:], *acts[0][experts - 1][0][1:]))
    done.append(own_plane)
    acts[0][0] = (exchange([own_plane]), 0)
    last(experts - 1, 1)
    last(0, 0)
    last(0, 1)
    outs = []
    for values, own in zip(sums, base):
        total = sum(value.astype(jnp.float32) for value in (sum_rows(values[-1:], (*done[-1:], *outs)), *values[:-1], own))
        outs.append(total.astype(jnp.bfloat16))
    return tuple(out[None] for out in outs)


def power_of_two(number):
    return number & (number - 1) == 0


def shards(*args):
    experts, nodes = lax.axis_size("dev"), lax.axis_size("node")
    tokens, capacity = args[0].shape[1], args[9].shape[2] // experts
    fits = tokens <= args[0].shape[2]
    if fits and capacity == tokens and experts > 1 and power_of_two(nodes) and tokens % (16 * nodes) == 0:
        return ring_shards(*args)
    return shards_by_slots(*args)


def solution(mesh):
    return jax.shard_map(
        shards,
        mesh=mesh,
        in_specs=(
            P("section", "dev", "node"),
            P("section", "dev", None),
            P("section", "dev", None),
            P("section", "dev", "node"),
            P("section", "dev", None),
            P("section", "dev", None),
            P("section", "dev", "node", None),
            P("section", "dev", "node", None),
            P("section", "dev", None, "node"),
            P("section", "dev", None, None),
            P("section", "dev", None, None),
        ),
        out_specs=(P("section", "dev", "node"), P("section", "dev", "node")),
        check_vma=False,
    )
```

```python
import functools

import jax
import jax.numpy as jnp
from jax import lax
from jax.experimental import pallas as pl
from jax.experimental.pallas import tpu as pltpu
from jax.sharding import PartitionSpec as P


def from_behind(value, axis, steps):
    count = lax.axis_size(axis)
    pairs = [(source, (source + steps) % count) for source in range(count)]
    return lax.ppermute(value, axis, pairs)


def slot_targets(routing, experts, capacity):
    flat = routing.reshape(-1)
    onehot = (flat[:, None] == jnp.arange(experts, dtype=jnp.int32)[None, :]).astype(jnp.int32)
    earlier = jnp.cumsum(onehot, axis=0) - onehot
    return flat * capacity + jnp.sum(earlier * onehot, axis=1)


def pack_rows(token_rows, targets, slot_count, chosen):
    match = (jnp.arange(slot_count, dtype=jnp.int32)[:, None] == targets[None, :]).astype(
        jnp.bfloat16
    )
    select = jnp.sum(match.reshape(slot_count, token_rows.shape[0], chosen), axis=2)
    return jnp.dot(select, token_rows, preferred_element_type=jnp.float32).astype(jnp.bfloat16)


def combine_rows(token_rows, weights_of, returned_rows, targets):
    width = token_rows.shape[1]
    picked = returned_rows.reshape(-1, width)[targets]
    picked = picked.reshape(token_rows.shape[0], weights_of.shape[1], width).astype(jnp.float32)
    mixed = token_rows.astype(jnp.float32) + jnp.sum(weights_of[:, :, None] * picked, axis=1)
    return mixed.astype(jnp.bfloat16)


def backward_act(grad_hidden, stored_gate, stored_up):
    act_gate = stored_gate.astype(jnp.float32)
    act_up = stored_up.astype(jnp.float32)
    squash = jax.nn.sigmoid(act_gate)
    grad_gate = (grad_hidden * act_up * squash * (1.0 + act_gate * (1.0 - squash))).astype(
        jnp.bfloat16
    )
    grad_up = (grad_hidden * act_gate * squash).astype(jnp.bfloat16)
    return (grad_gate, grad_up)


def shards_by_slots(
    inputs_forward,
    routes_forward,
    gates_forward,
    grads_backward,
    routes_backward,
    gates_backward,
    w_gate,
    w_up,
    w_down,
    saved_gate,
    saved_up,
):
    experts = lax.axis_size("dev")
    chosen = routes_forward.shape[2]
    token_rows = inputs_forward[0]
    grad_rows = grads_backward[0]
    slot_total = saved_gate.shape[2]
    capacity = slot_total // experts
    width = token_rows.shape[1]
    targets_forward = slot_targets(routes_forward[0], experts, capacity)
    targets_backward = slot_targets(routes_backward[0], experts, capacity)
    sent_forward = pack_rows(token_rows, targets_forward, slot_total, chosen).reshape(
        experts, capacity, width
    )
    sent_backward = pack_rows(grad_rows, targets_backward, slot_total, chosen).reshape(
        experts, capacity, width
    )
    arrived_forward, arrived_backward = (
        lax.all_to_all(sent_forward, "dev", split_axis=0, concat_axis=0, tiled=True),
        lax.all_to_all(sent_backward, "dev", split_axis=0, concat_axis=0, tiled=True),
    )
    arrived_forward = arrived_forward.reshape(slot_total, width)
    arrived_backward = arrived_backward.reshape(slot_total, width)
    gate_local = w_gate[0, 0]
    up_local = w_up[0, 0]
    down_local = w_down[0, 0]
    stored_gate = saved_gate[0, 0]
    stored_up = saved_up[0, 0]
    contract_last = (((1,), (1,)), ((), ()))
    part_gate = jnp.dot(arrived_forward, gate_local, preferred_element_type=jnp.float32)
    part_up = jnp.dot(arrived_forward, up_local, preferred_element_type=jnp.float32)
    part_grad = lax.dot_general(
        arrived_backward, down_local, contract_last, preferred_element_type=jnp.float32
    )
    gate_share, up_share = (
        lax.psum_scatter(
            part_gate.astype(jnp.bfloat16), "node", scatter_dimension=1, tiled=True
        ).astype(jnp.float32),
        lax.psum_scatter(
            part_up.astype(jnp.bfloat16), "node", scatter_dimension=1, tiled=True
        ).astype(jnp.float32),
    )
    hidden_share = (jax.nn.silu(gate_share) * up_share).astype(jnp.bfloat16)
    hidden = lax.all_gather(hidden_share, "node", axis=1, tiled=True)
    grad_hidden = lax.psum(part_grad.astype(jnp.bfloat16), "node").astype(jnp.float32)
    grad_gate, grad_up = backward_act(grad_hidden, stored_gate, stored_up)
    result_forward = jnp.dot(hidden, down_local, preferred_element_type=jnp.float32).astype(
        jnp.bfloat16
    )
    result_backward = lax.dot_general(
        grad_gate, gate_local, contract_last, preferred_element_type=jnp.float32
    )
    result_backward = result_backward + lax.dot_general(
        grad_up, up_local, contract_last, preferred_element_type=jnp.float32
    )
    result_backward = result_backward.astype(jnp.bfloat16)
    back_forward, back_backward = (
        lax.all_to_all(
            result_forward.reshape(experts, capacity, width),
            "dev",
            split_axis=0,
            concat_axis=0,
            tiled=True,
        ),
        lax.all_to_all(
            result_backward.reshape(experts, capacity, width),
            "dev",
            split_axis=0,
            concat_axis=0,
            tiled=True,
        ),
    )
    mixed_forward = combine_rows(token_rows, gates_forward[0], back_forward, targets_forward)
    mixed_backward = combine_rows(grad_rows, gates_backward[0], back_backward, targets_backward)
    next_forward = from_behind(mixed_forward[None], "section", 1)
    next_backward = from_behind(mixed_backward[None], "section", -1)
    return (next_forward, next_backward)


CONTRACT_LAST = (((1,), (1,)), ((), ()))
PLAIN = (((1,), (0,)), ((), ()))
CONTRACT_FIRST = (((0,), (0,)), ((), ()))
VMEM = pl.BlockSpec(memory_space=pltpu.VMEM)
SMEM = pl.BlockSpec(memory_space=pltpu.SMEM)
VMEM_BYTES = 14 << 20
CF = 1.0
TURN_DOWN = True
SUM_COST = 1e10
SPACE_COST = 10**10
INFO_COST = 10**6
WIDE_BYTES = 56 << 20
ANY = pl.BlockSpec(memory_space=pl.ANY)
HBM = pl.BlockSpec(memory_space=pltpu.HBM)


def across(value, axis, mask):
    count = lax.axis_size(axis)
    return lax.ppermute(value, axis, [(source, source ^ mask) for source in range(count)])


def ring_order(count):
    return [0] + list(range(1, count, 2)) + list(range(2, count, 2))[::-1]


def ring_pairs(count, steps):
    order = ring_order(count)
    return [(order[i], order[(i + steps) % count]) for i in range(count)]


def along_ring(value, steps):
    return lax.ppermute(value, "dev", ring_pairs(lax.axis_size("dev"), steps))


def along_ring_and_sections(value, steps, shift):
    count, sections = lax.axis_size("dev"), lax.axis_size("section")
    pairs = [
        (section * count + source, (section + shift) % sections * count + target)
        for section in range(sections)
        for source, target in ring_pairs(count, steps)
    ]
    return lax.ppermute(value, ("section", "dev"), pairs)


def block_behind(expert, count, steps):
    block = 0
    for target, source in ring_pairs(count, -steps):
        block = block + jnp.where(expert == target, source, 0)
    return block


def call(body, place, operands, after, out_shape, scratch, flops, aliases={}):
    def with_after(place_ref, *refs):
        body(place_ref, *refs[: len(operands)], *refs[len(operands) + len(after) :])

    touched = sum(array.size * array.dtype.itemsize for array in operands)
    return pl.pallas_call(
        with_after,
        in_specs=[SMEM] + [VMEM] * len(operands) + [ANY] * len(after),
        out_specs=jax.tree.map(lambda _: VMEM, out_shape),
        scratch_shapes=scratch,
        out_shape=out_shape,
        input_output_aliases={index + 1: out for index, out in aliases.items()},
        cost_estimate=pl.CostEstimate(flops=int(CF * flops), bytes_accessed=int(CF * touched), transcendentals=0),
        compiler_params=pltpu.CompilerParams(vmem_limit_bytes=VMEM_BYTES),
    )(place, *operands, *after)


def matmul(left, right, dims=(((1,), (0,)), ((), ()))):
    return lax.dot_general(left, right, dims, preferred_element_type=jnp.float32)


def by_owner(place_ref, rows_ref, sorted_rows, nodes):
    rows = sorted_rows.shape[0] // nodes
    for mask in range(nodes):
        first = pl.multiple_of((place_ref[0] ^ mask) * rows, rows)
        sorted_rows[mask * rows : (mask + 1) * rows, :] = rows_ref[pl.ds(first, rows), :]


def first_products(place, token_rows, grad_rows, weights, dims, nodes, planes, after):
    (count, width), hidden = token_rows.shape, weights[0].shape[1]
    share = count // nodes

    def body(place_ref, token_ref, grad_ref, gate_ref, up_ref, down_ref, *refs):
        outs, (sorted_tokens, sorted_grads) = refs[:nodes], refs[nodes:]
        by_owner(place_ref, token_ref, sorted_tokens, nodes)
        by_owner(place_ref, grad_ref, sorted_grads, nodes)
        parts = (
            matmul(sorted_tokens[...], gate_ref[...]),
            matmul(sorted_tokens[...], up_ref[...]),
            matmul(sorted_grads[...], down_ref[...], dims),
        )
        for index, part in enumerate(parts):
            for mask in range(nodes):
                outs[mask][index] = part[mask * share : (mask + 1) * share].astype(jnp.bfloat16)

    return call(
        body,
        place,
        (token_rows, grad_rows, *weights),
        after,
        [jax.ShapeDtypeStruct((planes, share, hidden), jnp.bfloat16)] * nodes,
        [pltpu.VMEM((count, width), jnp.bfloat16)] * 2,
        6 * count * width * hidden,
    )


def transposed(place, weight, after):
    def body(place_ref, weight_ref, out):
        out[...] = weight_ref[...].T

    shape = jax.ShapeDtypeStruct(weight.shape[::-1], weight.dtype)
    return call(body, place, (weight,), after, shape, [], 0)


def activations(place, pieces, filled, after, extra=()):
    nodes, (_, share, hidden) = len(pieces), pieces[0].shape

    def body(place_ref, *refs):
        piece_refs, extra_refs = refs[:nodes], refs[nodes + len(filled) :][: len(extra)]
        outs = refs[nodes + len(filled) + len(extra) :]
        gate, up, grad = (
            sum(ref[index].astype(jnp.float32) for ref in piece_refs) for index in range(3)
        )
        act = (gate / (1.0 + jnp.exp(-gate)) * up).astype(jnp.bfloat16)
        grad = grad.astype(jnp.bfloat16)
        for out in outs:
            start = 3 if filled else 0
            out[start] = act
            out[start + 1] = grad
            for index, ref in enumerate(extra_refs):
                out[start + 2 + index] = ref[1]

    shapes = [jax.ShapeDtypeStruct(array.shape, array.dtype) for array in filled]
    return call(
        body,
        place,
        (*pieces, *filled, *extra),
        after,
        shapes or [jax.ShapeDtypeStruct((2 + len(extra), share, hidden), jnp.bfloat16)],
        [],
        16 * share * hidden,
        {nodes + index: index for index in range(len(filled))},
    )


def first_plane(place, planes, after):
    def body(place_ref, planes_ref, out):
        out[0] = planes_ref[0]

    shape = (1, *planes.shape[1:])
    return call(body, place, (planes,), after, jax.ShapeDtypeStruct(shape, planes.dtype), [], 0)


def join(place_ref, piece_refs, index, joined):
    rows = piece_refs[0].shape[1]
    for mask, ref in enumerate(piece_refs):
        first = pl.multiple_of((place_ref[0] ^ mask) * rows, rows)
        joined[pl.ds(first, rows), :] = ref[index]


def copied(sources, targets, sems):
    copies = [
        pltpu.make_async_copy(source, target, sems.at[index])
        for index, (source, target) in enumerate(zip(sources, targets))
    ]
    for copy in copies:
        copy.start()
    return copies


def with_info(rows, routes, gates, after):
    (count, width), chosen = rows.shape, routes[0].shape[0]
    height = -(-6 * chosen // 16) * 16
    small = (*routes, *gates)

    def body(rows_ref, *refs):
        infos, out = refs[:4], refs[-1]
        lines = [ref[...].astype(jnp.float32) for ref in infos[:2]]
        for ref in infos[2:]:
            coarse = ref[...].astype(jnp.bfloat16).astype(jnp.float32)
            lines += [coarse, ref[...] - coarse]
        lines.append(jnp.zeros((height - 6 * chosen, count), jnp.float32))
        out[0:count, :] = rows_ref[...]
        out[count:, :] = jnp.zeros((height, width), jnp.bfloat16)
        out[count:, 0:count] = jnp.concatenate(lines).astype(jnp.bfloat16)

    return pl.pallas_call(
        body,
        in_specs=[VMEM] * 5 + [ANY] * len(after),
        out_specs=VMEM,
        out_shape=jax.ShapeDtypeStruct((count + height, width), jnp.bfloat16),
        cost_estimate=pl.CostEstimate(flops=INFO_COST, bytes_accessed=INFO_COST // 100, transcendentals=0),
        compiler_params=pltpu.CompilerParams(vmem_limit_bytes=4 << 20),
    )(rows, *small, *after)


def marker():
    def body(out):
        out[...] = jnp.zeros_like(out)

    return pl.pallas_call(
        body,
        out_specs=VMEM,
        out_shape=jax.ShapeDtypeStruct((8, 128), jnp.float32),
        cost_estimate=pl.CostEstimate(flops=SPACE_COST, bytes_accessed=SPACE_COST // 100, transcendentals=0),
        compiler_params=pltpu.CompilerParams(vmem_limit_bytes=1 << 20),
    )()


def opening_products(place, token_rows, grad_rows, weights, nodes):
    (count, width), hidden = grad_rows.shape, weights[0].shape[1]
    share = count // nodes
    operands = (token_rows, weights[0], weights[1], grad_rows, weights[2])
    cuts = 4

    def body(place_ref, *refs):
        inputs, pieces, held = refs[:5], refs[5 : 5 + nodes], refs[5 + nodes : 10 + nodes]
        sorted_rows, sems = refs[10 + nodes :]

        def pieces_of(ref):
            rows = ref.shape[0] // cuts
            return [ref.at[pl.ds(cut * rows, rows)] for cut in range(cuts)]

        parts = [
            copied(pieces_of(source), pieces_of(target), sems.at[index])
            for index, (source, target) in enumerate(zip(inputs, held))
        ]

        def wait(index):
            for copy in parts[index]:
                copy.wait()

        def give(index, part):
            for mask in range(nodes):
                pieces[mask][index] = part[mask * share : (mask + 1) * share].astype(jnp.bfloat16)

        wait(0)
        by_owner(place_ref, held[0], sorted_rows, nodes)
        for index in (0, 1):
            wait(index + 1)
            give(index, matmul(sorted_rows[...], held[index + 1][...]))
        wait(3)
        by_owner(place_ref, held[3], sorted_rows, nodes)
        wait(4)
        give(2, matmul(sorted_rows[...], held[4][...], CONTRACT_LAST))

    return pl.pallas_call(
        body,
        in_specs=[SMEM] + [HBM] * 5,
        out_specs=[VMEM] * nodes,
        out_shape=[jax.ShapeDtypeStruct((3, share, hidden), jnp.bfloat16)] * nodes,
        scratch_shapes=[pltpu.VMEM(value.shape, value.dtype) for value in operands]
        + [pltpu.VMEM((count, width), jnp.bfloat16), pltpu.SemaphoreType.DMA((5, cuts))],
        cost_estimate=pl.CostEstimate(
            flops=int(CF * 6 * count * width * hidden),
            bytes_accessed=int(CF * 6 * width * hidden),
            transcendentals=0,
        ),
        compiler_params=pltpu.CompilerParams(vmem_limit_bytes=WIDE_BYTES),
    )(place, *operands)


def info_of(ref, count, chosen, which):
    lines = ref[count:, 0:count].astype(jnp.float32)
    routes = lines[which * chosen : (which + 1) * chosen].astype(jnp.int32)
    first = 2 * (which + 1) * chosen
    return routes, lines[first : first + chosen] + lines[first + chosen : first + 2 * chosen]


def weight_column(expert, routes, gates):
    chosen, count = routes.shape
    line = jnp.zeros((1, count), jnp.float32)
    for choice in range(chosen):
        line += jnp.where(routes[choice : choice + 1] == expert, gates[choice : choice + 1], 0.0)
    diagonal = lax.broadcasted_iota(jnp.int32, (count, count), 0) == lax.broadcasted_iota(
        jnp.int32, (count, count), 1
    )
    return jnp.sum(jnp.where(diagonal, line, 0.0), axis=1, keepdims=True)


def slot_selection(expert, routes, capacity):
    chosen, count = routes.shape
    named = jnp.zeros((1, count), jnp.float32)
    for choice in range(chosen):
        named += (routes[choice : choice + 1] == expert).astype(jnp.float32)
    earlier = lax.broadcasted_iota(jnp.int32, (count, count), 0) < lax.broadcasted_iota(
        jnp.int32, (count, count), 1
    )
    rank = matmul(
        jnp.broadcast_to(named, (16, count)).astype(jnp.bfloat16),
        earlier.astype(jnp.float32).astype(jnp.bfloat16),
    )[0:1]
    slot = jnp.where(named > 0, rank, -1.0)
    slots = lax.broadcasted_iota(jnp.int32, (capacity, count), 0).astype(jnp.float32)
    return (slots == slot).astype(jnp.float32).astype(jnp.bfloat16)


def give(out, weight, result, added_refs):
    total = weight * result.astype(jnp.bfloat16).astype(jnp.float32)
    for ref in added_refs:
        total += ref[0 : out.shape[0], :].astype(jnp.float32)
    out[...] = total.astype(jnp.bfloat16)


def forward_results(place, pieces, plane, w_down, info, chosen, added, after):
    nodes, (_, share, hidden), width = len(pieces), pieces[0].shape, w_down.shape[1]
    count = share * nodes

    def body(place_ref, *refs):
        piece_refs, refs = refs[:nodes], refs[nodes:]
        (down_ref, info_ref), added_refs, (out, joined) = refs[:2], refs[2:-2], refs[-2:]
        join(place_ref, piece_refs, plane, joined)
        weight = weight_column(place_ref[1], *info_of(info_ref, count, chosen, 0))
        give(out, weight, matmul(joined[...], down_ref[...]), added_refs)

    return call(
        body,
        place,
        (*pieces, w_down, info, *added),
        after,
        jax.ShapeDtypeStruct((count, width), jnp.bfloat16),
        [pltpu.VMEM((count, hidden), jnp.bfloat16)],
        2 * count * width * hidden,
    )


def backward_factors(place, saved_gate, saved_up, info, chosen, count, block, after):
    slots, hidden = saved_gate.shape
    experts = slots // count

    def body(place_ref, saved_gate_ref, saved_up_ref, info_ref, gate_out, up_out):
        routes, _ = info_of(info_ref, count, chosen, 1)
        select = slot_selection(place_ref[1], routes, count)
        first = pl.multiple_of(block_behind(place_ref[1], experts, block) * count, count)
        act_gate = matmul(select, saved_gate_ref[pl.ds(first, count), :], CONTRACT_FIRST)
        act_up = matmul(select, saved_up_ref[pl.ds(first, count), :], CONTRACT_FIRST)
        squash = 1.0 / (1.0 + jnp.exp(-act_gate))
        gate_out[...] = act_up * squash * (1.0 + act_gate * (1.0 - squash))
        up_out[...] = act_gate * squash

    return call(
        body,
        place,
        (saved_gate, saved_up, info),
        after,
        [jax.ShapeDtypeStruct((count, hidden), jnp.float32)] * 2,
        [],
        4 * count * count * hidden,
    )


def backward_results(place, pieces, plane, w_gate, w_up, factors, info, chosen, added, after):
    nodes, (_, share, hidden), width = len(pieces), pieces[0].shape, w_gate.shape[1]
    count = share * nodes

    def body(place_ref, *refs):
        piece_refs, refs = refs[:nodes], refs[nodes:]
        gate_ref, up_ref, gate_factor, up_factor, info_ref = refs[:5]
        added_refs, (out, joined) = refs[5:-2], refs[-2:]
        join(place_ref, piece_refs, plane, joined)
        weight = weight_column(place_ref[1], *info_of(info_ref, count, chosen, 1))
        grad_hidden = joined[...].astype(jnp.float32)
        grad_gate = (grad_hidden * gate_factor[...]).astype(jnp.bfloat16)
        grad_up = (grad_hidden * up_factor[...]).astype(jnp.bfloat16)
        result = matmul(grad_gate, gate_ref[...])
        result += matmul(grad_up, up_ref[...])
        give(out, weight, result, added_refs)

    return call(
        body,
        place,
        (*pieces, w_gate, w_up, *factors, info, *added),
        after,
        jax.ShapeDtypeStruct((count, width), jnp.bfloat16),
        [pltpu.VMEM((count, hidden), jnp.bfloat16)],
        4 * count * width * hidden,
    )


def sum_rows(values, after):
    def body(*refs):
        total = sum(ref[...].astype(jnp.float32) for ref in refs[: len(values)])
        refs[-1][...] = total

    return pl.pallas_call(
        body,
        in_specs=[VMEM] * len(values) + [ANY] * len(after),
        out_specs=VMEM,
        out_shape=jax.ShapeDtypeStruct(values[0].shape, jnp.float32),
        cost_estimate=pl.CostEstimate(
            flops=int(SUM_COST), bytes_accessed=int(SUM_COST / 100), transcendentals=0
        ),
        compiler_params=pltpu.CompilerParams(vmem_limit_bytes=VMEM_BYTES),
    )(*values, *after)


def ring_shards(
    inputs_forward,
    routes_forward,
    gates_forward,
    grads_backward,
    routes_backward,
    gates_backward,
    w_gate,
    w_up,
    w_down,
    saved_gate,
    saved_up,
):
    experts, nodes = lax.axis_size("dev"), lax.axis_size("node")
    place = jnp.stack([lax.axis_index("node"), lax.axis_index("dev")]).astype(jnp.int32)
    weights = (w_gate[0, 0], w_up[0, 0], w_down[0, 0])
    stored_gate, stored_up = saved_gate[0, 0], saved_up[0, 0]

    chosen = routes_forward.shape[2]
    tokens = [inputs_forward[0]]
    grads = [
        with_info(
            grads_backward[0],
            (routes_forward[0].T, routes_backward[0].T),
            (gates_forward[0].T, gates_backward[0].T),
            (marker(),),
        )
    ]
    for _ in range(1, experts):
        tokens.append(along_ring(tokens[-1], 1))
        grads.append(along_ring(grads[-1], 1))

    count = grads_backward.shape[1]
    sent, parts = [None] * experts, [None] * experts
    acts = [None] * experts, [None] * experts
    done = []

    def exchange(own):
        arrived = [across(own[mask % len(own)], "node", mask) for mask in range(nodes - 1, 0, -1)]
        return [own[0]] + arrived[::-1]

    factors = [None] * experts

    def prepare(step):
        factors[step] = backward_factors(
            place, stored_gate, stored_up, grads[step], chosen, count, step, done[-1:]
        )
        done.append(factors[step][0])

    first_weights = [weights, CONTRACT_LAST]
    turned = [None, None]

    def turn(index):
        value = transposed(place, weights[index], done[-1:])
        done.append(value)
        return value

    def first(step, *after):
        sent[step] = first_products(
            place, tokens[step], grads[step], first_weights[0], first_weights[1], nodes, 5 if step > 1 else 3, (*done[-1:], *after)
        )
        done.append(sent[step][0])
        if step < 2:
            parts[step] = exchange(sent[step])

    def middle(step, *after):
        joint = 0 < step < experts - 1
        filled, extra = (sent[step + 1], ()) if joint else ((), (own_acts,))
        own = activations(place, parts[step], filled, (*done[-1:], *after), extra)
        done.append(own[0])
        arrived = exchange(own)
        plane = 3 if joint else 0
        acts[0][step], acts[1][step] = (arrived, plane), (arrived, plane + 1)
        if joint:
            parts[step + 1] = arrived
        else:
            acts[1][0] = (arrived, plane + 2)

    sums, hops, base = [[], []], [(), ()], [None, None]

    def last(step, kind, *after):
        shift = 1 - 2 * kind
        added = (inputs_forward[0], grads_backward[0])[kind : kind + 1] if step == 0 else ()
        if step >= 2:
            added = hops[kind]
        if kind == 0:
            value = forward_results(
                place, *acts[0][step], weights[2], grads[step], chosen, added, (*done[-1:], *after)
            )
        else:
            value = backward_results(
                place, *acts[1][step], *turned, factors[step], grads[step], chosen, added, (*done[-1:], *after)
            )
        done.append(value)
        if step == 0:
            base[kind] = from_behind(value, "section", shift)
        elif step == 1:
            sums[kind].append(along_ring_and_sections(value, -1, shift))
        elif step < experts - 1:
            hops[kind] = (along_ring(value, 1),)
        else:
            sums[kind].append(along_ring_and_sections(value, 1, shift))

    first(0)
    if TURN_DOWN:
        first_weights[:] = (*weights[:2], turn(2)), PLAIN
    first(1)
    own_acts = activations(place, parts[0], (), done[-1:])[0]
    done.append(own_acts)
    for step in range(1, experts - 1):
        first(step + 1)
        prepare(step)
        if step == experts - 2:
            turned[:] = turn(0), turn(1)
        middle(step)
        if step >= 2:
            last(step - 1, 0)
            last(step - 1, 1)
    prepare(experts - 1)
    prepare(0)
    middle(experts - 1)
    if experts > 2:
        last(experts - 2, 0)
        last(experts - 2, 1, *[values[0] for values in sums if values])
    last(experts - 1, 0)
    own_plane = first_plane(place, own_acts, (*done[-1:], *acts[0][experts - 1][0][1:]))
    done.append(own_plane)
    acts[0][0] = (exchange([own_plane]), 0)
    last(experts - 1, 1)
    last(0, 1)
    last(0, 0)
    outs = []
    for values, own in zip(sums, base):
        total = sum(value.astype(jnp.float32) for value in (sum_rows(values[-1:], (*done[-1:], *outs)), *values[:-1], own))
        outs.append(total.astype(jnp.bfloat16))
    return tuple(out[None] for out in outs)


def power_of_two(number):
    return number & (number - 1) == 0


def shards(*args):
    experts, nodes = lax.axis_size("dev"), lax.axis_size("node")
    tokens, capacity = args[0].shape[1], args[9].shape[2] // experts
    if capacity == tokens and experts > 1 and power_of_two(nodes) and tokens % (16 * nodes) == 0:
        return ring_shards(*args)
    return shards_by_slots(*args)


def solution(mesh):
    return jax.shard_map(
        shards,
        mesh=mesh,
        in_specs=(
            P("section", "dev", "node"),
            P("section", "dev", None),
            P("section", "dev", None),
            P("section", "dev", "node"),
            P("section", "dev", None),
            P("section", "dev", None),
            P("section", "dev", "node", None),
            P("section", "dev", "node", None),
            P("section", "dev", None, "node"),
            P("section", "dev", None, None),
            P("section", "dev", None, None),
        ),
        out_specs=(P("section", "dev", "node"), P("section", "dev", "node")),
        check_vma=False,
    )
```

```python
import functools

import jax
import jax.numpy as jnp
from jax import lax
from jax.experimental import pallas as pl
from jax.experimental.pallas import tpu as pltpu
from jax.sharding import PartitionSpec as P


def from_behind(value, axis, steps):
    count = lax.axis_size(axis)
    pairs = [(source, (source + steps) % count) for source in range(count)]
    return lax.ppermute(value, axis, pairs)


def slot_targets(routing, experts, capacity):
    flat = routing.reshape(-1)
    onehot = (flat[:, None] == jnp.arange(experts, dtype=jnp.int32)[None, :]).astype(jnp.int32)
    earlier = jnp.cumsum(onehot, axis=0) - onehot
    return flat * capacity + jnp.sum(earlier * onehot, axis=1)


def pack_rows(token_rows, targets, slot_count, chosen):
    match = (jnp.arange(slot_count, dtype=jnp.int32)[:, None] == targets[None, :]).astype(
        jnp.bfloat16
    )
    select = jnp.sum(match.reshape(slot_count, token_rows.shape[0], chosen), axis=2)
    return jnp.dot(select, token_rows, preferred_element_type=jnp.float32).astype(jnp.bfloat16)


def combine_rows(token_rows, weights_of, returned_rows, targets):
    width = token_rows.shape[1]
    picked = returned_rows.reshape(-1, width)[targets]
    picked = picked.reshape(token_rows.shape[0], weights_of.shape[1], width).astype(jnp.float32)
    mixed = token_rows.astype(jnp.float32) + jnp.sum(weights_of[:, :, None] * picked, axis=1)
    return mixed.astype(jnp.bfloat16)


def backward_act(grad_hidden, stored_gate, stored_up):
    act_gate = stored_gate.astype(jnp.float32)
    act_up = stored_up.astype(jnp.float32)
    squash = jax.nn.sigmoid(act_gate)
    grad_gate = (grad_hidden * act_up * squash * (1.0 + act_gate * (1.0 - squash))).astype(
        jnp.bfloat16
    )
    grad_up = (grad_hidden * act_gate * squash).astype(jnp.bfloat16)
    return (grad_gate, grad_up)


def shards_by_slots(
    inputs_forward,
    routes_forward,
    gates_forward,
    grads_backward,
    routes_backward,
    gates_backward,
    w_gate,
    w_up,
    w_down,
    saved_gate,
    saved_up,
):
    experts = lax.axis_size("dev")
    chosen = routes_forward.shape[2]
    token_rows = inputs_forward[0]
    grad_rows = grads_backward[0]
    slot_total = saved_gate.shape[2]
    capacity = slot_total // experts
    width = token_rows.shape[1]
    targets_forward = slot_targets(routes_forward[0], experts, capacity)
    targets_backward = slot_targets(routes_backward[0], experts, capacity)
    sent_forward = pack_rows(token_rows, targets_forward, slot_total, chosen).reshape(
        experts, capacity, width
    )
    sent_backward = pack_rows(grad_rows, targets_backward, slot_total, chosen).reshape(
        experts, capacity, width
    )
    arrived_forward, arrived_backward = (
        lax.all_to_all(sent_forward, "dev", split_axis=0, concat_axis=0, tiled=True),
        lax.all_to_all(sent_backward, "dev", split_axis=0, concat_axis=0, tiled=True),
    )
    arrived_forward = arrived_forward.reshape(slot_total, width)
    arrived_backward = arrived_backward.reshape(slot_total, width)
    gate_local = w_gate[0, 0]
    up_local = w_up[0, 0]
    down_local = w_down[0, 0]
    stored_gate = saved_gate[0, 0]
    stored_up = saved_up[0, 0]
    contract_last = (((1,), (1,)), ((), ()))
    part_gate = jnp.dot(arrived_forward, gate_local, preferred_element_type=jnp.float32)
    part_up = jnp.dot(arrived_forward, up_local, preferred_element_type=jnp.float32)
    part_grad = lax.dot_general(
        arrived_backward, down_local, contract_last, preferred_element_type=jnp.float32
    )
    gate_share, up_share = (
        lax.psum_scatter(
            part_gate.astype(jnp.bfloat16), "node", scatter_dimension=1, tiled=True
        ).astype(jnp.float32),
        lax.psum_scatter(
            part_up.astype(jnp.bfloat16), "node", scatter_dimension=1, tiled=True
        ).astype(jnp.float32),
    )
    hidden_share = (jax.nn.silu(gate_share) * up_share).astype(jnp.bfloat16)
    hidden = lax.all_gather(hidden_share, "node", axis=1, tiled=True)
    grad_hidden = lax.psum(part_grad.astype(jnp.bfloat16), "node").astype(jnp.float32)
    grad_gate, grad_up = backward_act(grad_hidden, stored_gate, stored_up)
    result_forward = jnp.dot(hidden, down_local, preferred_element_type=jnp.float32).astype(
        jnp.bfloat16
    )
    result_backward = lax.dot_general(
        grad_gate, gate_local, contract_last, preferred_element_type=jnp.float32
    )
    result_backward = result_backward + lax.dot_general(
        grad_up, up_local, contract_last, preferred_element_type=jnp.float32
    )
    result_backward = result_backward.astype(jnp.bfloat16)
    back_forward, back_backward = (
        lax.all_to_all(
            result_forward.reshape(experts, capacity, width),
            "dev",
            split_axis=0,
            concat_axis=0,
            tiled=True,
        ),
        lax.all_to_all(
            result_backward.reshape(experts, capacity, width),
            "dev",
            split_axis=0,
            concat_axis=0,
            tiled=True,
        ),
    )
    mixed_forward = combine_rows(token_rows, gates_forward[0], back_forward, targets_forward)
    mixed_backward = combine_rows(grad_rows, gates_backward[0], back_backward, targets_backward)
    next_forward = from_behind(mixed_forward[None], "section", 1)
    next_backward = from_behind(mixed_backward[None], "section", -1)
    return (next_forward, next_backward)


CONTRACT_LAST = (((1,), (1,)), ((), ()))
PLAIN = (((1,), (0,)), ((), ()))
CONTRACT_FIRST = (((0,), (0,)), ((), ()))
VMEM = pl.BlockSpec(memory_space=pltpu.VMEM)
SMEM = pl.BlockSpec(memory_space=pltpu.SMEM)
VMEM_BYTES = 14 << 20
CF = 1.0
TURN_DOWN = True
SUM_COST = 1e10
SPACE_COST = 10**10
INFO_COST = 10**6
WIDE_BYTES = 56 << 20
ANY = pl.BlockSpec(memory_space=pl.ANY)
HBM = pl.BlockSpec(memory_space=pltpu.HBM)


def across(value, axis, mask):
    count = lax.axis_size(axis)
    return lax.ppermute(value, axis, [(source, source ^ mask) for source in range(count)])


def ring_order(count):
    return [0] + list(range(1, count, 2)) + list(range(2, count, 2))[::-1]


def ring_pairs(count, steps):
    order = ring_order(count)
    return [(order[i], order[(i + steps) % count]) for i in range(count)]


def along_ring(value, steps):
    return lax.ppermute(value, "dev", ring_pairs(lax.axis_size("dev"), steps))


def along_ring_and_sections(value, steps, shift):
    count, sections = lax.axis_size("dev"), lax.axis_size("section")
    pairs = [
        (section * count + source, (section + shift) % sections * count + target)
        for section in range(sections)
        for source, target in ring_pairs(count, steps)
    ]
    return lax.ppermute(value, ("section", "dev"), pairs)


def block_behind(expert, count, steps):
    block = 0
    for target, source in ring_pairs(count, -steps):
        block = block + jnp.where(expert == target, source, 0)
    return block


def call(body, place, operands, after, out_shape, scratch, flops, aliases={}):
    def with_after(place_ref, *refs):
        body(place_ref, *refs[: len(operands)], *refs[len(operands) + len(after) :])

    touched = sum(array.size * array.dtype.itemsize for array in operands)
    return pl.pallas_call(
        with_after,
        in_specs=[SMEM] + [VMEM] * len(operands) + [ANY] * len(after),
        out_specs=jax.tree.map(lambda _: VMEM, out_shape),
        scratch_shapes=scratch,
        out_shape=out_shape,
        input_output_aliases={index + 1: out for index, out in aliases.items()},
        cost_estimate=pl.CostEstimate(flops=int(CF * flops), bytes_accessed=int(CF * touched), transcendentals=0),
        compiler_params=pltpu.CompilerParams(vmem_limit_bytes=VMEM_BYTES),
    )(place, *operands, *after)


def matmul(left, right, dims=(((1,), (0,)), ((), ()))):
    return lax.dot_general(left, right, dims, preferred_element_type=jnp.float32)


def by_owner(place_ref, rows_ref, sorted_rows, nodes):
    rows = sorted_rows.shape[0] // nodes
    for mask in range(nodes):
        first = pl.multiple_of((place_ref[0] ^ mask) * rows, rows)
        sorted_rows[mask * rows : (mask + 1) * rows, :] = rows_ref[pl.ds(first, rows), :]


def first_products(place, token_rows, grad_rows, weights, dims, nodes, planes, after):
    (count, width), hidden = token_rows.shape, weights[0].shape[1]
    share = count // nodes

    def body(place_ref, token_ref, grad_ref, gate_ref, up_ref, down_ref, *refs):
        outs, (sorted_tokens, sorted_grads) = refs[:nodes], refs[nodes:]
        by_owner(place_ref, token_ref, sorted_tokens, nodes)
        by_owner(place_ref, grad_ref, sorted_grads, nodes)
        parts = (
            matmul(sorted_tokens[...], gate_ref[...]),
            matmul(sorted_tokens[...], up_ref[...]),
            matmul(sorted_grads[...], down_ref[...], dims),
        )
        for index, part in enumerate(parts):
            for mask in range(nodes):
                outs[mask][index] = part[mask * share : (mask + 1) * share].astype(jnp.bfloat16)

    return call(
        body,
        place,
        (token_rows, grad_rows, *weights),
        after,
        [jax.ShapeDtypeStruct((planes, share, hidden), jnp.bfloat16)] * nodes,
        [pltpu.VMEM((count, width), jnp.bfloat16)] * 2,
        6 * count * width * hidden,
    )


def transposed(place, weight, after):
    def body(place_ref, weight_ref, out):
        out[...] = weight_ref[...].T

    shape = jax.ShapeDtypeStruct(weight.shape[::-1], weight.dtype)
    return call(body, place, (weight,), after, shape, [], 0)


def activations(place, pieces, filled, after, extra=()):
    nodes, (_, share, hidden) = len(pieces), pieces[0].shape

    def body(place_ref, *refs):
        piece_refs, extra_refs = refs[:nodes], refs[nodes + len(filled) :][: len(extra)]
        outs = refs[nodes + len(filled) + len(extra) :]
        gate, up, grad = (
            sum(ref[index].astype(jnp.float32) for ref in piece_refs) for index in range(3)
        )
        act = (gate / (1.0 + jnp.exp(-gate)) * up).astype(jnp.bfloat16)
        grad = grad.astype(jnp.bfloat16)
        for out in outs:
            start = 3 if filled else 0
            out[start] = act
            out[start + 1] = grad
            for index, ref in enumerate(extra_refs):
                out[start + 2 + index] = ref[1]

    shapes = [jax.ShapeDtypeStruct(array.shape, array.dtype) for array in filled]
    return call(
        body,
        place,
        (*pieces, *filled, *extra),
        after,
        shapes or [jax.ShapeDtypeStruct((2 + len(extra), share, hidden), jnp.bfloat16)],
        [],
        16 * share * hidden,
        {nodes + index: index for index in range(len(filled))},
    )


def first_plane(place, planes, after):
    def body(place_ref, planes_ref, out):
        out[0] = planes_ref[0]

    shape = (1, *planes.shape[1:])
    return call(body, place, (planes,), after, jax.ShapeDtypeStruct(shape, planes.dtype), [], 0)


def join(place_ref, piece_refs, index, joined):
    rows = piece_refs[0].shape[1]
    for mask, ref in enumerate(piece_refs):
        first = pl.multiple_of((place_ref[0] ^ mask) * rows, rows)
        joined[pl.ds(first, rows), :] = ref[index]


def copied(sources, targets, sems):
    copies = [
        pltpu.make_async_copy(source, target, sems.at[index])
        for index, (source, target) in enumerate(zip(sources, targets))
    ]
    for copy in copies:
        copy.start()
    return copies


def with_info(rows, routes, gates, after):
    (count, width), chosen = rows.shape, routes[0].shape[0]
    height = -(-6 * chosen // 16) * 16
    small = (*routes, *gates)

    def body(rows_ref, *refs):
        infos, out = refs[:4], refs[-1]
        lines = [ref[...].astype(jnp.float32) for ref in infos[:2]]
        for ref in infos[2:]:
            coarse = ref[...].astype(jnp.bfloat16).astype(jnp.float32)
            lines += [coarse, ref[...] - coarse]
        lines.append(jnp.zeros((height - 6 * chosen, count), jnp.float32))
        out[0:count, :] = rows_ref[...]
        out[count:, :] = jnp.zeros((height, width), jnp.bfloat16)
        out[count:, 0:count] = jnp.concatenate(lines).astype(jnp.bfloat16)

    return pl.pallas_call(
        body,
        in_specs=[VMEM] * 5 + [ANY] * len(after),
        out_specs=VMEM,
        out_shape=jax.ShapeDtypeStruct((count + height, width), jnp.bfloat16),
        cost_estimate=pl.CostEstimate(flops=INFO_COST, bytes_accessed=INFO_COST // 100, transcendentals=0),
        compiler_params=pltpu.CompilerParams(vmem_limit_bytes=4 << 20),
    )(rows, *small, *after)


def marker():
    def body(out):
        out[...] = jnp.zeros_like(out)

    return pl.pallas_call(
        body,
        out_specs=VMEM,
        out_shape=jax.ShapeDtypeStruct((8, 128), jnp.float32),
        cost_estimate=pl.CostEstimate(flops=SPACE_COST, bytes_accessed=SPACE_COST // 100, transcendentals=0),
        compiler_params=pltpu.CompilerParams(vmem_limit_bytes=1 << 20),
    )()


def opening_products(place, token_rows, grad_rows, weights, nodes):
    (count, width), hidden = grad_rows.shape, weights[0].shape[1]
    share = count // nodes
    operands = (token_rows, weights[0], weights[1], grad_rows, weights[2])
    cuts = 4

    def body(place_ref, *refs):
        inputs, pieces, held = refs[:5], refs[5 : 5 + nodes], refs[5 + nodes : 10 + nodes]
        sorted_rows, sems = refs[10 + nodes :]

        def pieces_of(ref):
            rows = ref.shape[0] // cuts
            return [ref.at[pl.ds(cut * rows, rows)] for cut in range(cuts)]

        parts = [
            copied(pieces_of(source), pieces_of(target), sems.at[index])
            for index, (source, target) in enumerate(zip(inputs, held))
        ]

        def wait(index):
            for copy in parts[index]:
                copy.wait()

        def give(index, part):
            for mask in range(nodes):
                pieces[mask][index] = part[mask * share : (mask + 1) * share].astype(jnp.bfloat16)

        wait(0)
        by_owner(place_ref, held[0], sorted_rows, nodes)
        for index in (0, 1):
            wait(index + 1)
            give(index, matmul(sorted_rows[...], held[index + 1][...]))
        wait(3)
        by_owner(place_ref, held[3], sorted_rows, nodes)
        wait(4)
        give(2, matmul(sorted_rows[...], held[4][...], CONTRACT_LAST))

    return pl.pallas_call(
        body,
        in_specs=[SMEM] + [HBM] * 5,
        out_specs=[VMEM] * nodes,
        out_shape=[jax.ShapeDtypeStruct((3, share, hidden), jnp.bfloat16)] * nodes,
        scratch_shapes=[pltpu.VMEM(value.shape, value.dtype) for value in operands]
        + [pltpu.VMEM((count, width), jnp.bfloat16), pltpu.SemaphoreType.DMA((5, cuts))],
        cost_estimate=pl.CostEstimate(
            flops=int(CF * 6 * count * width * hidden),
            bytes_accessed=int(CF * 6 * width * hidden),
            transcendentals=0,
        ),
        compiler_params=pltpu.CompilerParams(vmem_limit_bytes=WIDE_BYTES),
    )(place, *operands)


def info_of(ref, count, chosen, which):
    lines = ref[count:, 0:count].astype(jnp.float32)
    routes = lines[which * chosen : (which + 1) * chosen].astype(jnp.int32)
    first = 2 * (which + 1) * chosen
    return routes, lines[first : first + chosen] + lines[first + chosen : first + 2 * chosen]


def weight_column(expert, routes, gates):
    chosen, count = routes.shape
    line = jnp.zeros((1, count), jnp.float32)
    for choice in range(chosen):
        line += jnp.where(routes[choice : choice + 1] == expert, gates[choice : choice + 1], 0.0)
    diagonal = lax.broadcasted_iota(jnp.int32, (count, count), 0) == lax.broadcasted_iota(
        jnp.int32, (count, count), 1
    )
    return jnp.sum(jnp.where(diagonal, line, 0.0), axis=1, keepdims=True)


def slot_selection(expert, routes, capacity):
    chosen, count = routes.shape
    named = jnp.zeros((1, count), jnp.float32)
    for choice in range(chosen):
        named += (routes[choice : choice + 1] == expert).astype(jnp.float32)
    earlier = lax.broadcasted_iota(jnp.int32, (count, count), 0) < lax.broadcasted_iota(
        jnp.int32, (count, count), 1
    )
    rank = matmul(
        jnp.broadcast_to(named, (16, count)).astype(jnp.bfloat16),
        earlier.astype(jnp.float32).astype(jnp.bfloat16),
    )[0:1]
    slot = jnp.where(named > 0, rank, -1.0)
    slots = lax.broadcasted_iota(jnp.int32, (capacity, count), 0).astype(jnp.float32)
    return (slots == slot).astype(jnp.float32).astype(jnp.bfloat16)


def give(out, weight, result, added_refs):
    total = weight * result.astype(jnp.bfloat16).astype(jnp.float32)
    for ref in added_refs:
        total += ref[0 : out.shape[0], :].astype(jnp.float32)
    out[...] = total.astype(jnp.bfloat16)


def forward_results(place, pieces, plane, w_down, info, chosen, added, after):
    nodes, (_, share, hidden), width = len(pieces), pieces[0].shape, w_down.shape[1]
    count = share * nodes

    def body(place_ref, *refs):
        piece_refs, refs = refs[:nodes], refs[nodes:]
        (down_ref, info_ref), added_refs, (out, joined) = refs[:2], refs[2:-2], refs[-2:]
        join(place_ref, piece_refs, plane, joined)
        weight = weight_column(place_ref[1], *info_of(info_ref, count, chosen, 0))
        give(out, weight, matmul(joined[...], down_ref[...]), added_refs)

    return call(
        body,
        place,
        (*pieces, w_down, info, *added),
        after,
        jax.ShapeDtypeStruct((count, width), jnp.bfloat16),
        [pltpu.VMEM((count, hidden), jnp.bfloat16)],
        2 * count * width * hidden,
    )


def backward_factors(place, saved_gate, saved_up, info, chosen, count, block, after):
    slots, hidden = saved_gate.shape
    experts = slots // count

    def body(place_ref, saved_gate_ref, saved_up_ref, info_ref, gate_out, up_out):
        routes, _ = info_of(info_ref, count, chosen, 1)
        select = slot_selection(place_ref[1], routes, count)
        first = pl.multiple_of(block_behind(place_ref[1], experts, block) * count, count)
        act_gate = matmul(select, saved_gate_ref[pl.ds(first, count), :], CONTRACT_FIRST)
        act_up = matmul(select, saved_up_ref[pl.ds(first, count), :], CONTRACT_FIRST)
        squash = 1.0 / (1.0 + jnp.exp(-act_gate))
        gate_out[...] = act_up * squash * (1.0 + act_gate * (1.0 - squash))
        up_out[...] = act_gate * squash

    return call(
        body,
        place,
        (saved_gate, saved_up, info),
        after,
        [jax.ShapeDtypeStruct((count, hidden), jnp.float32)] * 2,
        [],
        4 * count * count * hidden,
    )


def backward_results(place, pieces, plane, w_gate, w_up, factors, info, chosen, added, after):
    nodes, (_, share, hidden), width = len(pieces), pieces[0].shape, w_gate.shape[1]
    count = share * nodes

    def body(place_ref, *refs):
        piece_refs, refs = refs[:nodes], refs[nodes:]
        gate_ref, up_ref, gate_factor, up_factor, info_ref = refs[:5]
        added_refs, (out, joined) = refs[5:-2], refs[-2:]
        join(place_ref, piece_refs, plane, joined)
        weight = weight_column(place_ref[1], *info_of(info_ref, count, chosen, 1))
        grad_hidden = joined[...].astype(jnp.float32)
        grad_gate = (grad_hidden * gate_factor[...]).astype(jnp.bfloat16)
        grad_up = (grad_hidden * up_factor[...]).astype(jnp.bfloat16)
        result = matmul(grad_gate, gate_ref[...])
        result += matmul(grad_up, up_ref[...])
        give(out, weight, result, added_refs)

    return call(
        body,
        place,
        (*pieces, w_gate, w_up, *factors, info, *added),
        after,
        jax.ShapeDtypeStruct((count, width), jnp.bfloat16),
        [pltpu.VMEM((count, hidden), jnp.bfloat16)],
        4 * count * width * hidden,
    )


def sum_rows(values, after):
    def body(*refs):
        total = sum(ref[...].astype(jnp.float32) for ref in refs[: len(values)])
        refs[-1][...] = total

    return pl.pallas_call(
        body,
        in_specs=[VMEM] * len(values) + [ANY] * len(after),
        out_specs=VMEM,
        out_shape=jax.ShapeDtypeStruct(values[0].shape, jnp.float32),
        cost_estimate=pl.CostEstimate(
            flops=int(SUM_COST), bytes_accessed=int(SUM_COST / 100), transcendentals=0
        ),
        compiler_params=pltpu.CompilerParams(vmem_limit_bytes=VMEM_BYTES),
    )(*values, *after)


def ring_shards(
    inputs_forward,
    routes_forward,
    gates_forward,
    grads_backward,
    routes_backward,
    gates_backward,
    w_gate,
    w_up,
    w_down,
    saved_gate,
    saved_up,
):
    experts, nodes = lax.axis_size("dev"), lax.axis_size("node")
    place = jnp.stack([lax.axis_index("node"), lax.axis_index("dev")]).astype(jnp.int32)
    weights = (w_gate[0, 0], w_up[0, 0], w_down[0, 0])
    stored_gate, stored_up = saved_gate[0, 0], saved_up[0, 0]

    chosen = routes_forward.shape[2]
    tokens = [inputs_forward[0]]
    grads = [
        with_info(
            grads_backward[0],
            (routes_forward[0].T, routes_backward[0].T),
            (gates_forward[0].T, gates_backward[0].T),
            (marker(),),
        )
    ]
    for _ in range(1, experts):
        tokens.append(along_ring(tokens[-1], 1))
        grads.append(along_ring(grads[-1], 1))

    count = grads_backward.shape[1]
    sent, parts = [None] * experts, [None] * experts
    acts = [None] * experts, [None] * experts
    done = []

    def exchange(own):
        arrived = [across(own[mask % len(own)], "node", mask) for mask in range(nodes - 1, 0, -1)]
        return [own[0]] + arrived[::-1]

    factors = [None] * experts

    def prepare(step):
        factors[step] = backward_factors(
            place, stored_gate, stored_up, grads[step], chosen, count, step, done[-1:]
        )
        done.append(factors[step][0])

    first_weights = [weights, CONTRACT_LAST]
    turned = [None, None]

    def turn(index):
        value = transposed(place, weights[index], done[-1:])
        done.append(value)
        return value

    def first(step, *after):
        sent[step] = first_products(
            place, tokens[step], grads[step], first_weights[0], first_weights[1], nodes, 5 if step > 1 else 3, (*done[-1:], *after)
        )
        done.append(sent[step][0])
        if step < 2:
            parts[step] = exchange(sent[step])

    def middle(step, *after):
        joint = 0 < step < experts - 1
        filled, extra = (sent[step + 1], ()) if joint else ((), (own_acts,))
        own = activations(place, parts[step], filled, (*done[-1:], *after), extra)
        done.append(own[0])
        arrived = exchange(own)
        plane = 3 if joint else 0
        acts[0][step], acts[1][step] = (arrived, plane), (arrived, plane + 1)
        if joint:
            parts[step + 1] = arrived
        else:
            acts[1][0] = (arrived, plane + 2)

    sums, hops, base = [[], []], [(), ()], [None, None]

    def last(step, kind, *after):
        shift = 1 - 2 * kind
        added = (inputs_forward[0], grads_backward[0])[kind : kind + 1] if step == 0 else ()
        if step >= 2:
            added = hops[kind]
        if kind == 0:
            value = forward_results(
                place, *acts[0][step], weights[2], grads[step], chosen, added, (*done[-1:], *after)
            )
        else:
            value = backward_results(
                place, *acts[1][step], *turned, factors[step], grads[step], chosen, added, (*done[-1:], *after)
            )
        done.append(value)
        if step == 0:
            base[kind] = from_behind(value, "section", shift)
        elif step == 1:
            sums[kind].append(along_ring_and_sections(value, -1, shift))
        elif step < experts - 1:
            hops[kind] = (along_ring(value, 1),)
        else:
            sums[kind].append(along_ring_and_sections(value, 1, shift))

    first(0)
    first(1)
    first_weights[:] = (*weights[:2], turn(2)), PLAIN
    own_acts = activations(place, parts[0], (), done[-1:])[0]
    done.append(own_acts)
    for step in range(1, experts - 1):
        if step == experts - 2:
            turned[:] = turn(0), turn(1)
        first(step + 1)
        prepare(step)
        middle(step)
        if step >= 2:
            last(step - 1, 0)
            last(step - 1, 1)
    prepare(experts - 1)
    prepare(0)
    middle(experts - 1)
    if experts > 2:
        last(experts - 2, 0)
        last(experts - 2, 1, *[values[0] for values in sums if values])
    last(experts - 1, 0)
    own_plane = first_plane(place, own_acts, (*done[-1:], *acts[0][experts - 1][0][1:]))
    done.append(own_plane)
    acts[0][0] = (exchange([own_plane]), 0)
    last(experts - 1, 1)
    last(0, 0)
    last(0, 1)
    outs = []
    for values, own in zip(sums, base):
        total = sum(value.astype(jnp.float32) for value in (sum_rows(values[-1:], (*done[-1:], *outs)), *values[:-1], own))
        outs.append(total.astype(jnp.bfloat16))
    return tuple(out[None] for out in outs)


def power_of_two(number):
    return number & (number - 1) == 0


def shards(*args):
    experts, nodes = lax.axis_size("dev"), lax.axis_size("node")
    tokens, capacity = args[0].shape[1], args[9].shape[2] // experts
    if capacity == tokens and experts > 1 and power_of_two(nodes) and tokens % (16 * nodes) == 0:
        return ring_shards(*args)
    return shards_by_slots(*args)


def solution(mesh):
    return jax.shard_map(
        shards,
        mesh=mesh,
        in_specs=(
            P("section", "dev", "node"),
            P("section", "dev", None),
            P("section", "dev", None),
            P("section", "dev", "node"),
            P("section", "dev", None),
            P("section", "dev", None),
            P("section", "dev", "node", None),
            P("section", "dev", "node", None),
            P("section", "dev", None, "node"),
            P("section", "dev", None, None),
            P("section", "dev", None, None),
        ),
        out_specs=(P("section", "dev", "node"), P("section", "dev", "node")),
        check_vma=False,
    )
```
